32 devices in a mesh: section: 2 (over x), dp: 16 (over z, y, core).
Axes of the slice: x: 2, y: 2, z: 4, core: 2. Of those that a mesh axis runs over, the one named last changes fastest.
Arguments:
- edge_rows: bfloat16 [2, 4096, 768], P('section', 'dp'), may hold values from -24 to 24
- lengths: int32 [32, 3], P('dp'), may hold values from 1 to 64, 128 in all within a row
- routes: int32 [2, 4096, 1], P('section', 'dp'), may hold values from 0 to 7; in each aligned block of 128 rows (0 to 127, 128 to 255, ..., all dimensions but the last counted through in order) at most 32 rows name the same one
- norm_gains: bfloat16 [2, 2, 768], P('section', None, 'dp'), may hold values from 0.5 to 1.5
- qkv_weight: bfloat16 [2, 768, 2304], P('section', 'dp'), may hold values from -0.21875 to 0.21875
- out_weight: bfloat16 [2, 768, 768], P('section', 'dp'), may hold values from -0.875 to 0.875
- router_weight: bfloat16 [2, 768, 8], P('section', 'dp'), may hold values from -0.109375 to 0.109375
- bias_table: bfloat16 [2, 384], P('section', 'dp'), may hold values from -4 to 4
- expert_in: bfloat16 [2, 768, 24576], P('section', None, 'dp'), may hold values from -0.21875 to 0.21875
- expert_out: bfloat16 [2, 24576, 768], P('section', 'dp'), may hold values from -0.875 to 0.875
Outputs:
- edge_results: float32 [2, 4096, 768], P('section', 'dp')
- grad_gains: float32 [2, 2, 768], P('section', None, 'dp')
- grad_qkv: float32 [2, 768, 2304], P('section', 'dp')
- grad_out: float32 [2, 768, 768], P('section', 'dp')
- grad_router: float32 [2, 768, 8], P('section', 'dp')
- grad_table: float32 [2, 384], P('section', 'dp')
- grad_expert_in: float32 [2, 768, 24576], P('section', None, 'dp')
- grad_expert_out: float32 [2, 24576, 768], P('section', 'dp')
The draws below stay inside these ranges and needn't reach their ends.
Inputs may be any that keep to these rules, and one draw needn't show every extreme that they name: Each block of 128 tokens holds 3 sequences whose lengths sum to 128; the longest of each block has exactly 64 tokens. `routes`: among the 128 tokens of one block at most 32 name the same expert, and in some blocks an expert is named by exactly 32.
All inputs are finite; a program needn't handle non-finite values.
Results may differ from the reference program's by a relative error of at most 0.019.
Values may be sent and summed in bfloat16 or wider, within the bound.
No kernel may reach another device: no remote copies, remote signals or barrier semaphores. Data moves between devices by JAX's collectives and lax.ppermute only.
A program may use at most 192 MiB of HBM per device.

```python
import math
import jax
import jax.numpy as jnp
import numpy as np
from jax import lax

D = 768
HEADS = 12
HEAD_DIM = 64
FF = 3072
BUCKETS = 32
SLOT = 128
MICRO = 2
SEQS = 3
LAYERS = 2
EXPERTS = 8
CAP = 32
BLOCKS = 32
TOKENS = 4096
N_DP = 16


def draw_edge_rows(key, part):
    key = jax.random.fold_in(key, 11)
    subkeys = jax.random.split(key, 3)
    dims_all = (LAYERS, TOKENS, D)
    row_scale = jnp.exp(jax.random.uniform(subkeys[1], (LAYERS, TOKENS, 1), minval=math.log(0.6), maxval=math.log(2.0)))
    col_scale = jnp.exp(jax.random.uniform(subkeys[2], (LAYERS, 1, D), minval=math.log(0.3), maxval=math.log(3.0)))
    values = jax.random.normal(subkeys[0], dims_all) * row_scale * col_scale
    return jnp.clip(values, -24.0, 24.0).astype(jnp.bfloat16)


def level_of(key, shape, shards, low, high):
    gain, own = 1.0, jax.random.fold_in(key, 6)
    for position, shards_of in shards:
        heights = jnp.exp(jax.random.uniform(jax.random.fold_in(own, position), (shards_of,), jnp.float32, low / len(shards), high / len(shards)))
        gain = gain * jnp.repeat(heights, shape[position] // shards_of).reshape([-1 if axis == position else 1 for axis in range(len(shape))])
    return gain


def length_profile(amount, total, most, skew):
    portions = [(1 << 20) // math.isqrt(grade ** skew) + 1 for grade in range(2, amount + 1)]
    spare, given = total - most - (amount - 1), [1] * (amount - 1)
    while spare > 0:
        candidates = [i for i in range(amount - 1) if given[i] < most]
        pool, remaining = sum([portions[i] for i in candidates]), spare
        for i in candidates:
            addition = min(most - given[i], max(1, remaining * portions[i] // pool), spare)
            given[i] = given[i] + addition
            spare = spare - addition
    return np.array([most] + given)


def uneven(own_key, number_of, total, bound, lean):
    if number_of == 2:
        one = jax.random.randint(own_key, (), max(1, total - bound), min(bound, total - 1) + 1)
        return jnp.stack([one, total - one])
    sizes = jnp.asarray(length_profile(number_of, total, bound, lean), jnp.int32)
    couples = (number_of - 1) // 2
    source_of, sink = sizes[1:1 + 2 * couples:2], sizes[2:2 + 2 * couples:2]
    room = jnp.minimum(source_of - 1, bound - sink)
    shifted = jax.random.randint(jax.random.fold_in(own_key, 1), (couples,), 0, 1 << 20) % (room + 1)
    sizes = sizes.at[1:1 + 2 * couples:2].set(source_of - shifted).at[2:2 + 2 * couples:2].set(sink + shifted)
    return sizes[jax.random.permutation(jax.random.fold_in(own_key, 2), number_of)]


def shared_out(stream_key, own, number, rows, amount, top, limit, skew):
    sequence = jax.random.permutation(stream_key, amount)
    crowded, usual = shares(amount, rows * top, limit, skew, True), shares(amount, rows * top, limit, skew, False)
    places = jnp.arange(amount)

    def named(sizes, turn):
        used = int((sizes > 0).sum())
        fixed = max(1, used // 4)
        moved = fixed + (places - fixed + turn * (used - fixed)) % max(1, amount - fixed)
        return jnp.zeros((amount,), jnp.int32).at[sequence[jnp.where(places < fixed, places, moved)]].set(jnp.asarray(sizes, jnp.int32))

    sizes = jnp.where(number % 4 == 0, named(crowded, number // 4), named(usual, number - number // 4 - 1))
    mixed = jax.random.permutation(jax.random.fold_in(own, 3), amount)
    source_of, receiver = mixed[0:amount // 2 * 2:2], mixed[1:amount // 2 * 2:2]
    margin = jnp.minimum(sizes[source_of] - 1, limit - sizes[receiver]) // 2
    margin = jnp.where((source_of == sequence[0]) | (receiver == sequence[0]) | (sizes[receiver] == 0), 0, jnp.maximum(margin, 0))
    moved = jax.random.randint(jax.random.fold_in(own, 4), (amount // 2,), 0, 1 << 20) % (margin + 1)
    sizes = sizes.at[source_of].add(-moved).at[receiver].add(moved)
    labels = jnp.searchsorted(jnp.cumsum(sizes), jnp.arange(rows * top), side="right").astype(jnp.int32)
    grid = labels.reshape(top, rows).T
    grid = grid[jax.random.permutation(jax.random.fold_in(own, 1), rows)]
    turn = jax.random.randint(jax.random.fold_in(own, 2), (rows, 1), 0, top)
    return jnp.take_along_axis(grid, (jnp.arange(top)[None, :] + turn) % top, axis=1)


def shares(count, total, most, skew, full):
    portions = [(1 << 20) // math.isqrt(grade ** skew) + 1 for grade in range(1, count + 1)]
    largest = most if full else min(most, max(-(-total // count), total * portions[0] // sum(portions)))
    least = 1 if total - largest >= count - 1 else 0
    holding, rest = [largest] + [least] * (count - 1), total - largest - least * (count - 1)
    while rest > 0:
        movable = [i for i in range(1, count) if holding[i] < largest] or [i for i in range(1, count) if holding[i] < most]
        pool, budget = sum([portions[i] for i in movable]), rest
        for i in movable:
            more = min(most - holding[i], max(1, budget * portions[i] // pool), rest)
            holding[i] = holding[i] + more
            rest = rest - more
    return np.array(holding)


def noise(stream_key, shape, scale, most, cuts=(), kind=jnp.bfloat16):
    entries = jax.random.normal(stream_key, shape, jnp.float32) * scale
    if len(cuts) > 0:
        entries = level_of(stream_key, shape, cuts, -0.22, 0.18) * entries
    return jnp.clip(entries, min=-most, max=most).astype(kind)


def setup_inputs(seed: int = 0) -> dict:
    seeds = jax.random.split(jax.random.key(seed), 11)
    edge_rows = draw_edge_rows(jax.random.fold_in(seeds[10], 71), 0)
    lengths = jax.vmap(lambda own: uneven(own, SEQS, SLOT, SLOT // 2, 2))(jax.random.split(seeds[1], BLOCKS)).reshape((BLOCKS, SEQS)).astype(jnp.int32)
    routes_keys = jax.random.split(jax.random.fold_in(seeds[2], 1), LAYERS * TOKENS // SLOT)
    routes_turns = jax.random.permutation(jax.random.fold_in(seeds[2], 3), LAYERS * TOKENS // SLOT)
    routes = jax.vmap(lambda own, number: shared_out(jax.random.fold_in(seeds[2], 2), own, number, SLOT, EXPERTS, 1, CAP, 2))(routes_keys, routes_turns).reshape((LAYERS, TOKENS, 1))
    norm_gains = jnp.clip(1.0 + 0.1 * jax.random.normal(seeds[3], (LAYERS, 2, D), jnp.float32), 0.5, 1.5).astype(jnp.bfloat16)
    qkv_weight = noise(seeds[4], (LAYERS, D, 3 * D), D ** -0.5, 0.21875, ((0, 2), (1, 16)))
    out_weight = noise(seeds[5], (LAYERS, D, D), (D // 16) ** -0.5, 0.875, ((0, 2), (1, 16)))
    router_weight = noise(seeds[6], (LAYERS, D, EXPERTS), (4 * D) ** -0.5, 0.109375, ((0, 2), (1, 16)))
    bias_table = noise(seeds[7], (LAYERS, BUCKETS * HEADS), 1.0, 4.0, ((0, 2), (1, 16)))
    expert_in = noise(seeds[8], (LAYERS, D, EXPERTS * FF), D ** -0.5, 0.21875, ((0, 2), (2, 16)))
    expert_out = noise(seeds[9], (LAYERS, EXPERTS * FF, D), (max(1, FF // (EXPERTS * EXPERTS))) ** -0.5, 0.875, ((0, 2), (1, 16)))
    return {"edge_rows": edge_rows, "lengths": lengths, "routes": routes, "norm_gains": norm_gains, "qkv_weight": qkv_weight, "out_weight": out_weight, "router_weight": router_weight, "bias_table": bias_table, "expert_in": expert_in, "expert_out": expert_out}


norm_eps = 1e-06
bucket_edges = (1, 2, 3, 4, 5, 6, 7, 8, 12, 16, 23, 32, 46, 64, 91)
highest = lax.Precision.HIGHEST

@jax.custom_vjp
def low(v):
    return lax.optimization_barrier(v.astype(jnp.bfloat16)).astype(jnp.float32)

@jax.custom_vjp
def low_back(v):
    return v

def low_keep(v):
    return (low(v), None)

def low_pass(kept, grad):
    return (grad,)

def back_keep(v):
    return (v, None)

def back_low(kept, grad):
    return (low(grad),)
low.defvjp(low_keep, low_pass)
low_back.defvjp(back_keep, back_low)

def normalize(values, gain_row):
    inv_rms = lax.rsqrt(lax.optimization_barrier(jnp.mean(values * values, axis=-1, keepdims=True)) + norm_eps)
    return values * inv_rms * gain_row

def bucket_onehot():
    places = jnp.arange(SLOT, dtype=jnp.int32)
    offset = places[None, :] - places[:, None]
    distance = jnp.abs(offset)
    bucket = jnp.zeros_like(distance)
    for threshold in bucket_edges:
        bucket = bucket + (distance >= threshold).astype(jnp.int32)
    bucket = bucket + BUCKETS // 2 * (offset > 0).astype(jnp.int32)
    return (bucket[:, :, None] == jnp.arange(BUCKETS, dtype=jnp.int32)).astype(jnp.float32)

def same_sequence(lengths):
    bounds = jnp.cumsum(lengths, axis=-1)
    places = jnp.arange(SLOT, dtype=jnp.int32)
    owners = lax.optimization_barrier(jnp.sum((places[:, None] >= bounds[..., None, :]).astype(jnp.int32), axis=-1))
    return owners[..., :, None] == owners[..., None, :]

def expert_slots(route_ids):
    choose = (route_ids[:, None] == jnp.arange(EXPERTS, dtype=jnp.int32)[None, :]).astype(jnp.int32)
    blocked = choose.reshape(BLOCKS, SLOT, EXPERTS)
    before = jnp.cumsum(blocked, axis=1) - blocked
    rank_ids = lax.optimization_barrier(jnp.sum(before * blocked, axis=-1)).reshape(TOKENS)
    block_id = jnp.arange(TOKENS, dtype=jnp.int32) // SLOT
    return route_ids * (BLOCKS * CAP) + block_id * CAP + rank_ids

def attention_group(pieces, relative):
    queries, key_vecs, value_vecs, same_seq = pieces
    scores = jnp.einsum('mqhd,mkhd->mhqk', queries, key_vecs, precision=highest) * HEAD_DIM ** (-0.5) + relative[None]
    scores = low_back(jnp.where(same_seq[:, None], scores, -1e+30))
    weights = low(jax.nn.softmax(scores, axis=-1))
    attended = jnp.einsum('mhqk,mkhd->mqhd', weights, value_vecs, precision=highest)
    return low_back(low(attended))

def expert_group(pieces):
    row_block, weight_in, weight_out = pieces
    summed = jnp.zeros_like(row_block)
    for which_half in range(2):
        shared = low_back(row_block)
        hidden = low_back(jnp.dot(shared, weight_in[:, which_half], precision=highest))
        active = low(jax.nn.gelu(hidden))
        summed = summed + low_back(low(jnp.dot(active, weight_out[which_half], precision=highest)))
    return summed

def encoder_layer(inputs, params, route_ids, same_seq, onehot):
    gain_rows, qkv_w, out_w, router_w, table, weight_in, weight_out = params
    normed = low(normalize(inputs, gain_rows[0]))
    projected = low_back(low(jnp.dot(normed, qkv_w, precision=highest)))
    projected = projected.reshape(N_DP, MICRO, SLOT, 3, HEADS, HEAD_DIM)
    relative = jnp.einsum('qkb,bh->hqk', onehot, table.reshape(BUCKETS, HEADS), precision=highest)
    attend = jax.checkpoint(attention_group)
    attended = lax.map(lambda pieces: attend(pieces, relative), (projected[:, :, :, 0], projected[:, :, :, 1], projected[:, :, :, 2], same_seq))
    attended = attended.reshape(TOKENS, D)
    branch = low_back(jnp.dot(attended, out_w, precision=highest))
    middle = inputs + branch
    routed = low(normalize(middle, gain_rows[1]))
    logits = low_back(jnp.dot(routed, router_w, precision=highest))
    choose = route_ids[:, None] == jnp.arange(EXPERTS, dtype=jnp.int32)[None, :]
    gate_prob = lax.optimization_barrier(jnp.sum(jnp.where(choose, jax.nn.softmax(logits, axis=-1), 0.0), axis=-1))
    targets = expert_slots(route_ids)
    buffers = jnp.zeros((EXPERTS * BLOCKS * CAP, D), routed.dtype).at[targets].set(routed)
    split_in = weight_in.reshape(D, EXPERTS, 2, FF // 2).transpose(1, 0, 2, 3)
    split_out = weight_out.reshape(EXPERTS, 2, FF // 2, D)
    replies = lax.map(jax.checkpoint(expert_group), (buffers.reshape(EXPERTS, BLOCKS * CAP, D), split_in, split_out))
    result = replies.reshape(EXPERTS * BLOCKS * CAP, D)[targets]
    return middle + gate_prob[:, None] * result

def reference(edge_rows, lengths, routes, norm_gains, qkv_weight, out_weight, router_weight, bias_table, expert_in, expert_out):
    same_seq = same_sequence(lengths.reshape(N_DP, MICRO, SEQS))
    onehot = bucket_onehot()
    weights = tuple((tensor.astype(jnp.float32) for tensor in (norm_gains, qkv_weight, out_weight, router_weight, bias_table, expert_in, expert_out)))
    source = edge_rows[0].astype(jnp.float32)
    cotangent = edge_rows[1].astype(jnp.float32)

    def forward(anchor, params):
        first_params = tuple((tensor[0] for tensor in params))
        second_params = tuple((tensor[1] for tensor in params))
        first_out = encoder_layer(anchor, first_params, routes[0, :, 0], same_seq, onehot)
        passed = low_back(low(first_out))
        return encoder_layer(passed, second_params, routes[1, :, 0], same_seq, onehot)
    result, pullback = jax.vjp(forward, source, weights)
    grad_source, gradients = pullback(cotangent)
    return (jnp.stack([grad_source, result]), gradients[0], gradients[1], gradients[2], gradients[3], gradients[4], gradients[5], gradients[6])
```

```python
import jax
import jax.numpy as jnp
from jax import lax
from jax.sharding import PartitionSpec as P

D = 768
HEADS = 12
HEAD_DIM = 64
BUCKETS = 32
SLOT = 128


norm_eps = 1e-06
masked_score = -1e30
bucket_edges = (1, 2, 3, 4, 5, 6, 7, 8, 12, 16, 23, 32, 46, 64, 91)
bf16 = jnp.bfloat16
f32 = jnp.float32


def dot(lhs, rhs):
    return jnp.dot(lhs, rhs, preferred_element_type=f32)


def section_shift(block, distance):
    devices = range(lax.axis_size("section"))
    route = [(i - distance, i) for i in devices if i - distance in devices]
    return lax.ppermute(block, "section", route)


def pair_swap(block):
    return lax.ppermute(block, "dp", [(i, i ^ 1) for i in range(lax.axis_size("dp"))])


def chip_all_to_all(block):
    devices = lax.axis_size("dp")
    groups = [list(range(core, devices, 2)) for core in range(2)]
    return lax.all_to_all(
        block, "dp", split_axis=0, concat_axis=0, tiled=True, axis_index_groups=groups
    )


def rms_scale(values):
    return lax.rsqrt(jnp.mean(values * values, axis=-1, keepdims=True) + norm_eps)


def norm_backward(grad_normed, values, gain_row):
    inv_rms = rms_scale(values)
    weighted = grad_normed * gain_row
    grad_gain = jnp.sum(grad_normed * values * inv_rms, axis=0)
    grad_values = inv_rms * weighted - values * inv_rms**3 * jnp.mean(
        weighted * values, axis=-1, keepdims=True
    )
    return (grad_values, grad_gain)


def bucket_onehot():
    places = jnp.arange(SLOT, dtype=jnp.int32)
    offset = places[None, :] - places[:, None]
    distance = jnp.abs(offset)
    bucket = jnp.zeros_like(distance)
    for threshold in bucket_edges:
        bucket = bucket + (distance >= threshold).astype(jnp.int32)
    bucket = bucket + BUCKETS // 2 * (offset > 0).astype(jnp.int32)
    return (bucket[:, :, None] == jnp.arange(BUCKETS, dtype=jnp.int32)).astype(bf16)


def same_sequence(lengths):
    bounds = jnp.cumsum(lengths, axis=-1)
    places = jnp.arange(SLOT, dtype=jnp.int32)
    owners = jnp.sum((places[:, None] >= bounds[:, None, :]).astype(jnp.int32), axis=-1)
    return owners[:, :, None] == owners[:, None, :]


def expert_places(route_ids, experts, capacity):
    blocks = route_ids.shape[0]
    names = jnp.arange(experts, dtype=jnp.int32)
    choose = (route_ids[:, :, None] == names).astype(jnp.int32)
    places = jnp.arange(SLOT, dtype=jnp.int32)
    earlier = (places[:, None] > places[None, :]).astype(bf16)
    before = jnp.einsum(
        "tu,bue->bte", earlier, choose.astype(bf16), preferred_element_type=f32
    ).astype(jnp.int32)
    rank_ids = jnp.sum(before * choose, axis=-1)
    block_ids = jnp.arange(blocks, dtype=jnp.int32)[:, None]
    targets = ((route_ids * blocks + block_ids) * capacity + rank_ids).reshape(-1)
    slots = jnp.arange(experts * blocks * capacity, dtype=jnp.int32)
    placing = (targets[:, None] == slots[None, :]).astype(bf16)
    return (choose.astype(f32).reshape(-1, experts), placing)


def to_experts(row_data, placing):
    packed = jnp.einsum("ts,td->sd", placing, row_data, preferred_element_type=f32).astype(bf16)
    experts = lax.axis_size("dp") // 2
    arrived = chip_all_to_all(packed.reshape(experts, -1, D)).reshape(-1, D)
    return (arrived, pair_swap(arrived))


def from_experts(own, other, placing):
    summed = (own + pair_swap(other.astype(bf16)).astype(f32)).astype(bf16)
    experts = lax.axis_size("dp") // 2
    returned = chip_all_to_all(summed.reshape(experts, -1, D)).reshape(-1, D)
    return dot(placing, returned)


def split_heads(rows):
    return rows.reshape(-1, SLOT, HEADS, HEAD_DIM)


def score_block(queries, keys, relative, same_seq):
    scores = (
        jnp.einsum("bqhd,bkhd->bhqk", queries, keys, preferred_element_type=f32)
        * HEAD_DIM ** (-0.5)
        + relative
    )
    return jnp.where(same_seq[:, None], scores, masked_score)


def gelu_parts(hidden):
    rate, cubic = 0.7978845608028654, 0.044715
    squared = hidden * hidden
    bend = jnp.tanh(rate * hidden * (1.0 + cubic * squared))
    active = 0.5 * hidden * (1.0 + bend)
    slope = 0.5 * (1.0 + bend) + 0.5 * hidden * (1.0 - bend * bend) * rate * (
        1.0 + 3.0 * cubic * squared
    )
    return (active.astype(bf16), slope.astype(bf16))


def layer_forward(inputs, dense, fixed, experts_held):
    gain_rows, qkv_w, out_w, router_w = dense
    relative, same_seq, choose, placing = fixed
    weight_in, weight_out = experts_held
    normed = (inputs * rms_scale(inputs) * gain_rows[0]).astype(bf16)
    projected = dot(normed, qkv_w).astype(bf16)
    queries, keys, values = [split_heads(part) for part in jnp.split(projected, 3, axis=-1)]
    scores = score_block(queries, keys, relative, same_seq)
    top_score = jnp.max(scores, axis=-1, keepdims=True)
    raised = jnp.exp(scores - top_score)
    probs = raised / jnp.sum(raised, axis=-1, keepdims=True)
    weights = probs.astype(bf16)
    attended = (
        jnp.einsum("bhqk,bkhd->bqhd", weights, values, preferred_element_type=f32)
        .astype(bf16)
        .reshape(-1, D)
    )
    middle = inputs + dot(attended, out_w)
    routed = (middle * rms_scale(middle) * gain_rows[1]).astype(bf16)
    route_probs = jax.nn.softmax(dot(routed, router_w), axis=-1)
    gate_prob = jnp.sum(route_probs * choose, axis=-1)
    arrived = to_experts(routed, placing)
    active, slope = zip(*[gelu_parts(dot(rows, weight_in)) for rows in arrived])
    replies = [dot(rows, weight_out) for rows in active]
    result = from_experts(replies[0], replies[1], placing)
    outputs = middle + gate_prob[:, None] * result
    kept = (
        inputs,
        normed,
        (queries, keys, values),
        probs,
        attended,
        middle,
        routed,
        route_probs,
        gate_prob,
        result,
        arrived,
        active,
        slope,
    )
    return (outputs, kept)


def layer_backward(grad_out, kept, dense, fixed, onehot, experts_held):
    (
        inputs,
        normed,
        (queries, keys, values),
        probs,
        attended,
        middle,
        routed,
        route_probs,
        gate_prob,
        result,
        arrived,
        active,
        slope,
    ) = kept
    gain_rows, qkv_w, out_w, router_w = dense
    relative, same_seq, choose, placing = fixed
    weight_in, weight_out = experts_held
    grad_gate = jnp.sum(grad_out * result, axis=-1)
    grad_result = (gate_prob[:, None] * grad_out).astype(bf16)
    grad_rows = to_experts(grad_result, placing)
    grad_hidden = [
        (
            jnp.einsum("rd,fd->rf", rows, weight_out, preferred_element_type=f32)
            * steep.astype(f32)
        ).astype(bf16)
        for rows, steep in zip(grad_rows, slope)
    ]
    grad_sent = [
        jnp.einsum("rf,df->rd", rows, weight_in, preferred_element_type=f32)
        for rows in grad_hidden
    ]
    grad_routed = from_experts(grad_sent[0], grad_sent[1], placing)
    grad_expert_out = jnp.einsum(
        "krf,krd->fd", jnp.stack(active), jnp.stack(grad_rows), preferred_element_type=f32
    )
    grad_expert_in = jnp.einsum(
        "krd,krf->df", jnp.stack(arrived), jnp.stack(grad_hidden), preferred_element_type=f32
    )
    grad_logits = ((grad_gate * gate_prob)[:, None] * (choose - route_probs)).astype(bf16)
    grad_router = jnp.einsum("td,te->de", routed, grad_logits, preferred_element_type=f32)
    grad_routed = grad_routed + jnp.einsum(
        "te,de->td", grad_logits, router_w, preferred_element_type=f32
    )
    grad_middle_norm, grad_gain_two = norm_backward(grad_routed, middle, gain_rows[1])
    grad_middle = grad_out + grad_middle_norm
    grad_branch = grad_middle.astype(bf16)
    grad_out_w = jnp.einsum("tf,td->fd", attended, grad_branch, preferred_element_type=f32)
    grad_attended = split_heads(
        jnp.einsum("td,fd->tf", grad_branch, out_w, preferred_element_type=f32).astype(bf16)
    )
    grad_values = jnp.einsum(
        "bhqk,bqhd->bkhd", probs.astype(bf16), grad_attended, preferred_element_type=f32
    )
    grad_probs = jnp.einsum(
        "bqhd,bkhd->bhqk", grad_attended, values, preferred_element_type=f32
    )
    grad_scores = (
        probs * (grad_probs - jnp.sum(probs * grad_probs, axis=-1, keepdims=True))
    ).astype(bf16)
    scale_qk = HEAD_DIM ** (-0.5)
    grad_queries = (
        jnp.einsum("bhqk,bkhd->bqhd", grad_scores, keys, preferred_element_type=f32) * scale_qk
    )
    grad_keys = (
        jnp.einsum("bhqk,bqhd->bkhd", grad_scores, queries, preferred_element_type=f32) * scale_qk
    )
    grad_table = jnp.einsum(
        "bhqk,qkn->nh", grad_scores, onehot, preferred_element_type=f32
    ).reshape(-1)
    grad_projected = jnp.concatenate(
        [part.astype(bf16).reshape(-1, D) for part in (grad_queries, grad_keys, grad_values)],
        axis=-1,
    )
    grad_qkv = jnp.einsum("td,tf->df", normed, grad_projected, preferred_element_type=f32)
    grad_normed = jnp.einsum("tf,df->td", grad_projected, qkv_w, preferred_element_type=f32)
    grad_inputs_norm, grad_gain_one = norm_backward(grad_normed, inputs, gain_rows[0])
    grad_inputs = grad_middle + grad_inputs_norm
    dense_grads = (
        jnp.stack([grad_gain_one, grad_gain_two]),
        grad_qkv,
        grad_out_w,
        grad_router,
        grad_table,
    )
    return (grad_inputs, dense_grads, (grad_expert_in, grad_expert_out))


def pack_dense(gains, qkv, out, router, table, owners, kind):
    extent = qkv.shape[0] // owners
    entries = jnp.pad(
        table.reshape(owners, -1), ((0, 0), (0, extent - table.size // owners))
    ).reshape(-1, 1)
    extra = jnp.concatenate(
        [router.astype(kind), gains.T.astype(kind), entries.astype(kind)], axis=1
    )
    extra = jnp.pad(extra, ((0, 0), (0, 128 - extra.shape[1])))
    return jnp.concatenate([qkv.astype(kind), out.astype(kind), extra], axis=1)


def unpack_dense(packed, owners, experts):
    qkv, out, extra = packed[:, : 3 * D], packed[:, 3 * D : 4 * D], packed[:, 4 * D :]
    used = packed.shape[0] // owners * BUCKETS * HEADS // D
    table = extra[:, experts + 2].reshape(owners, -1)[:, :used].reshape(-1)
    return (extra[:, experts : experts + 2].T, qkv, out, extra[:, :experts], table)


def scatter_dense(packed):
    devices = lax.axis_size("dp")
    core = lax.axis_index("dp") % 2
    packed = packed.reshape(devices // 2, 2, D // devices, -1)
    mine = lax.dynamic_index_in_dim(packed, core, axis=1, keepdims=False)
    others = lax.dynamic_index_in_dim(packed, 1 - core, axis=1, keepdims=False)
    summed = (mine + pair_swap(others.astype(bf16)).astype(f32)).astype(bf16)
    return jnp.sum(chip_all_to_all(summed).astype(f32), axis=0)


def shards(
    edge_rows,
    lengths,
    routes,
    norm_gains,
    qkv_weight,
    out_weight,
    router_weight,
    bias_table,
    expert_in,
    expert_out,
):
    devices = lax.axis_size("dp")
    experts = devices // 2
    first_section = lax.axis_index("section") == 0
    local_rows = edge_rows[0].astype(f32)
    onehot = bucket_onehot()
    experts_held = (expert_in[0], expert_out[0])
    packed = pack_dense(
        norm_gains[0], qkv_weight[0], out_weight[0], router_weight[0], bias_table[0], 1, bf16
    )
    gathered = lax.all_gather(packed, "dp", axis=0, tiled=True)
    gains, qkv_w, out_w, router_w, table = unpack_dense(gathered, devices, experts)
    dense = (gains.astype(f32), qkv_w, out_w, router_w)
    relative = jnp.einsum(
        "qkb,bh->hqk", onehot, table.reshape(BUCKETS, HEADS), preferred_element_type=f32
    )
    route_ids = routes[0, :, 0].reshape(-1, SLOT)
    choose, placing = expert_places(route_ids, experts, 4 * SLOT // devices)
    fixed = (relative, same_sequence(lengths), choose, placing)
    outputs, _ = layer_forward(local_rows, dense, fixed, experts_held)
    carried = section_shift(outputs.astype(bf16), 1).astype(f32)
    inputs = jnp.where(first_section, local_rows, carried)
    outputs, kept = layer_forward(inputs, dense, fixed, experts_held)
    grad_inputs, _, _ = layer_backward(local_rows, kept, dense, fixed, onehot, experts_held)
    carried = section_shift(grad_inputs.astype(bf16), -1).astype(f32)
    grad_out = jnp.where(first_section, carried, local_rows)
    grad_inputs, dense_grads, expert_grads = layer_backward(
        grad_out, kept, dense, fixed, onehot, experts_held
    )
    edge_results = jnp.where(first_section, grad_inputs, outputs)
    total = scatter_dense(pack_dense(*dense_grads, devices, f32))
    grad_gains, grad_qkv, grad_out_w, grad_router, grad_table = unpack_dense(total, 1, experts)
    return (
        edge_results[None],
        grad_gains[None],
        grad_qkv[None],
        grad_out_w[None],
        grad_router[None],
        grad_table[None],
        expert_grads[0][None],
        expert_grads[1][None],
    )


def solution(mesh):
    return jax.shard_map(
        shards,
        mesh=mesh,
        in_specs=(
            P("section", "dp", None),
            P("dp", None),
            P("section", "dp", None),
            P("section", None, "dp"),
            P("section", "dp", None),
            P("section", "dp", None),
            P("section", "dp", None),
            P("section", "dp"),
            P("section", None, "dp"),
            P("section", "dp", None),
        ),
        out_specs=(
            P("section", "dp", None),
            P("section", None, "dp"),
            P("section", "dp", None),
            P("section", "dp", None),
            P("section", "dp", None),
            P("section", "dp"),
            P("section", None, "dp"),
            P("section", "dp", None),
        ),
        check_vma=False,
    )
```

```python
import functools

import jax
import jax.numpy as jnp
from jax import lax
from jax.experimental import pallas as pl
from jax.experimental.pallas import tpu as pltpu
from jax.sharding import PartitionSpec as P

D = 768
HEADS = 12
HEAD_DIM = 64
BUCKETS = 32
SLOT = 128


norm_eps = 1e-06
masked_score = -1e30
bucket_edges = (1, 2, 3, 4, 5, 6, 7, 8, 12, 16, 23, 32, 46, 64, 91)
bf16 = jnp.bfloat16
f32 = jnp.float32


def dot(lhs, rhs):
    return jnp.dot(lhs, rhs, preferred_element_type=f32)


def section_shift(block, distance):
    devices = range(lax.axis_size("section"))
    route = [(i - distance, i) for i in devices if i - distance in devices]
    return lax.ppermute(block, "section", route)


def pair_swap(block):
    return lax.ppermute(block, "dp", [(i, i ^ 1) for i in range(lax.axis_size("dp"))])


def chip_all_to_all(block):
    devices = lax.axis_size("dp")
    groups = [list(range(core, devices, 2)) for core in range(2)]
    return lax.all_to_all(
        block, "dp", split_axis=0, concat_axis=0, tiled=True, axis_index_groups=groups
    )


def rms_scale(values):
    return lax.rsqrt(jnp.mean(values * values, axis=-1, keepdims=True) + norm_eps)


def norm_backward(grad_normed, values, gain_row):
    inv_rms = rms_scale(values)
    weighted = grad_normed * gain_row
    grad_gain = jnp.sum(grad_normed * values * inv_rms, axis=0)
    grad_values = inv_rms * weighted - values * inv_rms**3 * jnp.mean(
        weighted * values, axis=-1, keepdims=True
    )
    return (grad_values, grad_gain)


def bucket_onehot():
    offset = jnp.arange(2 * SLOT, dtype=jnp.int32) - SLOT
    distance = jnp.abs(offset)
    bucket = jnp.zeros_like(distance)
    for threshold in bucket_edges:
        bucket = bucket + (distance >= threshold).astype(jnp.int32)
    bucket = bucket + BUCKETS // 2 * (offset > 0).astype(jnp.int32)
    return (bucket[:, None] == jnp.arange(BUCKETS, dtype=jnp.int32)).astype(f32)


def same_sequence(lengths):
    bounds = jnp.cumsum(lengths, axis=-1)
    places = jnp.arange(SLOT, dtype=jnp.int32)
    owners = jnp.sum((places[:, None] >= bounds[:, None, :]).astype(jnp.int32), axis=-1)
    return (owners[:, :, None] == owners[:, None, :]).astype(f32)


def expert_places(route_ids, experts, capacity):
    blocks = route_ids.shape[0]
    names = jnp.arange(experts, dtype=jnp.int32)
    choose = (route_ids[:, :, None] == names).astype(jnp.int32)
    places = jnp.arange(SLOT, dtype=jnp.int32)
    earlier = (places[:, None] > places[None, :]).astype(bf16)
    before = jnp.einsum(
        "tu,bue->bte", earlier, choose.astype(bf16), preferred_element_type=f32
    ).astype(jnp.int32)
    rank_ids = jnp.sum(before * choose, axis=-1)
    block_ids = jnp.arange(blocks, dtype=jnp.int32)[:, None]
    targets = ((route_ids * blocks + block_ids) * capacity + rank_ids).reshape(-1)
    slots = jnp.arange(experts * blocks * capacity, dtype=jnp.int32)
    placing = (targets[:, None] == slots[None, :]).astype(bf16)
    return (targets, placing)


def to_experts(packed):
    experts = lax.axis_size("dp") // 2
    arrived = chip_all_to_all(packed.reshape(experts, -1, D)).reshape(-1, D)
    return (arrived, pair_swap(arrived))


def from_experts(own, other):
    summed = (own + pair_swap(other.astype(bf16)).astype(f32)).astype(bf16)
    experts = lax.axis_size("dp") // 2
    return chip_all_to_all(summed.reshape(experts, -1, D)).reshape(-1, D)


def dot_nt(lhs, rhs):
    return lax.dot_general(lhs, rhs, (((1,), (1,)), ((), ())), preferred_element_type=f32)


def dot_tn(lhs, rhs):
    return lax.dot_general(lhs, rhs, (((0,), (0,)), ((), ())), preferred_element_type=f32)


def lane_masks():
    low = lax.broadcasted_iota(jnp.int32, (1, 2 * HEAD_DIM), 1) < HEAD_DIM
    first = jnp.where(low, 1.0, 0.0)
    return (low, first.astype(bf16), (1.0 - first).astype(bf16))


def both_heads(slab, first, second):
    return jnp.concatenate([slab * first, slab * second], axis=0)


def own_lanes(low, stacked):
    return jnp.where(low, stacked[:SLOT], stacked[SLOT:])


def front_kernel(
    experts,
    inputs_ref,
    gains_ref,
    weight_ref,
    router_ref,
    diagonals_ref,
    same_ref,
    route_ref,
    target_ref,
    packed_ref,
    projected_ref,
    probs_ref,
    attended_ref,
    middle_ref,
    route_probs_ref,
    gate_ref,
):
    blocks = inputs_ref.shape[0] // SLOT
    inputs = inputs_ref[...]
    normed = (inputs * rms_scale(inputs) * gains_ref[0:1]).astype(bf16)
    projected_ref[...] = dot(normed, weight_ref[:, : 3 * D]).astype(bf16)
    low, first, second = lane_masks()
    width = 2 * HEAD_DIM
    for pair in range(HEADS // 2):
        relative = jnp.concatenate(
            [
                pltpu.roll(
                    jnp.broadcast_to(diagonals_ref[head : head + 1], (SLOT, 2 * SLOT)),
                    SLOT,
                    1,
                    stride=1,
                    stride_axis=0,
                )[:, :SLOT]
                for head in (2 * pair, 2 * pair + 1)
            ],
            axis=0,
        )
        for block in range(blocks):
            rows = slice(block * SLOT, (block + 1) * SLOT)
            queries, keys, values = [
                projected_ref[rows, part * D + pair * width : part * D + (pair + 1) * width]
                for part in range(3)
            ]
            same = same_ref[block]
            scores = (
                dot_nt(both_heads(queries, first, second), keys) * HEAD_DIM ** (-0.5) + relative
            )
            scores = jnp.where(jnp.concatenate([same, same], axis=0) > 0, scores, masked_score)
            raised = jnp.exp(scores - jnp.max(scores, axis=-1, keepdims=True))
            probs = raised / jnp.sum(raised, axis=-1, keepdims=True)
            probs_ref[block, pair] = probs
            attended_ref[rows, pair * width : (pair + 1) * width] = own_lanes(
                low, dot(probs.astype(bf16), values)
            ).astype(bf16)
    middle = inputs + dot(attended_ref[...], weight_ref[:, 3 * D :])
    middle_ref[...] = middle
    routed = (middle * rms_scale(middle) * gains_ref[1:2]).astype(bf16)
    logits = dot_nt(routed, router_ref[...])
    names = lax.broadcasted_iota(jnp.int32, (1, logits.shape[1]), 1)
    logits = jnp.where(names < experts, logits, masked_score)
    raised = jnp.exp(logits - jnp.max(logits, axis=-1, keepdims=True))
    route_probs = raised / jnp.sum(raised, axis=-1, keepdims=True)
    route_probs_ref[...] = route_probs
    gate_ref[...] = jnp.sum(
        jnp.where(names == route_ref[...], route_probs, 0.0), axis=-1, keepdims=True
    )
    slots = lax.broadcasted_iota(jnp.int32, (packed_ref.shape[0], 1), 0)
    placing = jnp.where(slots == target_ref[...], 1.0, 0.0).astype(bf16)
    packed_ref[...] = dot(placing, routed).astype(bf16)


def back_kernel(
    experts,
    full,
    grad_out_ref,
    returned_ref,
    target_ref,
    route_ref,
    inputs_ref,
    gains_ref,
    weight_ref,
    router_ref,
    projected_ref,
    probs_ref,
    attended_ref,
    middle_ref,
    route_probs_ref,
    gate_ref,
    result_ref,
    grad_inputs_ref,
    *rest,
):
    projected_grad_ref = rest[-1]
    blocks = inputs_ref.shape[0] // SLOT
    grad_out = grad_out_ref[...]
    gate = gate_ref[...]
    grad_gate = jnp.sum(grad_out * result_ref[...], axis=-1, keepdims=True)
    names = lax.broadcasted_iota(jnp.int32, (1, router_ref.shape[0]), 1)
    choose = jnp.where(names == route_ref[...], 1.0, 0.0)
    grad_logits = (grad_gate * gate * (choose - route_probs_ref[...])).astype(bf16)
    slots = lax.broadcasted_iota(jnp.int32, (1, returned_ref.shape[0]), 1)
    placing = jnp.where(slots == target_ref[...], 1.0, 0.0).astype(bf16)
    grad_routed = dot(placing, returned_ref[...]) + dot(grad_logits, router_ref[...])
    middle = middle_ref[...]
    grad_middle_norm, grad_gain_two = norm_backward(grad_routed, middle, gains_ref[1:2])
    grad_middle = grad_out + grad_middle_norm
    grad_branch = grad_middle.astype(bf16)
    grad_attended = dot_nt(grad_branch, weight_ref[:, 3 * D :]).astype(bf16)
    low, first, second = lane_masks()
    width = 2 * HEAD_DIM
    scale_qk = HEAD_DIM ** (-0.5)
    places = [lax.broadcasted_iota(jnp.int32, (SLOT, SLOT), axis) for axis in range(2)]
    reverse = jnp.where(places[0] + places[1] == SLOT - 1, 1.0, 0.0).astype(bf16)
    for pair in range(HEADS // 2):
        scores_total = jnp.zeros((2 * SLOT, SLOT), f32)
        for block in range(blocks):
            rows = slice(block * SLOT, (block + 1) * SLOT)
            columns = [
                slice(part * D + pair * width, part * D + (pair + 1) * width) for part in range(3)
            ]
            queries, keys, values = [projected_ref[rows, part] for part in columns]
            grads = both_heads(
                grad_attended[rows, pair * width : (pair + 1) * width], first, second
            )
            probs = probs_ref[block, pair]
            grad_probs = dot_nt(grads, values)
            grad_scores = (
                probs * (grad_probs - jnp.sum(probs * grad_probs, axis=-1, keepdims=True))
            ).astype(bf16)
            projected_grad_ref[rows, columns[0]] = (
                own_lanes(low, dot(grad_scores, keys)) * scale_qk
            ).astype(bf16)
            projected_grad_ref[rows, columns[1]] = (
                dot_tn(grad_scores, both_heads(queries, first, second)) * scale_qk
            ).astype(bf16)
            projected_grad_ref[rows, columns[2]] = dot_tn(probs.astype(bf16), grads).astype(bf16)
            if full:
                scores_total = scores_total + jnp.concatenate(
                    [dot(reverse, grad_scores[:SLOT]), dot(reverse, grad_scores[SLOT:])], axis=0
                )
        if full:
            for own in range(2):
                part = scores_total[own * SLOT : (own + 1) * SLOT]
                wide = jnp.concatenate([part, jnp.zeros_like(part)], axis=1)
                moved = pltpu.roll(wide, 1, 1, stride=1, stride_axis=0)
                rest[2][2 * pair + own : 2 * pair + own + 1] = jnp.sum(
                    moved, axis=0, keepdims=True
                )
    inputs = inputs_ref[...]
    grad_normed = dot_nt(projected_grad_ref[...], weight_ref[:, : 3 * D])
    grad_inputs_norm, grad_gain_one = norm_backward(grad_normed, inputs, gains_ref[0:1])
    grad_inputs_ref[...] = grad_middle + grad_inputs_norm
    if full:
        dense_ref, small_ref = rest[0], rest[1]
        normed = (inputs * rms_scale(inputs) * gains_ref[0:1]).astype(bf16)
        routed = (middle * rms_scale(middle) * gains_ref[1:2]).astype(bf16)
        for part in range(3):
            columns = slice(part * D, (part + 1) * D)
            dense_ref[:, columns] = dot_tn(normed, projected_grad_ref[:, columns]).astype(bf16)
        dense_ref[:, 3 * D :] = dot_tn(attended_ref[...], grad_branch).astype(bf16)
        small_ref[0:1] = grad_gain_one[None]
        small_ref[1:2] = grad_gain_two[None]
        small_ref[8:] = dot_tn(grad_logits, routed)[:experts]


def front_call(inputs, dense, fixed):
    gains, weight, router, diagonals = dense
    same_seq, route_ids, targets, placing = fixed
    extent = inputs.shape[0]
    experts = lax.axis_size("dp") // 2
    shape = jax.ShapeDtypeStruct
    return pl.pallas_call(
        functools.partial(front_kernel, experts),
        out_shape=(
            shape((placing.shape[1], D), bf16),
            shape((extent, 3 * D), bf16),
            shape((extent // SLOT, HEADS // 2, 2 * SLOT, SLOT), f32),
            shape((extent, D), bf16),
            shape((extent, D), f32),
            shape((extent, router.shape[0]), f32),
            shape((extent, 1), f32),
        ),
        compiler_params=pltpu.CompilerParams(vmem_limit_bytes=50 * 1024 * 1024),
        cost_estimate=pl.CostEstimate(
            flops=2 * extent * D * 4 * D, bytes_accessed=12_000_000, transcendentals=400_000
        ),
        name="attention_front",
    )(inputs, gains, weight, router, diagonals, same_seq, route_ids[:, None], targets[None, :])


def back_call(grad_out, returned, kept, dense, fixed, full):
    gains, weight, router, diagonals = dense
    same_seq, route_ids, targets, placing = fixed
    inputs, projected, probs, attended, middle, route_probs, gate, result = kept
    extent = inputs.shape[0]
    experts = lax.axis_size("dp") // 2
    shape = jax.ShapeDtypeStruct
    out_shape = [shape((extent, D), f32)]
    if full:
        out_shape = out_shape + [
            shape((D, 4 * D), bf16),
            shape((8 + experts, D), f32),
            shape((HEADS, 2 * SLOT), f32),
        ]
    return pl.pallas_call(
        functools.partial(back_kernel, experts, full),
        out_shape=tuple(out_shape),
        scratch_shapes=[pltpu.VMEM((extent, 3 * D), bf16)],
        compiler_params=pltpu.CompilerParams(vmem_limit_bytes=50 * 1024 * 1024),
        cost_estimate=pl.CostEstimate(
            flops=4 * extent * D * 4 * D, bytes_accessed=20_000_000, transcendentals=1000
        ),
        name="attention_back_full" if full else "attention_back",
    )(
        grad_out,
        returned,
        targets[:, None],
        route_ids[:, None],
        inputs,
        gains,
        weight,
        router,
        projected,
        probs,
        attended,
        middle,
        route_probs,
        gate,
        result,
    )


def gelu_parts(hidden):
    rate, cubic = 0.7978845608028654, 0.044715
    squared = hidden * hidden
    bend = jnp.tanh(rate * hidden * (1.0 + cubic * squared))
    active = 0.5 * hidden * (1.0 + bend)
    slope = 0.5 * (1.0 + bend) + 0.5 * hidden * (1.0 - bend * bend) * rate * (
        1.0 + 3.0 * cubic * squared
    )
    return (active.astype(bf16), slope.astype(bf16))


def layer_forward(inputs, dense, fixed, experts_held):
    placing = fixed[-1]
    weight_in, weight_out = experts_held
    packed, projected, probs, attended, middle, route_probs, gate = front_call(
        inputs, dense, fixed
    )
    arrived = to_experts(packed)
    active, slope = zip(*[gelu_parts(dot(rows, weight_in)) for rows in arrived])
    replies = [dot(rows, weight_out) for rows in active]
    result = dot(placing, from_experts(replies[0], replies[1]))
    outputs = middle + gate * result
    kept = (inputs, projected, probs, attended, middle, route_probs, gate, result)
    return (outputs, kept, (arrived, active, slope))


def layer_backward(grad_out, kept, expert_kept, dense, fixed, experts_held, full):
    arrived, active, slope = expert_kept
    placing = fixed[-1]
    weight_in, weight_out = experts_held
    grad_result = (kept[6] * grad_out).astype(bf16)
    grad_rows = to_experts(
        jnp.einsum("ts,td->sd", placing, grad_result, preferred_element_type=f32).astype(bf16)
    )
    grad_hidden = [
        (
            jnp.einsum("rd,fd->rf", rows, weight_out, preferred_element_type=f32)
            * steep.astype(f32)
        ).astype(bf16)
        for rows, steep in zip(grad_rows, slope)
    ]
    grad_sent = [
        jnp.einsum("rf,df->rd", rows, weight_in, preferred_element_type=f32)
        for rows in grad_hidden
    ]
    returned = from_experts(grad_sent[0], grad_sent[1])
    outs = back_call(grad_out, returned, kept, dense, fixed, full)
    if not full:
        return outs[0]
    grad_expert_out = jnp.einsum(
        "krf,krd->fd", jnp.stack(active), jnp.stack(grad_rows), preferred_element_type=f32
    )
    grad_expert_in = jnp.einsum(
        "krd,krf->df", jnp.stack(arrived), jnp.stack(grad_hidden), preferred_element_type=f32
    )
    return (*outs, grad_expert_in, grad_expert_out)


def pack_small(gains, router, table):
    rows = 8 + router.shape[1]
    packed = jnp.zeros((rows + -rows % 16, 128), bf16)
    packed = packed.at[0:2, : gains.shape[1]].set(gains)
    packed = packed.at[2, : table.shape[0]].set(table)
    return packed.at[8:rows, : router.shape[0]].set(router.T)


def unpack_small(packed, devices, experts):
    extent = D // devices
    packed = packed.reshape(devices, -1, 128).swapaxes(0, 1)
    gains = packed[0:2, :, :extent].reshape(2, D).astype(f32)
    table = packed[2, :, : BUCKETS * HEADS // devices].reshape(BUCKETS, HEADS).astype(f32)
    router = packed[8 : 8 + experts, :, :extent].reshape(experts, D)
    return (gains, table, jnp.pad(router, ((0, -experts % 128), (0, 0))))


def scatter_dense(packed):
    devices = lax.axis_size("dp")
    core = lax.axis_index("dp") % 2
    packed = packed.reshape(devices // 2, 2, D // devices, -1)
    mine = lax.dynamic_index_in_dim(packed, core, axis=1, keepdims=False)
    others = lax.dynamic_index_in_dim(packed, 1 - core, axis=1, keepdims=False)
    summed = (mine.astype(f32) + pair_swap(others).astype(f32)).astype(bf16)
    return jnp.sum(chip_all_to_all(summed).astype(f32), axis=0)


def scatter_small(small, table, devices):
    entries = jnp.pad(
        table.reshape(devices, -1), ((0, 0), (0, D // devices - table.size // devices))
    )
    small = small.at[2].set(entries.reshape(-1))
    small = small.reshape(-1, devices, D // devices).swapaxes(0, 1)
    small = jnp.pad(small, ((0, 0), (0, 0), (0, 128 - D // devices)))
    total = jnp.sum(
        lax.all_to_all(small, "dp", split_axis=0, concat_axis=0, tiled=True), axis=0
    )
    return (
        total[0:2, : D // devices],
        total[8:, : D // devices].T,
        total[2, : table.size // devices],
    )


def shards(
    edge_rows,
    lengths,
    routes,
    norm_gains,
    qkv_weight,
    out_weight,
    router_weight,
    bias_table,
    expert_in,
    expert_out,
):
    devices = lax.axis_size("dp")
    experts = devices // 2
    first_section = lax.axis_index("section") == 0
    local_rows = edge_rows[0].astype(f32)
    onehot = bucket_onehot()
    experts_held = (expert_in[0], expert_out[0])
    weight = lax.all_gather(
        jnp.concatenate([qkv_weight[0], out_weight[0]], axis=1), "dp", axis=0, tiled=True
    )
    small = lax.all_gather(
        pack_small(norm_gains[0], router_weight[0], bias_table[0]), "dp", axis=0, tiled=True
    )
    gains, table, router = unpack_small(small, devices, experts)
    diagonals = jnp.einsum("ib,bh->hi", onehot, table, precision=lax.Precision.HIGHEST)
    dense = (gains, weight, router, diagonals)
    route_ids = routes[0, :, 0]
    targets, placing = expert_places(route_ids.reshape(-1, SLOT), experts, 4 * SLOT // devices)
    fixed = (same_sequence(lengths), route_ids, targets, placing)
    outputs, _, _ = layer_forward(local_rows, dense, fixed, experts_held)
    carried = section_shift(outputs.astype(bf16), 1).astype(f32)
    inputs = jnp.where(first_section, local_rows, carried)
    outputs, kept, expert_kept = layer_forward(inputs, dense, fixed, experts_held)
    grad_inputs = layer_backward(
        local_rows, kept, expert_kept, dense, fixed, experts_held, False
    )
    carried = section_shift(grad_inputs.astype(bf16), -1).astype(f32)
    grad_out = jnp.where(first_section, carried, local_rows)
    grad_inputs, dense_grads, small_grads, diagonal_grads, grad_in, grad_exp_out = layer_backward(
        grad_out, kept, expert_kept, dense, fixed, experts_held, True
    )
    edge_results = jnp.where(first_section, grad_inputs, outputs)
    grad_table = jnp.einsum(
        "ib,hi->bh", onehot, diagonal_grads, precision=lax.Precision.HIGHEST
    ).reshape(-1)
    grad_gains, grad_router, grad_table = scatter_small(small_grads, grad_table, devices)
    total = scatter_dense(dense_grads)
    return (
        edge_results[None],
        grad_gains[None],
        total[None, :, : 3 * D],
        total[None, :, 3 * D :],
        grad_router[None],
        grad_table[None],
        grad_in[None],
        grad_exp_out[None],
    )


def solution(mesh):
    return jax.shard_map(
        shards,
        mesh=mesh,
        in_specs=(
            P("section", "dp", None),
            P("dp", None),
            P("section", "dp", None),
            P("section", None, "dp"),
            P("section", "dp", None),
            P("section", "dp", None),
            P("section", "dp", None),
            P("section", "dp"),
            P("section", None, "dp"),
            P("section", "dp", None),
        ),
        out_specs=(
            P("section", "dp", None),
            P("section", None, "dp"),
            P("section", "dp", None),
            P("section", "dp", None),
            P("section", "dp", None),
            P("section", "dp"),
            P("section", None, "dp"),
            P("section", "dp", None),
        ),
        check_vma=False,
    )
```

```python
import functools

import jax
import jax.numpy as jnp
from jax import lax
from jax.experimental import pallas as pl
from jax.experimental.pallas import tpu as pltpu
from jax.sharding import PartitionSpec as P

D = 768
HEADS = 12
HEAD_DIM = 64
BUCKETS = 32
SLOT = 128


norm_eps = 1e-06
masked_score = -1e30
bucket_edges = (1, 2, 3, 4, 5, 6, 7, 8, 12, 16, 23, 32, 46, 64, 91)
bf16 = jnp.bfloat16
f32 = jnp.float32


def dot(lhs, rhs):
    return jnp.dot(lhs, rhs, preferred_element_type=f32)


def section_shift(block, distance):
    devices = range(lax.axis_size("section"))
    route = [(i - distance, i) for i in devices if i - distance in devices]
    return lax.ppermute(block, "section", route)


def pair_swap(block):
    return lax.ppermute(block, "dp", [(i, i ^ 1) for i in range(lax.axis_size("dp"))])


def chip_all_to_all(block):
    devices = lax.axis_size("dp")
    groups = [list(range(core, devices, 2)) for core in range(2)]
    return lax.all_to_all(
        block, "dp", split_axis=0, concat_axis=0, tiled=True, axis_index_groups=groups
    )


def rms_scale(values):
    return lax.rsqrt(jnp.mean(values * values, axis=-1, keepdims=True) + norm_eps)


def norm_backward(grad_normed, values, gain_row):
    inv_rms = rms_scale(values)
    weighted = grad_normed * gain_row
    grad_gain = jnp.sum(grad_normed * values * inv_rms, axis=0)
    grad_values = inv_rms * weighted - values * inv_rms**3 * jnp.mean(
        weighted * values, axis=-1, keepdims=True
    )
    return (grad_values, grad_gain)


def bucket_onehot():
    offset = jnp.arange(2 * SLOT, dtype=jnp.int32) - SLOT
    distance = jnp.abs(offset)
    bucket = jnp.zeros_like(distance)
    for threshold in bucket_edges:
        bucket = bucket + (distance >= threshold).astype(jnp.int32)
    bucket = bucket + BUCKETS // 2 * (offset > 0).astype(jnp.int32)
    return (bucket[:, None] == jnp.arange(BUCKETS, dtype=jnp.int32)).astype(f32)


def same_sequence(lengths):
    bounds = jnp.cumsum(lengths, axis=-1)
    places = jnp.arange(SLOT, dtype=jnp.int32)
    owners = jnp.sum((places[:, None] >= bounds[:, None, :]).astype(jnp.int32), axis=-1)
    return (owners[:, :, None] == owners[:, None, :]).astype(f32)


def expert_places(route_ids, experts, capacity):
    names = jnp.arange(experts, dtype=jnp.int32)
    choose = (route_ids[:, None] == names).astype(jnp.int32)
    places = jnp.arange(SLOT, dtype=jnp.int32)
    earlier = (places[:, None] > places[None, :]).astype(bf16)
    before = dot(earlier, choose.astype(bf16)).astype(jnp.int32)
    rank_ids = jnp.sum(before * choose, axis=-1)
    return route_ids * capacity + rank_ids


def to_experts(packed):
    width = packed.shape[-1]
    experts = lax.axis_size("dp") // 2
    arrived = chip_all_to_all(packed.reshape(experts, -1, width)).reshape(-1, width)
    return (arrived, pair_swap(arrived))


def from_experts(own, other):
    width = own.shape[-1]
    summed = (own.astype(f32) + pair_swap(other).astype(f32)).astype(bf16)
    experts = lax.axis_size("dp") // 2
    return chip_all_to_all(summed.reshape(experts, -1, width)).reshape(-1, width)


def dot_nt(lhs, rhs):
    return lax.dot_general(lhs, rhs, (((1,), (1,)), ((), ())), preferred_element_type=f32)


def dot_tn(lhs, rhs):
    return lax.dot_general(lhs, rhs, (((0,), (0,)), ((), ())), preferred_element_type=f32)


def lane_masks():
    low = lax.broadcasted_iota(jnp.int32, (1, 2 * HEAD_DIM), 1) < HEAD_DIM
    first = jnp.where(low, 1.0, 0.0)
    return (low, first.astype(bf16), (1.0 - first).astype(bf16))


def both_heads(slab, first, second):
    return jnp.concatenate([slab * first, slab * second], axis=0)


def own_lanes(low, stacked):
    return jnp.where(low, stacked[:SLOT], stacked[SLOT:])


def gelu_parts(hidden):
    rate, cubic = 0.7978845608028654, 0.044715
    squared = hidden * hidden
    bend = jnp.tanh(rate * hidden * (1.0 + cubic * squared))
    active = 0.5 * hidden * (1.0 + bend)
    slope = 0.5 * (1.0 + bend) + 0.5 * hidden * (1.0 - bend * bend) * rate * (
        1.0 + 3.0 * cubic * squared
    )
    return (active.astype(bf16), slope.astype(bf16))


def placing_of(targets, slots, dtype=bf16):
    return jnp.where(slots == targets, 1.0, 0.0).astype(dtype)


def front_kernel(experts, cotangent, *refs):
    if cotangent:
        cotangent_ref, refs = refs[0], refs[1:]
    (
        inputs_ref,
        gains_ref,
        weight_ref,
        router_ref,
        diagonals_ref,
        same_ref,
        route_ref,
        target_ref,
        packed_ref,
        projected_ref,
        probs_ref,
        attended_ref,
        middle_ref,
        route_probs_ref,
        gate_ref,
    ) = refs
    inputs = inputs_ref[...]
    normed = (inputs * rms_scale(inputs) * gains_ref[0:1]).astype(bf16)
    projected_ref[...] = dot(normed, weight_ref[:, : 3 * D]).astype(bf16)
    low, first, second = lane_masks()
    width = 2 * HEAD_DIM
    same = same_ref[...]
    same = jnp.concatenate([same, same], axis=0) > 0
    for pair in range(HEADS // 2):
        relative = jnp.concatenate(
            [
                pltpu.roll(
                    jnp.broadcast_to(diagonals_ref[head : head + 1], (SLOT, 2 * SLOT)),
                    SLOT,
                    1,
                    stride=1,
                    stride_axis=0,
                )[:, :SLOT]
                for head in (2 * pair, 2 * pair + 1)
            ],
            axis=0,
        )
        queries, keys, values = [
            projected_ref[:, part * D + pair * width : part * D + (pair + 1) * width]
            for part in range(3)
        ]
        scores = dot_nt(both_heads(queries, first, second), keys) * HEAD_DIM ** (-0.5) + relative
        scores = jnp.where(same, scores, masked_score)
        raised = jnp.exp(scores - jnp.max(scores, axis=-1, keepdims=True))
        probs = raised / jnp.sum(raised, axis=-1, keepdims=True)
        probs_ref[pair] = probs
        attended_ref[:, pair * width : (pair + 1) * width] = own_lanes(
            low, dot(probs.astype(bf16), values)
        ).astype(bf16)
    middle = inputs + dot(attended_ref[...], weight_ref[:, 3 * D :])
    middle_ref[...] = middle
    routed = (middle * rms_scale(middle) * gains_ref[1:2]).astype(bf16)
    logits = dot_nt(routed, router_ref[...])
    names = lax.broadcasted_iota(jnp.int32, (1, logits.shape[1]), 1)
    logits = jnp.where(names < experts, logits, masked_score)
    raised = jnp.exp(logits - jnp.max(logits, axis=-1, keepdims=True))
    route_probs = raised / jnp.sum(raised, axis=-1, keepdims=True)
    route_probs_ref[...] = route_probs
    gate = jnp.sum(jnp.where(names == route_ref[...], route_probs, 0.0), axis=-1, keepdims=True)
    gate_ref[...] = gate
    slots = lax.broadcasted_iota(jnp.int32, (packed_ref.shape[0], 1), 0)
    placing = placing_of(target_ref[...], slots)
    packed_ref[:, :D] = dot(placing, routed).astype(bf16)
    if cotangent:
        grad_result = (gate * cotangent_ref[...]).astype(bf16)
        packed_ref[:, D:] = dot(placing, grad_result).astype(bf16)


def expert_kernel(forward, backward, keep, own_ref, other_ref, *refs):
    if backward and not forward:
        slope_ref, refs = refs[0], refs[1:]
    weight_in_ref, weight_out_ref, own_out_ref, other_out_ref = refs[:4]
    kept_refs = refs[4:]
    grad_at = slice(D, 2 * D) if forward else slice(0, D)
    extent = own_ref.shape[0]
    rows = jnp.concatenate([own_ref[...], other_ref[...]], axis=0)
    hidden_units = weight_in_ref.shape[1]
    step = 512
    reply = jnp.zeros((2 * extent, D), f32)
    grad_reply = jnp.zeros((2 * extent, D), f32)
    for start in range(0, hidden_units, step):
        units = slice(start, start + step)
        if forward:
            active, slope = gelu_parts(dot(rows[:, :D], weight_in_ref[:, units]))
            reply = reply + dot(active, weight_out_ref[units])
            if keep:
                kept_refs[0][:, units] = active
                kept_refs[1][:, units] = slope.astype(bf16)
        else:
            slope = slope_ref[:, units]
        if backward:
            grad_hidden = (
                dot_nt(rows[:, grad_at], weight_out_ref[units]) * slope.astype(f32)
            ).astype(bf16)
            grad_reply = grad_reply + dot_nt(grad_hidden, weight_in_ref[:, units])
            if not forward:
                kept_refs[0][:, units] = grad_hidden
    if forward:
        own_out_ref[:, :D] = reply[:extent].astype(own_out_ref.dtype)
        other_out_ref[:, :D] = reply[extent:].astype(bf16)
    if backward:
        own_out_ref[:, grad_at] = grad_reply[:extent].astype(own_out_ref.dtype)
        other_out_ref[:, grad_at] = grad_reply[extent:].astype(bf16)


def merge_back(
    grad_out, result, grad_sent, middle, gate, route_probs, route, router_ref, gains_ref
):
    grad_gate = jnp.sum(grad_out * result, axis=-1, keepdims=True)
    names = lax.broadcasted_iota(jnp.int32, (1, router_ref.shape[0]), 1)
    choose = jnp.where(names == route, 1.0, 0.0)
    grad_logits = (grad_gate * gate * (choose - route_probs)).astype(bf16)
    grad_routed = grad_sent + dot(grad_logits, router_ref[...])
    grad_middle_norm, grad_gain = norm_backward(grad_routed, middle, gains_ref[1:2])
    return (grad_out + grad_middle_norm, grad_gain, grad_logits)


def attention_back(
    grad_middle, inputs, gains_ref, weight_ref, projected_ref, probs_ref, grads_ref, table_ref
):
    grad_attended = dot_nt(grad_middle.astype(bf16), weight_ref[:, 3 * D :]).astype(bf16)
    low, first, second = lane_masks()
    width = 2 * HEAD_DIM
    scale_qk = HEAD_DIM ** (-0.5)
    places = [lax.broadcasted_iota(jnp.int32, (SLOT, SLOT), axis) for axis in range(2)]
    reverse = jnp.where(places[0] + places[1] == SLOT - 1, 1.0, 0.0).astype(bf16)
    for pair in range(HEADS // 2):
        columns = [
            slice(part * D + pair * width, part * D + (pair + 1) * width) for part in range(3)
        ]
        queries, keys, values = [projected_ref[:, part] for part in columns]
        grads = both_heads(grad_attended[:, pair * width : (pair + 1) * width], first, second)
        probs = probs_ref[pair]
        grad_probs = dot_nt(grads, values)
        grad_scores = (
            probs * (grad_probs - jnp.sum(probs * grad_probs, axis=-1, keepdims=True))
        ).astype(bf16)
        grads_ref[:, columns[0]] = (own_lanes(low, dot(grad_scores, keys)) * scale_qk).astype(bf16)
        grads_ref[:, columns[1]] = (
            dot_tn(grad_scores, both_heads(queries, first, second)) * scale_qk
        ).astype(bf16)
        grads_ref[:, columns[2]] = dot_tn(probs.astype(bf16), grads).astype(bf16)
        if table_ref is not None:
            for own in range(2):
                part = dot(reverse, grad_scores[own * SLOT : (own + 1) * SLOT])
                wide = jnp.concatenate([part, jnp.zeros_like(part)], axis=1)
                moved = pltpu.roll(wide, 1, 1, stride=1, stride_axis=0)
                head = 2 * pair + own
                table_ref[head : head + 1] = jnp.sum(moved, axis=0, keepdims=True)
    grad_normed = dot_nt(grads_ref[...], weight_ref[:, : 3 * D])
    grad_inputs_norm, grad_gain = norm_backward(grad_normed, inputs, gains_ref[0:1])
    return (grad_middle + grad_inputs_norm, grad_gain)


def turn_kernel(
    cotangent_ref,
    returned_ref,
    target_ref,
    route_ref,
    inputs_ref,
    gains_ref,
    weight_ref,
    router_ref,
    projected_ref,
    probs_ref,
    middle_ref,
    route_probs_ref,
    gate_ref,
    outputs_ref,
    result_ref,
    grad_inputs_ref,
    grads_ref,
):
    slots = lax.broadcasted_iota(jnp.int32, (1, returned_ref.shape[0]), 1)
    both = dot(placing_of(target_ref[...], slots), returned_ref[...])
    result = both[:, :D]
    result_ref[...] = result
    middle, gate = middle_ref[...], gate_ref[...]
    outputs_ref[...] = middle + gate * result
    grad_middle, _, _ = merge_back(
        cotangent_ref[...].astype(f32),
        result,
        both[:, D:],
        middle,
        gate,
        route_probs_ref[...],
        route_ref[...],
        router_ref,
        gains_ref,
    )
    grad_inputs_ref[...], _ = attention_back(
        grad_middle,
        inputs_ref[...],
        gains_ref,
        weight_ref,
        projected_ref,
        probs_ref,
        grads_ref,
        None,
    )


def merge_kernel(
    experts,
    grad_out_ref,
    returned_ref,
    target_ref,
    route_ref,
    gains_ref,
    router_ref,
    middle_ref,
    route_probs_ref,
    gate_ref,
    result_ref,
    grad_middle_ref,
    small_ref,
):
    slots = lax.broadcasted_iota(jnp.int32, (1, returned_ref.shape[0]), 1)
    middle = middle_ref[...]
    grad_middle, grad_gain, grad_logits = merge_back(
        grad_out_ref[...],
        result_ref[...],
        dot(placing_of(target_ref[...], slots), returned_ref[...]),
        middle,
        gate_ref[...],
        route_probs_ref[...],
        route_ref[...],
        router_ref,
        gains_ref,
    )
    grad_middle_ref[...] = grad_middle
    routed = (middle * rms_scale(middle) * gains_ref[1:2]).astype(bf16)
    small_ref[0:8] = jnp.broadcast_to(grad_gain[None], (8, D))
    small_ref[8:] = dot_tn(grad_logits, routed)[:experts]


def attention_back_kernel(
    grad_middle_ref,
    inputs_ref,
    gains_ref,
    weight_ref,
    projected_ref,
    probs_ref,
    grad_inputs_ref,
    grads_ref,
    gain_ref,
    table_ref,
):
    grad_inputs_ref[...], grad_gain = attention_back(
        grad_middle_ref[...],
        inputs_ref[...],
        gains_ref,
        weight_ref,
        projected_ref,
        probs_ref,
        grads_ref,
        table_ref,
    )
    gain_ref[...] = grad_gain[None]


def out_grad_kernel(blocks, *refs):
    out_ref = refs[-1]
    total = jnp.zeros(out_ref.shape, f32)
    for attended_ref, grad_middle_ref in zip(refs[:blocks], refs[blocks : 2 * blocks]):
        total = total + dot_tn(attended_ref[...], grad_middle_ref[...].astype(bf16))
    out_ref[...] = total.astype(bf16)


def qkv_grad_kernel(blocks, experts, order_ref, gains_ref, spread_ref, owner_ref, *refs):
    mine_ref, others_ref, wide_ref = refs[-3:]
    inputs_refs, grads_refs, gain_refs, table_refs, small_refs = [
        refs[part * blocks : (part + 1) * blocks] for part in range(5)
    ]
    ordering = jnp.where(
        lax.broadcasted_iota(jnp.int32, (D, 1), 0) == order_ref[...], 1.0, 0.0
    ).astype(bf16)
    half = D // 2
    normed = []
    for inputs_ref in inputs_refs:
        inputs = inputs_ref[...]
        own = (inputs * rms_scale(inputs) * gains_ref[0:1]).astype(bf16)
        normed.append(dot(own, ordering).astype(bf16))
    normed = jnp.concatenate(normed, axis=0)
    for part in range(3):
        columns = slice(part * D, (part + 1) * D)
        grads = jnp.concatenate([grads_ref[:, columns] for grads_ref in grads_refs], axis=0)
        total = dot_tn(normed, grads).astype(bf16)
        mine_ref[:, columns] = total[:half]
        others_ref[:, columns] = total[half:]
    diagonals = sum([table_ref[...] for table_ref in table_refs])
    entries = jnp.sum(
        owner_ref[...]
        * jnp.dot(
            diagonals,
            spread_ref[...],
            preferred_element_type=f32,
            precision=lax.Precision.HIGHEST,
        ),
        axis=0,
        keepdims=True,
    )
    small = sum([small_ref[...] for small_ref in small_refs])
    wide_ref[...] = jnp.zeros_like(wide_ref)
    wide_ref[0:1] = sum([gain_ref[...] for gain_ref in gain_refs])
    wide_ref[1:2] = small[0:1]
    wide_ref[2:3] = entries
    wide_ref[8 : 8 + experts] = small[8:]
    columns = dot_tn(ordering, wide_ref[...].T.astype(bf16)).astype(bf16)
    mine_ref[:, 3 * D :] = columns[:half]
    others_ref[:, 3 * D :] = columns[half:]


def kernel_call(kernel, name, out_shape, operands, micros, scratch=()):
    return pl.pallas_call(
        kernel,
        out_shape=tuple(jax.ShapeDtypeStruct(*pair) for pair in out_shape),
        scratch_shapes=list(scratch),
        compiler_params=pltpu.CompilerParams(vmem_limit_bytes=48 * 1024 * 1024),
        cost_estimate=pl.CostEstimate(
            flops=int(micros * 5e8), bytes_accessed=int(micros * 3e6), transcendentals=0
        ),
        name=name,
    )(*operands)


def front_call(inputs, cotangent, dense, place):
    gains, weight, router, diagonals = dense
    same_seq, route_ids, targets, slots = place
    width = D if cotangent is None else 2 * D
    return kernel_call(
        functools.partial(front_kernel, lax.axis_size("dp") // 2, cotangent is not None),
        "attention_front",
        (
            ((slots, width), bf16),
            ((SLOT, 3 * D), bf16),
            ((HEADS // 2, 2 * SLOT, SLOT), f32),
            ((SLOT, D), bf16),
            ((SLOT, D), f32),
            ((SLOT, router.shape[0]), f32),
            ((SLOT, 1), f32),
        ),
        (() if cotangent is None else (cotangent,))
        + (inputs, gains, weight, router, diagonals, same_seq)
        + (route_ids[:, None], targets[None, :]),
        5,
    )


def expert_call(arrived, slope, experts_held, forward, backward, keep):
    own, other = arrived
    extent, units = own.shape[0], experts_held[0].shape[1]
    width = 2 * D if forward and backward else D
    kept = 0 if not keep else 2 if forward else 1
    return kernel_call(
        functools.partial(expert_kernel, forward, backward, keep),
        "experts_" + ("f" if forward else "") + ("b" if backward else ""),
        (((extent, width), f32), ((extent, width), bf16))
        + (((2 * extent, units), bf16),) * kept,
        (own, other) + (() if slope is None else (slope,)) + experts_held,
        6 if width == D else 10,
    )


def turn_call(cotangent, returned, inputs, kept, dense, place):
    gains, weight, router, _ = dense
    _, route_ids, targets, _ = place
    projected, probs, _, middle, route_probs, gate = kept
    rows = ((SLOT, D), f32)
    return kernel_call(
        turn_kernel,
        "turn_back",
        (rows, rows, rows, ((SLOT, 3 * D), bf16)),
        (cotangent, returned, targets[:, None], route_ids[:, None], inputs, gains, weight)
        + (router, projected, probs, middle, route_probs, gate),
        7,
    )


def merge_call(grad_out, returned, result, kept, dense, place):
    gains, weight, router, _ = dense
    _, route_ids, targets, _ = place
    _, _, _, middle, route_probs, gate = kept
    experts = lax.axis_size("dp") // 2
    return kernel_call(
        functools.partial(merge_kernel, experts),
        "merge_back",
        (((SLOT, D), f32), ((8 + experts, D), f32)),
        (grad_out, returned, targets[:, None], route_ids[:, None], gains, router, middle)
        + (route_probs, gate, result),
        2,
    )


def attention_back_call(grad_middle, inputs, kept, dense):
    gains, weight, _, _ = dense
    projected, probs = kept[:2]
    return kernel_call(
        attention_back_kernel,
        "attention_back",
        (
            ((SLOT, D), f32),
            ((SLOT, 3 * D), bf16),
            ((1, D), f32),
            ((HEADS, 2 * SLOT), f32),
        ),
        (grad_middle, inputs, gains, weight, projected, probs),
        7,
    )


def pack_small(gains, router, table):
    rows = 8 + router.shape[1]
    packed = jnp.zeros((rows + -rows % 16, 128), bf16)
    packed = packed.at[0:2, : gains.shape[1]].set(gains)
    packed = packed.at[2, : table.shape[0]].set(table)
    return packed.at[8:rows, : router.shape[0]].set(router.T)


def unpack_small(packed, devices, experts):
    extent = D // devices
    packed = packed.reshape(devices, -1, 128).swapaxes(0, 1)
    gains = packed[0:2, :, :extent].reshape(2, D).astype(f32)
    table = packed[2, :, : BUCKETS * HEADS // devices].reshape(BUCKETS, HEADS).astype(f32)
    router = packed[8 : 8 + experts, :, :extent].reshape(experts, D)
    return (gains, table, jnp.pad(router, ((0, -experts % 128), (0, 0))))


def scatter_dense(mine, others, devices):
    summed = (mine.astype(f32) + pair_swap(others).astype(f32)).astype(bf16)
    summed = summed.reshape(devices // 2, D // devices, -1)
    return jnp.sum(chip_all_to_all(summed).astype(f32), axis=0)


def feature_order(devices):
    extent = D // devices
    places = jnp.arange(D, dtype=jnp.int32)
    chip, row = places % (D // 2) // extent, places % extent
    core = (places // (D // 2) + lax.axis_index("dp") % 2) % 2
    return ((2 * chip + core) * extent + row)[None]


def table_places(onehot, devices):
    extent, used = D // devices, BUCKETS * HEADS // devices
    places = jnp.arange(D, dtype=jnp.int32)
    entry = jnp.where(places % extent < used, places // extent * used + places % extent, -HEADS)
    bucket, head = entry // HEADS, entry % HEADS
    spread = jnp.take(onehot, jnp.maximum(bucket, 0), axis=1) * (bucket >= 0).astype(f32)
    owner = (head[None] == jnp.arange(HEADS, dtype=jnp.int32)[:, None]).astype(f32)
    return (spread, owner)


def shards(
    edge_rows,
    lengths,
    routes,
    norm_gains,
    qkv_weight,
    out_weight,
    router_weight,
    bias_table,
    expert_in,
    expert_out,
):
    devices = lax.axis_size("dp")
    experts = devices // 2
    first_section = lax.axis_index("section") == 0
    onehot = bucket_onehot()
    experts_held = (expert_in[0], expert_out[0])
    weight = lax.all_gather(
        jnp.concatenate([qkv_weight[0], out_weight[0]], axis=1), "dp", axis=0, tiled=True
    )
    small = lax.all_gather(
        pack_small(norm_gains[0], router_weight[0], bias_table[0]), "dp", axis=0, tiled=True
    )
    gains, table, router = unpack_small(small, devices, experts)
    diagonals = jnp.einsum("ib,bh->hi", onehot, table, precision=lax.Precision.HIGHEST)
    dense = (gains, weight, router, diagonals)
    same_seq = same_sequence(lengths)
    capacity = 4 * SLOT // devices
    blocks = range(edge_rows.shape[1] // SLOT)
    local_rows = [edge_rows[0, b * SLOT : (b + 1) * SLOT].astype(f32) for b in blocks]
    routes_of = [routes[0, b * SLOT : (b + 1) * SLOT, 0] for b in blocks]
    places = [
        (same_seq[b], routes_of[b], expert_places(routes_of[b], experts, capacity), experts * capacity)
        for b in blocks
    ]
    slot_ids = jnp.arange(experts * capacity, dtype=jnp.int32)
    placings = [
        (place[2][:, None] == slot_ids[None]).astype(bf16) for place in places
    ]

    inputs = []
    for b in blocks:
        packed, _, _, _, middle, _, gate = front_call(local_rows[b], None, dense, places[b])
        own, other = expert_call(to_experts(packed), None, experts_held, True, False, False)
        result = dot(placings[b], from_experts(own, other))
        carried = section_shift((middle + gate * result).astype(bf16), 1).astype(f32)
        inputs.append(jnp.where(first_section, local_rows[b], carried))

    outputs, grad_outs, kept, results, expert_kept = [], [], [], [], []
    for b in blocks:
        packed, *kept_now = front_call(inputs[b], local_rows[b], dense, places[b])
        arrived = to_experts(packed)
        own, other, active, slope = expert_call(arrived, None, experts_held, True, True, True)
        output, result, grad_inputs, _ = turn_call(
            local_rows[b], from_experts(own, other), inputs[b], kept_now, dense, places[b]
        )
        carried = section_shift(grad_inputs.astype(bf16), -1).astype(f32)
        outputs.append(output)
        kept.append(kept_now)
        results.append(result)
        expert_kept.append((arrived, active, slope))
        grad_outs.append(jnp.where(first_section, carried, local_rows[b]))

    grad_middles, smalls, expert_rows = [], [], []
    for b in blocks:
        grad_result = (kept[b][5] * grad_outs[b]).astype(bf16)
        grad_rows = to_experts(
            jnp.einsum(
                "ts,td->sd", placings[b], grad_result, preferred_element_type=f32
            ).astype(bf16)
        )
        arrived, active, slope = expert_kept[b]
        own, other, grad_hidden = expert_call(grad_rows, slope, experts_held, False, True, True)
        grad_middle, small = merge_call(
            grad_outs[b], from_experts(own, other), results[b], kept[b], dense, places[b]
        )
        grad_middles.append(grad_middle)
        smalls.append(small)
        expert_rows.append((arrived, active, grad_rows, grad_hidden))
    (grad_out_w,) = kernel_call(
        functools.partial(out_grad_kernel, len(blocks)),
        "out_gradient",
        (((D, D), bf16),),
        tuple(kept[b][2] for b in blocks) + tuple(grad_middles),
        2,
    )
    grad_out_w = lax.psum_scatter(grad_out_w, "dp", scatter_dimension=0, tiled=True)
    grad_inputs, grads, gain_ones, tables = zip(
        *[attention_back_call(grad_middles[b], inputs[b], kept[b], dense) for b in blocks]
    )
    mine, others = kernel_call(
        functools.partial(qkv_grad_kernel, len(blocks), experts),
        "qkv_gradient",
        (((D // 2, 3 * D + 128), bf16),) * 2,
        (feature_order(devices), gains, *table_places(onehot, devices))
        + (*inputs, *grads, *gain_ones, *tables, *smalls),
        4,
        (pltpu.VMEM((128, D), f32),),
    )
    total = scatter_dense(mine, others, devices)
    arrived, active, grad_rows, grad_hidden = zip(*expert_rows)
    arrived = jnp.concatenate([rows[:, :D] for pair in arrived for rows in pair])
    grad_rows = jnp.concatenate([rows for pair in grad_rows for rows in pair])
    grad_expert_out = jnp.einsum(
        "rf,rd->fd", jnp.concatenate(active), grad_rows, preferred_element_type=f32
    )
    grad_expert_in = jnp.einsum(
        "rd,rf->df", arrived, jnp.concatenate(grad_hidden), preferred_element_type=f32
    )
    edge_results = jnp.concatenate(
        [jnp.where(first_section, grad_inputs[b], outputs[b]) for b in blocks]
    )
    extra = total[:, 3 * D :]
    return (
        edge_results[None],
        extra[None, :, 0:2].swapaxes(1, 2),
        total[None, :, : 3 * D],
        grad_out_w[None].astype(f32),
        extra[None, :, 8 : 8 + experts],
        extra[None, : BUCKETS * HEADS // devices, 2],
        grad_expert_in[None],
        grad_expert_out[None],
    )


def solution(mesh):
    return jax.shard_map(
        shards,
        mesh=mesh,
        in_specs=(
            P("section", "dp", None),
            P("dp", None),
            P("section", "dp", None),
            P("section", None, "dp"),
            P("section", "dp", None),
            P("section", "dp", None),
            P("section", "dp", None),
            P("section", "dp"),
            P("section", None, "dp"),
            P("section", "dp", None),
        ),
        out_specs=(
            P("section", "dp", None),
            P("section", None, "dp"),
            P("section", "dp", None),
            P("section", "dp", None),
            P("section", "dp", None),
            P("section", "dp"),
            P("section", None, "dp"),
            P("section", "dp", None),
        ),
        check_vma=False,
    )
```

```python
import functools

import jax
import jax.numpy as jnp
import numpy as np
from jax import lax
from jax.experimental import pallas as pl
from jax.experimental.pallas import tpu as pltpu
from jax.sharding import PartitionSpec as P

D = 768
HEADS = 12
HEAD_DIM = 64
BUCKETS = 32
SLOT = 128


norm_eps = 1e-06
masked_score = -1e30
bucket_edges = (1, 2, 3, 4, 5, 6, 7, 8, 12, 16, 23, 32, 46, 64, 91)
bf16 = jnp.bfloat16
f32 = jnp.float32


def dot(lhs, rhs):
    return jnp.dot(lhs, rhs, preferred_element_type=f32)


def section_shift(block, distance):
    devices = range(lax.axis_size("section"))
    route = [(i - distance, i) for i in devices if i - distance in devices]
    return lax.ppermute(block, "section", route)


def pair_swap(block):
    return lax.ppermute(block, "dp", [(i, i ^ 1) for i in range(lax.axis_size("dp"))])


def chip_all_to_all(block):
    devices = lax.axis_size("dp")
    groups = [list(range(core, devices, 2)) for core in range(2)]
    return lax.all_to_all(
        block, "dp", split_axis=0, concat_axis=0, tiled=True, axis_index_groups=groups
    )


def rms_scale(values):
    return lax.rsqrt(jnp.mean(values * values, axis=-1, keepdims=True) + norm_eps)


def norm_backward(grad_normed, values, gain_row):
    inv_rms = rms_scale(values)
    weighted = grad_normed * gain_row
    grad_gain = jnp.sum(grad_normed * values * inv_rms, axis=0)
    grad_values = inv_rms * weighted - values * inv_rms**3 * jnp.mean(
        weighted * values, axis=-1, keepdims=True
    )
    return (grad_values, grad_gain)


def bucket_onehot():
    offset = np.arange(2 * SLOT) - SLOT
    bucket = np.sum(np.abs(offset)[:, None] >= np.array(bucket_edges), axis=1)
    bucket = bucket + BUCKETS // 2 * (offset > 0)
    return (bucket[:, None] == np.arange(BUCKETS)).astype(np.float32)


def same_sequence(lengths):
    bounds = jnp.cumsum(lengths, axis=-1)
    places = jnp.arange(SLOT, dtype=jnp.int32)
    owners = jnp.sum((places[:, None] >= bounds[:, None, :]).astype(jnp.int32), axis=-1)
    return (owners[:, :, None] == owners[:, None, :]).astype(f32)


def expert_places(route_ids, experts, capacity):
    names = jnp.arange(experts, dtype=jnp.int32)
    choose = (route_ids[:, None] == names).astype(jnp.int32)
    places = jnp.arange(SLOT, dtype=jnp.int32)
    earlier = (places[:, None] > places[None, :]).astype(bf16)
    before = dot(earlier, choose.astype(bf16)).astype(jnp.int32)
    rank_ids = jnp.sum(before * choose, axis=-1)
    return route_ids * capacity + rank_ids


def arrive(block):
    return (block, pair_swap(block))


def join_halves(own, other):
    return (own.astype(f32) + pair_swap(other).astype(f32)).astype(bf16)


def in_turns(streams):
    ends, values = [None] * len(streams), [None] * len(streams)
    travelling = None
    running = list(range(len(streams)))
    while running:
        for turn in list(running):
            try:
                block = streams[turn].send(values[turn])
            except StopIteration as stop:
                ends[turn] = stop.value
                running.remove(turn)
                if travelling is not None and running:
                    last, held = travelling
                    held, first = lax.optimization_barrier((held, ends[turn][0]))
                    ends[turn] = (first,) + ends[turn][1:]
                    values[last], travelling = held, None
                continue
            if travelling is not None:
                last, held = travelling
                held, block = lax.optimization_barrier((held, block))
                values[last] = held
            experts, width = lax.axis_size("dp") // 2, block.shape[-1]
            came = chip_all_to_all(block.reshape(experts, -1, width)).reshape(-1, width)
            values[turn], travelling = came, (turn, came)
    return ends


def dot_nt(lhs, rhs):
    return lax.dot_general(lhs, rhs, (((1,), (1,)), ((), ())), preferred_element_type=f32)


def dot_tn(lhs, rhs):
    return lax.dot_general(lhs, rhs, (((0,), (0,)), ((), ())), preferred_element_type=f32)


def lane_masks():
    low = lax.broadcasted_iota(jnp.int32, (1, 2 * HEAD_DIM), 1) < HEAD_DIM
    first = jnp.where(low, 1.0, 0.0)
    return (low, first.astype(bf16), (1.0 - first).astype(bf16))


def both_heads(slab, first, second):
    return jnp.concatenate([slab * first, slab * second], axis=0)


def own_lanes(low, stacked):
    return jnp.where(low, stacked[:SLOT], stacked[SLOT:])


def gelu_parts(hidden):
    rate, cubic = 0.7978845608028654, 0.044715
    squared = hidden * hidden
    bend = jnp.tanh(rate * hidden * (1.0 + cubic * squared))
    active = 0.5 * hidden * (1.0 + bend)
    slope = 0.5 * (1.0 + bend) + 0.5 * hidden * (1.0 - bend * bend) * rate * (
        1.0 + 3.0 * cubic * squared
    )
    return (active.astype(bf16), slope.astype(bf16))


def placing_of(targets, slots, dtype=bf16):
    return jnp.where(slots == targets, 1.0, 0.0).astype(dtype)


def front_kernel(experts, cotangent, *refs):
    if cotangent:
        cotangent_ref, refs = refs[0], refs[1:]
    (
        inputs_ref,
        gains_ref,
        weight_ref,
        router_ref,
        diagonals_ref,
        same_ref,
        route_ref,
        target_ref,
        packed_ref,
        projected_ref,
        probs_ref,
        attended_ref,
        middle_ref,
        route_probs_ref,
        gate_ref,
    ) = refs
    inputs = inputs_ref[...]
    normed = (inputs * rms_scale(inputs) * gains_ref[0:1]).astype(bf16)
    projected_ref[...] = dot(normed, weight_ref[:, : 3 * D]).astype(bf16)
    low, first, second = lane_masks()
    width = 2 * HEAD_DIM
    same = same_ref[...]
    same = jnp.concatenate([same, same], axis=0) > 0
    for pair in range(HEADS // 2):
        relative = jnp.concatenate(
            [
                pltpu.roll(
                    jnp.broadcast_to(diagonals_ref[head : head + 1], (SLOT, 2 * SLOT)),
                    SLOT,
                    1,
                    stride=1,
                    stride_axis=0,
                )[:, :SLOT]
                for head in (2 * pair, 2 * pair + 1)
            ],
            axis=0,
        )
        queries, keys, values = [
            projected_ref[:, part * D + pair * width : part * D + (pair + 1) * width]
            for part in range(3)
        ]
        scores = dot_nt(both_heads(queries, first, second), keys) * HEAD_DIM ** (-0.5) + relative
        scores = jnp.where(same, scores, masked_score)
        raised = jnp.exp(scores - jnp.max(scores, axis=-1, keepdims=True))
        probs = raised / jnp.sum(raised, axis=-1, keepdims=True)
        probs_ref[pair] = probs
        attended_ref[:, pair * width : (pair + 1) * width] = own_lanes(
            low, dot(probs.astype(bf16), values)
        ).astype(bf16)
    middle = inputs + dot(attended_ref[...], weight_ref[:, 3 * D :])
    middle_ref[...] = middle
    routed = (middle * rms_scale(middle) * gains_ref[1:2]).astype(bf16)
    logits = dot_nt(routed, router_ref[...])
    names = lax.broadcasted_iota(jnp.int32, (1, logits.shape[1]), 1)
    logits = jnp.where(names < experts, logits, masked_score)
    raised = jnp.exp(logits - jnp.max(logits, axis=-1, keepdims=True))
    route_probs = raised / jnp.sum(raised, axis=-1, keepdims=True)
    route_probs_ref[...] = route_probs
    gate = jnp.sum(jnp.where(names == route_ref[...], route_probs, 0.0), axis=-1, keepdims=True)
    gate_ref[...] = gate
    slots = lax.broadcasted_iota(jnp.int32, (packed_ref.shape[0], 1), 0)
    placing = placing_of(target_ref[...], slots)
    packed_ref[:, :D] = dot(placing, routed).astype(bf16)
    if cotangent:
        grad_result = (gate * cotangent_ref[...]).astype(bf16)
        packed_ref[:, D:] = dot(placing, grad_result).astype(bf16)


def expert_kernel(forward, backward, keep, own_ref, other_ref, *refs):
    if backward and not forward:
        slope_ref, refs = refs[0], refs[1:]
    weight_in_ref, weight_out_ref, own_out_ref, other_out_ref = refs[:4]
    kept_refs = refs[4:]
    grad_at = slice(D, 2 * D) if forward else slice(0, D)
    extent = own_ref.shape[0]
    rows = jnp.concatenate([own_ref[...], other_ref[...]], axis=0)
    hidden_units = weight_in_ref.shape[1]
    step = 512
    reply = jnp.zeros((2 * extent, D), f32)
    grad_reply = jnp.zeros((2 * extent, D), f32)
    for start in range(0, hidden_units, step):
        units = slice(start, start + step)
        if forward:
            active, slope = gelu_parts(dot(rows[:, :D], weight_in_ref[:, units]))
            reply = reply + dot(active, weight_out_ref[units])
            if keep:
                kept_refs[0][:, units] = active
                kept_refs[1][:, units] = slope.astype(bf16)
        else:
            slope = slope_ref[:, units]
        if backward:
            grad_hidden = (
                dot_nt(rows[:, grad_at], weight_out_ref[units]) * slope.astype(f32)
            ).astype(bf16)
            grad_reply = grad_reply + dot_nt(grad_hidden, weight_in_ref[:, units])
            if not forward:
                kept_refs[0][:, units] = grad_hidden
    if forward:
        own_out_ref[:, :D] = reply[:extent].astype(own_out_ref.dtype)
        other_out_ref[:, :D] = reply[extent:].astype(bf16)
    if backward:
        own_out_ref[:, grad_at] = grad_reply[:extent].astype(own_out_ref.dtype)
        other_out_ref[:, grad_at] = grad_reply[extent:].astype(bf16)


def merge_back(
    grad_out, result, grad_sent, middle, gate, route_probs, route, router_ref, gains_ref
):
    grad_gate = jnp.sum(grad_out * result, axis=-1, keepdims=True)
    names = lax.broadcasted_iota(jnp.int32, (1, router_ref.shape[0]), 1)
    choose = jnp.where(names == route, 1.0, 0.0)
    grad_logits = (grad_gate * gate * (choose - route_probs)).astype(bf16)
    grad_routed = grad_sent + dot(grad_logits, router_ref[...])
    grad_middle_norm, grad_gain = norm_backward(grad_routed, middle, gains_ref[1:2])
    return (grad_out + grad_middle_norm, grad_gain, grad_logits)


def attention_back(
    grad_middle, inputs, gains_ref, weight_ref, projected_ref, probs_ref, grads_ref, table_ref
):
    grad_attended = dot_nt(grad_middle.astype(bf16), weight_ref[:, 3 * D :]).astype(bf16)
    low, first, second = lane_masks()
    width = 2 * HEAD_DIM
    scale_qk = HEAD_DIM ** (-0.5)
    places = [lax.broadcasted_iota(jnp.int32, (SLOT, SLOT), axis) for axis in range(2)]
    reverse = jnp.where(places[0] + places[1] == SLOT - 1, 1.0, 0.0).astype(bf16)
    for pair in range(HEADS // 2):
        columns = [
            slice(part * D + pair * width, part * D + (pair + 1) * width) for part in range(3)
        ]
        queries, keys, values = [projected_ref[:, part] for part in columns]
        grads = both_heads(grad_attended[:, pair * width : (pair + 1) * width], first, second)
        probs = probs_ref[pair]
        grad_probs = dot_nt(grads, values)
        grad_scores = (
            probs * (grad_probs - jnp.sum(probs * grad_probs, axis=-1, keepdims=True))
        ).astype(bf16)
        grads_ref[:, columns[0]] = (own_lanes(low, dot(grad_scores, keys)) * scale_qk).astype(bf16)
        grads_ref[:, columns[1]] = (
            dot_tn(grad_scores, both_heads(queries, first, second)) * scale_qk
        ).astype(bf16)
        grads_ref[:, columns[2]] = dot_tn(probs.astype(bf16), grads).astype(bf16)
        if table_ref is not None:
            for own in range(2):
                part = dot(reverse, grad_scores[own * SLOT : (own + 1) * SLOT])
                wide = jnp.concatenate([part, jnp.zeros_like(part)], axis=1)
                moved = pltpu.roll(wide, 1, 1, stride=1, stride_axis=0)
                head = 2 * pair + own
                table_ref[head : head + 1] = jnp.sum(moved, axis=0, keepdims=True)
    grad_normed = dot_nt(grads_ref[...], weight_ref[:, : 3 * D])
    grad_inputs_norm, grad_gain = norm_backward(grad_normed, inputs, gains_ref[0:1])
    return (grad_middle + grad_inputs_norm, grad_gain)


def turn_kernel(
    cotangent_ref,
    returned_ref,
    target_ref,
    route_ref,
    inputs_ref,
    gains_ref,
    weight_ref,
    router_ref,
    projected_ref,
    probs_ref,
    middle_ref,
    route_probs_ref,
    gate_ref,
    outputs_ref,
    result_ref,
    grad_inputs_ref,
    grads_ref,
):
    slots = lax.broadcasted_iota(jnp.int32, (1, returned_ref.shape[0]), 1)
    both = dot(placing_of(target_ref[...], slots), returned_ref[...])
    result = both[:, :D]
    result_ref[...] = result
    middle, gate = middle_ref[...], gate_ref[...]
    outputs_ref[...] = middle + gate * result
    grad_middle, _, _ = merge_back(
        cotangent_ref[...].astype(f32),
        result,
        both[:, D:],
        middle,
        gate,
        route_probs_ref[...],
        route_ref[...],
        router_ref,
        gains_ref,
    )
    grad_inputs_ref[...], _ = attention_back(
        grad_middle,
        inputs_ref[...],
        gains_ref,
        weight_ref,
        projected_ref,
        probs_ref,
        grads_ref,
        None,
    )


def merge_kernel(
    experts,
    grad_out_ref,
    returned_ref,
    target_ref,
    route_ref,
    gains_ref,
    router_ref,
    middle_ref,
    route_probs_ref,
    gate_ref,
    result_ref,
    grad_middle_ref,
    small_ref,
):
    slots = lax.broadcasted_iota(jnp.int32, (1, returned_ref.shape[0]), 1)
    middle = middle_ref[...]
    grad_middle, grad_gain, grad_logits = merge_back(
        grad_out_ref[...],
        result_ref[...],
        dot(placing_of(target_ref[...], slots), returned_ref[...]),
        middle,
        gate_ref[...],
        route_probs_ref[...],
        route_ref[...],
        router_ref,
        gains_ref,
    )
    grad_middle_ref[...] = grad_middle
    routed = (middle * rms_scale(middle) * gains_ref[1:2]).astype(bf16)
    small_ref[0:8] = jnp.broadcast_to(grad_gain[None], (8, D))
    small_ref[8:] = dot_tn(grad_logits, routed)[:experts]


def attention_back_kernel(
    grad_middle_ref,
    inputs_ref,
    gains_ref,
    weight_ref,
    projected_ref,
    probs_ref,
    grad_inputs_ref,
    grads_ref,
    gain_ref,
    table_ref,
):
    grad_inputs_ref[...], grad_gain = attention_back(
        grad_middle_ref[...],
        inputs_ref[...],
        gains_ref,
        weight_ref,
        projected_ref,
        probs_ref,
        grads_ref,
        table_ref,
    )
    gain_ref[...] = grad_gain[None]


def owners_first(order_ref):
    return jnp.where(
        lax.broadcasted_iota(jnp.int32, (D, 1), 0) == order_ref[...], 1.0, 0.0
    ).astype(bf16)


def out_grad_kernel(blocks, order_ref, *refs):
    mine_ref, others_ref = refs[-2:]
    ordering = owners_first(order_ref)
    attended = jnp.concatenate([ref[...] for ref in refs[:blocks]], axis=0)
    grad_branch = jnp.concatenate([ref[...] for ref in refs[blocks : 2 * blocks]], axis=0)
    total = dot_tn(dot(attended, ordering).astype(bf16), grad_branch.astype(bf16)).astype(bf16)
    mine_ref[...] = total[: D // 2]
    others_ref[...] = total[D // 2 :]


def qkv_grad_kernel(blocks, experts, order_ref, gains_ref, spread_ref, owner_ref, *refs):
    mine_ref, others_ref, wide_ref = refs[-3:]
    inputs_refs, grads_refs, gain_refs, table_refs, small_refs = [
        refs[part * blocks : (part + 1) * blocks] for part in range(5)
    ]
    ordering = owners_first(order_ref)
    half = D // 2
    normed = []
    for inputs_ref in inputs_refs:
        inputs = inputs_ref[...]
        own = (inputs * rms_scale(inputs) * gains_ref[0:1]).astype(bf16)
        normed.append(dot(own, ordering).astype(bf16))
    normed = jnp.concatenate(normed, axis=0)
    for part in range(3):
        columns = slice(part * D, (part + 1) * D)
        grads = jnp.concatenate([grads_ref[:, columns] for grads_ref in grads_refs], axis=0)
        total = dot_tn(normed, grads).astype(bf16)
        mine_ref[:, columns] = total[:half]
        others_ref[:, columns] = total[half:]
    diagonals = sum([table_ref[...] for table_ref in table_refs])
    entries = jnp.sum(
        owner_ref[...]
        * jnp.dot(
            diagonals,
            spread_ref[...],
            preferred_element_type=f32,
            precision=lax.Precision.HIGHEST,
        ),
        axis=0,
        keepdims=True,
    )
    small = sum([small_ref[...] for small_ref in small_refs])
    wide_ref[...] = jnp.zeros_like(wide_ref)
    wide_ref[0:1] = sum([gain_ref[...] for gain_ref in gain_refs])
    wide_ref[1:2] = small[0:1]
    wide_ref[2:3] = entries
    wide_ref[8 : 8 + experts] = small[8:]
    columns = dot_tn(ordering, wide_ref[...].T.astype(bf16)).astype(bf16)
    mine_ref[:, 3 * D :] = columns[:half]
    others_ref[:, 3 * D :] = columns[half:]


def kernel_call(kernel, name, out_shape, operands, micros, scratch=()):
    return pl.pallas_call(
        kernel,
        out_shape=tuple(jax.ShapeDtypeStruct(*pair) for pair in out_shape),
        scratch_shapes=list(scratch),
        compiler_params=pltpu.CompilerParams(vmem_limit_bytes=62 * 1024 * 1024),
        cost_estimate=pl.CostEstimate(
            flops=int(micros * 5e8), bytes_accessed=int(micros * 3e6), transcendentals=0
        ),
        name=name,
    )(*operands)


def front_call(inputs, cotangent, dense, place):
    gains, weight, router, diagonals = dense
    same_seq, route_ids, targets, slots = place
    width = D if cotangent is None else 2 * D
    return kernel_call(
        functools.partial(front_kernel, lax.axis_size("dp") // 2, cotangent is not None),
        "attention_front",
        (
            ((slots, width), bf16),
            ((SLOT, 3 * D), bf16),
            ((HEADS // 2, 2 * SLOT, SLOT), f32),
            ((SLOT, D), bf16),
            ((SLOT, D), f32),
            ((SLOT, router.shape[0]), f32),
            ((SLOT, 1), f32),
        ),
        (() if cotangent is None else (cotangent,))
        + (inputs, gains, weight, router, diagonals, same_seq)
        + (route_ids[:, None], targets[None, :]),
        5,
    )


def expert_call(arrived, slope, experts_held, forward, backward, keep):
    own, other = arrived
    extent, units = own.shape[0], experts_held[0].shape[1]
    width = 2 * D if forward and backward else D
    kept = 0 if not keep else 2 if forward else 1
    return kernel_call(
        functools.partial(expert_kernel, forward, backward, keep),
        "experts_" + ("f" if forward else "") + ("b" if backward else ""),
        (((extent, width), f32), ((extent, width), bf16))
        + (((2 * extent, units), bf16),) * kept,
        (own, other) + (() if slope is None else (slope,)) + experts_held,
        6 if width == D else 10,
    )


def turn_call(cotangent, returned, inputs, kept, dense, place):
    gains, weight, router, _ = dense
    _, route_ids, targets, _ = place
    projected, probs, _, middle, route_probs, gate = kept
    rows = ((SLOT, D), f32)
    return kernel_call(
        turn_kernel,
        "turn_back",
        (rows, rows, rows, ((SLOT, 3 * D), bf16)),
        (cotangent, returned, targets[:, None], route_ids[:, None], inputs, gains, weight)
        + (router, projected, probs, middle, route_probs, gate),
        7,
    )


def merge_call(grad_out, returned, result, kept, dense, place):
    gains, weight, router, _ = dense
    _, route_ids, targets, _ = place
    _, _, _, middle, route_probs, gate = kept
    experts = lax.axis_size("dp") // 2
    return kernel_call(
        functools.partial(merge_kernel, experts),
        "merge_back",
        (((SLOT, D), f32), ((8 + experts, D), f32)),
        (grad_out, returned, targets[:, None], route_ids[:, None], gains, router, middle)
        + (route_probs, gate, result),
        2,
    )


def attention_back_call(grad_middle, inputs, kept, dense):
    gains, weight, _, _ = dense
    projected, probs = kept[:2]
    return kernel_call(
        attention_back_kernel,
        "attention_back",
        (
            ((SLOT, D), f32),
            ((SLOT, 3 * D), bf16),
            ((1, D), f32),
            ((HEADS, 2 * SLOT), f32),
        ),
        (grad_middle, inputs, gains, weight, projected, probs),
        7,
    )


def pack_small(gains, router, table):
    rows = 8 + router.shape[1]
    packed = jnp.zeros((rows + -rows % 16, 128), bf16)
    packed = packed.at[0:2, : gains.shape[1]].set(gains)
    packed = packed.at[2, : table.shape[0]].set(table)
    return packed.at[8:rows, : router.shape[0]].set(router.T)


def unpack_small(packed, devices, experts):
    extent = D // devices
    packed = packed.reshape(devices, -1, 128).swapaxes(0, 1)
    gains = packed[0:2, :, :extent].reshape(2, D).astype(f32)
    table = packed[2, :, : BUCKETS * HEADS // devices].reshape(BUCKETS, HEADS).astype(f32)
    router = packed[8 : 8 + experts, :, :extent].reshape(experts, D)
    return (gains, table, jnp.pad(router, ((0, -experts % 128), (0, 0))))


def by_chips(mine, others, devices):
    return join_halves(mine, others).reshape(devices // 2, D // devices, -1)


def total_of(came):
    return jnp.sum(came.astype(f32), axis=0)


def feature_order(devices):
    extent = D // devices
    places = jnp.arange(D, dtype=jnp.int32)
    chip, row = places % (D // 2) // extent, places % extent
    core = (places // (D // 2) + lax.axis_index("dp") % 2) % 2
    return ((2 * chip + core) * extent + row)[None]


def table_places(onehot, devices):
    extent, used = D // devices, BUCKETS * HEADS // devices
    places = np.arange(D)
    held = places % extent < used
    entry = np.where(held, places // extent * used + places % extent, 0)
    spread = onehot[:, entry // HEADS] * held
    owner = entry % HEADS == np.arange(HEADS)[:, None]
    return (spread.astype(np.float32), owner.astype(np.float32))


def shards(
    edge_rows,
    lengths,
    routes,
    norm_gains,
    qkv_weight,
    out_weight,
    router_weight,
    bias_table,
    expert_in,
    expert_out,
):
    devices = lax.axis_size("dp")
    experts = devices // 2
    first_section = lax.axis_index("section") == 0
    onehot = bucket_onehot()
    experts_held = (expert_in[0], expert_out[0])
    weight = lax.all_gather(
        jnp.concatenate([qkv_weight[0], out_weight[0]], axis=1), "dp", axis=0, tiled=True
    )
    small = lax.all_gather(
        pack_small(norm_gains[0], router_weight[0], bias_table[0]), "dp", axis=0, tiled=True
    )
    gains, table, router = unpack_small(small, devices, experts)
    diagonals = jnp.einsum("ib,bh->hi", onehot, table, precision=lax.Precision.HIGHEST)
    dense = (gains, weight, router, diagonals)
    same_seq = same_sequence(lengths)
    capacity = 4 * SLOT // devices
    blocks = range(edge_rows.shape[1] // SLOT)
    local_rows = [edge_rows[0, b * SLOT : (b + 1) * SLOT].astype(f32) for b in blocks]
    routes_of = [routes[0, b * SLOT : (b + 1) * SLOT, 0] for b in blocks]
    places = [
        (same_seq[b], routes_of[b], expert_places(routes_of[b], experts, capacity), experts * capacity)
        for b in blocks
    ]
    slot_ids = jnp.arange(experts * capacity, dtype=jnp.int32)
    placings = [
        (place[2][:, None] == slot_ids[None]).astype(bf16) for place in places
    ]

    def stream(b):
        place, placing, local = places[b], placings[b], local_rows[b]
        packed, _, _, _, middle, _, gate = front_call(local, None, dense, place)
        came = yield packed
        own, other = expert_call(arrive(came), None, experts_held, True, False, False)
        came = yield join_halves(own, other)
        outputs = middle + gate * dot(placing, came)
        carried = section_shift(outputs.astype(bf16), 1).astype(f32)
        inputs = jnp.where(first_section, local, carried)

        packed, *kept = front_call(inputs, local, dense, place)
        came = yield packed
        arrived = arrive(came)
        own, other, active, slope = expert_call(arrived, None, experts_held, True, True, True)
        came = yield join_halves(own, other)
        outputs, result, grad_inputs, _ = turn_call(local, came, inputs, kept, dense, place)
        carried = section_shift(grad_inputs.astype(bf16), -1).astype(f32)
        grad_out = jnp.where(first_section, carried, local)

        grad_result = (kept[5] * grad_out).astype(bf16)
        came = yield jnp.einsum(
            "ts,td->sd", placing, grad_result, preferred_element_type=f32
        ).astype(bf16)
        grad_rows = arrive(came)
        own, other, grad_hidden = expert_call(grad_rows, slope, experts_held, False, True, True)
        came = yield join_halves(own, other)
        grad_middle, small = merge_call(grad_out, came, result, kept, dense, place)
        last = b == len(blocks) - 1
        back = None if last else attention_back_call(grad_middle, inputs, kept, dense)
        return (
            (grad_middle, small, back),
            (inputs, outputs, kept, (arrived, active, grad_rows, grad_hidden)),
        )

    ends = in_turns([stream(b) for b in blocks])
    grad_middles, smalls, backs = [list(part) for part in zip(*[end[0] for end in ends])]
    inputs, outputs, kept, expert_rows = zip(*[end[1] for end in ends])
    order = feature_order(devices)
    mine, others = kernel_call(
        functools.partial(out_grad_kernel, len(blocks)),
        "out_gradient",
        (((D // 2, D), bf16),) * 2,
        (order,) + tuple(kept[b][2] for b in blocks) + tuple(grad_middles),
        2,
    )
    others, grad_middles[-1] = lax.optimization_barrier((others, grad_middles[-1]))
    grad_out_w = chip_all_to_all(by_chips(mine, others, devices))
    backs[-1] = attention_back_call(grad_middles[-1], inputs[-1], kept[-1], dense)
    grad_inputs, grads, gain_ones, tables = zip(*backs)
    mine, others = kernel_call(
        functools.partial(qkv_grad_kernel, len(blocks), experts),
        "qkv_gradient",
        (((D // 2, 3 * D + 128), bf16),) * 2,
        (order, gains, *table_places(onehot, devices))
        + (*inputs, *grads, *gain_ones, *tables, *smalls),
        4,
        (pltpu.VMEM((128, D), f32),),
    )
    grad_out_w, grad_rest = lax.optimization_barrier(
        (grad_out_w, by_chips(mine, others, devices))
    )
    total = total_of(chip_all_to_all(grad_rest))
    grad_out_w = total_of(grad_out_w)
    arrived, active, grad_rows, grad_hidden = zip(*expert_rows)
    arrived = jnp.concatenate([rows[:, :D] for pair in arrived for rows in pair])
    grad_rows = jnp.concatenate([rows for pair in grad_rows for rows in pair])
    grad_expert_out = jnp.einsum(
        "rf,rd->fd", jnp.concatenate(active), grad_rows, preferred_element_type=f32
    )
    grad_expert_in = jnp.einsum(
        "rd,rf->df", arrived, jnp.concatenate(grad_hidden), preferred_element_type=f32
    )
    edge_results = jnp.concatenate(
        [jnp.where(first_section, grad_inputs[b], outputs[b]) for b in blocks]
    )
    extra = total[:, 3 * D :]
    return (
        edge_results[None],
        extra[None, :, 0:2].swapaxes(1, 2),
        total[None, :, : 3 * D],
        grad_out_w[None],
        extra[None, :, 8 : 8 + experts],
        extra[None, : BUCKETS * HEADS // devices, 2],
        grad_expert_in[None],
        grad_expert_out[None],
    )


def solution(mesh):
    return jax.shard_map(
        shards,
        mesh=mesh,
        in_specs=(
            P("section", "dp", None),
            P("dp", None),
            P("section", "dp", None),
            P("section", None, "dp"),
            P("section", "dp", None),
            P("section", "dp", None),
            P("section", "dp", None),
            P("section", "dp"),
            P("section", None, "dp"),
            P("section", "dp", None),
        ),
        out_specs=(
            P("section", "dp", None),
            P("section", None, "dp"),
            P("section", "dp", None),
            P("section", "dp", None),
            P("section", "dp", None),
            P("section", "dp"),
            P("section", None, "dp"),
            P("section", "dp", None),
        ),
        check_vma=False,
    )
```

```python
import functools

import jax
import jax.numpy as jnp
import numpy as np
from jax import lax
from jax.experimental import pallas as pl
from jax.experimental.pallas import tpu as pltpu
from jax.sharding import PartitionSpec as P

D = 768
HEADS = 12
HEAD_DIM = 64
BUCKETS = 32
SLOT = 128


norm_eps = 1e-06
masked_score = -1e30
bucket_edges = (1, 2, 3, 4, 5, 6, 7, 8, 12, 16, 23, 32, 46, 64, 91)
bf16 = jnp.bfloat16
f32 = jnp.float32


def dot(lhs, rhs):
    return jnp.dot(lhs, rhs, preferred_element_type=f32)


def section_shift(block, distance):
    devices = range(lax.axis_size("section"))
    route = [(i - distance, i) for i in devices if i - distance in devices]
    return lax.ppermute(block, "section", route)


def pair_swap(block):
    return lax.ppermute(block, "dp", [(i, i ^ 1) for i in range(lax.axis_size("dp"))])


def chip_all_to_all(block):
    devices = lax.axis_size("dp")
    groups = [list(range(core, devices, 2)) for core in range(2)]
    return lax.all_to_all(
        block, "dp", split_axis=0, concat_axis=0, tiled=True, axis_index_groups=groups
    )


def rms_scale(values):
    return lax.rsqrt(jnp.mean(values * values, axis=-1, keepdims=True) + norm_eps)


def norm_backward(grad_normed, values, gain_row):
    inv_rms = rms_scale(values)
    weighted = grad_normed * gain_row
    grad_gain = jnp.sum(grad_normed * values * inv_rms, axis=0)
    grad_values = inv_rms * weighted - values * inv_rms**3 * jnp.mean(
        weighted * values, axis=-1, keepdims=True
    )
    return (grad_values, grad_gain)


def bucket_onehot():
    offset = np.arange(2 * SLOT) - SLOT
    bucket = np.sum(np.abs(offset)[:, None] >= np.array(bucket_edges), axis=1)
    bucket = bucket + BUCKETS // 2 * (offset > 0)
    return (bucket[:, None] == np.arange(BUCKETS)).astype(np.float32)


def same_sequence(lengths):
    bounds = jnp.cumsum(lengths, axis=-1)
    places = jnp.arange(SLOT, dtype=jnp.int32)
    owners = jnp.sum((places[:, None] >= bounds[:, None, :]).astype(jnp.int32), axis=-1)
    return (owners[:, :, None] == owners[:, None, :]).astype(f32)


def expert_places(route_ids, experts, capacity):
    names = jnp.arange(experts, dtype=jnp.int32)
    choose = (route_ids[:, None] == names).astype(jnp.int32)
    places = jnp.arange(SLOT, dtype=jnp.int32)
    earlier = (places[:, None] > places[None, :]).astype(bf16)
    before = dot(earlier, choose.astype(bf16)).astype(jnp.int32)
    rank_ids = jnp.sum(before * choose, axis=-1)
    return route_ids * capacity + rank_ids


def arrive(block):
    return (block, pair_swap(block))


def join_halves(own, other):
    return (own.astype(f32) + pair_swap(other).astype(f32)).astype(bf16)


def in_turns(streams):
    ends, values = [None] * len(streams), [None] * len(streams)
    travelling = None
    running = list(range(len(streams)))
    while running:
        for turn in list(running):
            try:
                block = streams[turn].send(values[turn])
            except StopIteration as stop:
                ends[turn] = stop.value
                running.remove(turn)
                if travelling is not None and running:
                    last, held = travelling
                    held, first = lax.optimization_barrier((held, ends[turn][0]))
                    ends[turn] = (first,) + ends[turn][1:]
                    values[last], travelling = held, None
                continue
            if travelling is not None:
                last, held = travelling
                held, block = lax.optimization_barrier((held, block))
                values[last] = held
            experts, width = lax.axis_size("dp") // 2, block.shape[-1]
            came = chip_all_to_all(block.reshape(experts, -1, width)).reshape(-1, width)
            values[turn], travelling = came, (turn, came)
    return ends


def dot_nt(lhs, rhs):
    return lax.dot_general(lhs, rhs, (((1,), (1,)), ((), ())), preferred_element_type=f32)


def dot_tn(lhs, rhs):
    return lax.dot_general(lhs, rhs, (((0,), (0,)), ((), ())), preferred_element_type=f32)


def lane_masks():
    low = lax.broadcasted_iota(jnp.int32, (1, 2 * HEAD_DIM), 1) < HEAD_DIM
    first = jnp.where(low, 1.0, 0.0)
    return (low, first.astype(bf16), (1.0 - first).astype(bf16))


def both_heads(slab, first, second):
    return jnp.concatenate([slab * first, slab * second], axis=0)


def own_lanes(low, stacked):
    return jnp.where(low, stacked[:SLOT], stacked[SLOT:])


def gelu_parts(hidden):
    rate, cubic = 0.7978845608028654, 0.044715
    squared = hidden * hidden
    bend = jnp.tanh(rate * hidden * (1.0 + cubic * squared))
    active = 0.5 * hidden * (1.0 + bend)
    slope = 0.5 * (1.0 + bend) + 0.5 * hidden * (1.0 - bend * bend) * rate * (
        1.0 + 3.0 * cubic * squared
    )
    return (active.astype(bf16), slope.astype(bf16))


def placing_of(targets, slots, dtype=bf16):
    return jnp.where(slots == targets, 1.0, 0.0).astype(dtype)


def load_weight(weight_ref, held_ref, sems):
    parts = [slice(0, 3 * D), slice(3 * D, 4 * D)]
    copies = [
        pltpu.make_async_copy(weight_ref.at[:, part], held_ref.at[:, part], sems.at[i])
        for i, part in enumerate(parts)
    ]
    return copies


def place_pieces(offsets_ref, piece_refs, held_ref, sems):
    copies = []
    for i, piece_ref in enumerate(piece_refs):
        rows = piece_ref.shape[0]
        start = pl.multiple_of(offsets_ref[i], 16) if len(piece_refs) > 1 else 0
        copies.append(
            pltpu.make_async_copy(piece_ref, held_ref.at[pl.ds(start, rows)], sems.at[i])
        )
    return copies


def front_kernel(experts, cotangent, pieces, *refs):
    if cotangent:
        cotangent_ref, refs = refs[0], refs[1:]
    inputs_ref, same_ref, route_ref, target_ref = refs[:4]
    refs = refs[4:]
    held_ref, sems = refs[-2:]
    if pieces:
        offsets_ref, spread_ref, owner_ref = refs[:3]
        piece_refs = refs[3 : 3 + pieces]
        refs = refs[3 + pieces :]
        weight_ref, gains_ref, router_ref, diagonals_ref = refs[7:11]
        copies = place_pieces(offsets_ref, piece_refs, held_ref, sems)
        for copy in copies:
            copy.start()
    else:
        weight_ref, gains_ref, router_ref, diagonals_ref = refs[:4]
        refs = refs[4:]
        copies = load_weight(weight_ref, held_ref, sems)
        for copy in copies:
            copy.start()
    (
        packed_ref,
        projected_ref,
        probs_ref,
        attended_ref,
        middle_ref,
        route_probs_ref,
        gate_ref,
    ) = refs[:7]
    inputs = inputs_ref[...]
    inv_rms = rms_scale(inputs)
    if pieces:
        for copy in copies:
            copy.wait()
        keep = pltpu.make_async_copy(held_ref.at[:, : 4 * D], weight_ref, sems.at[0])
        keep.start()
        extra = held_ref[:, 4 * D :].astype(f32).T
        gains_ref[...] = extra[0:8]
        router_ref[0:120] = extra[8:128].astype(bf16)
        router_ref[120:128] = jnp.zeros((8, D), bf16)
        diagonals_ref[...] = lax.dot_general(
            owner_ref[...] * extra[2:3],
            spread_ref[...],
            (((1,), (1,)), ((), ())),
            preferred_element_type=f32,
            precision=lax.Precision.HIGHEST,
        )
    else:
        copies[0].wait()
    normed = (inputs * inv_rms * gains_ref[0:1]).astype(bf16)
    projected_ref[...] = dot(normed, held_ref[:, : 3 * D]).astype(bf16)
    low, first, second = lane_masks()
    width = 2 * HEAD_DIM
    same = same_ref[...]
    same = jnp.concatenate([same, same], axis=0) > 0
    for pair in range(HEADS // 2):
        relative = jnp.concatenate(
            [
                pltpu.roll(
                    jnp.broadcast_to(diagonals_ref[head : head + 1], (SLOT, 2 * SLOT)),
                    SLOT,
                    1,
                    stride=1,
                    stride_axis=0,
                )[:, :SLOT]
                for head in (2 * pair, 2 * pair + 1)
            ],
            axis=0,
        )
        queries, keys, values = [
            projected_ref[:, part * D + pair * width : part * D + (pair + 1) * width]
            for part in range(3)
        ]
        scores = dot_nt(both_heads(queries, first, second), keys) * HEAD_DIM ** (-0.5) + relative
        scores = jnp.where(same, scores, masked_score)
        raised = jnp.exp(scores - jnp.max(scores, axis=-1, keepdims=True))
        probs = raised / jnp.sum(raised, axis=-1, keepdims=True)
        probs_ref[pair] = probs
        attended_ref[:, pair * width : (pair + 1) * width] = own_lanes(
            low, dot(probs.astype(bf16), values)
        ).astype(bf16)
    if not pieces:
        copies[1].wait()
    middle = inputs + dot(attended_ref[...], held_ref[:, 3 * D : 4 * D])
    middle_ref[...] = middle
    routed = (middle * rms_scale(middle) * gains_ref[1:2]).astype(bf16)
    logits = dot_nt(routed, router_ref[...])
    names = lax.broadcasted_iota(jnp.int32, (1, logits.shape[1]), 1)
    logits = jnp.where(names < experts, logits, masked_score)
    raised = jnp.exp(logits - jnp.max(logits, axis=-1, keepdims=True))
    route_probs = raised / jnp.sum(raised, axis=-1, keepdims=True)
    route_probs_ref[...] = route_probs
    gate = jnp.sum(jnp.where(names == route_ref[...], route_probs, 0.0), axis=-1, keepdims=True)
    gate_ref[...] = gate
    slots = lax.broadcasted_iota(jnp.int32, (packed_ref.shape[0], 1), 0)
    placing = placing_of(target_ref[...], slots)
    packed_ref[:, :D] = dot(placing, routed).astype(bf16)
    if cotangent:
        grad_result = (gate * cotangent_ref[...]).astype(bf16)
        packed_ref[:, D:] = dot(placing, grad_result).astype(bf16)
    if pieces:
        keep.wait()


def expert_kernel(forward, backward, keep, own_ref, other_ref, *refs):
    if backward and not forward:
        slope_ref, refs = refs[0], refs[1:]
    weight_in_ref, weight_out_ref, own_out_ref, other_out_ref = refs[:4]
    kept_refs, total_ref = refs[4:-1], refs[-1]
    grad_at = slice(D, 2 * D) if forward else slice(0, D)
    extent = own_ref.shape[0]
    step = pl.program_id(0)

    @pl.when(step == 0)
    def _():
        total_ref[...] = jnp.zeros_like(total_ref)

    rows = jnp.concatenate([own_ref[...], other_ref[...]], axis=0)
    if forward:
        active, slope = gelu_parts(dot(rows[:, :D], weight_in_ref[...]))
        total_ref[:, :D] += dot(active, weight_out_ref[...])
        if keep:
            kept_refs[0][...] = active
            kept_refs[1][...] = slope
    else:
        slope = slope_ref[...]
    if backward:
        grad_hidden = (
            dot_nt(rows[:, grad_at], weight_out_ref[...]) * slope.astype(f32)
        ).astype(bf16)
        total_ref[:, grad_at] += dot_nt(grad_hidden, weight_in_ref[...])
        if not forward:
            kept_refs[0][...] = grad_hidden

    @pl.when(step == pl.num_programs(0) - 1)
    def _():
        own_out_ref[...] = total_ref[:extent].astype(bf16)
        other_out_ref[...] = total_ref[extent:].astype(bf16)


def merge_back(
    grad_out, result, grad_sent, middle, gate, route_probs, route, router_ref, gains_ref
):
    grad_gate = jnp.sum(grad_out * result, axis=-1, keepdims=True)
    names = lax.broadcasted_iota(jnp.int32, (1, router_ref.shape[0]), 1)
    choose = jnp.where(names == route, 1.0, 0.0)
    grad_logits = (grad_gate * gate * (choose - route_probs)).astype(bf16)
    grad_routed = grad_sent + dot(grad_logits, router_ref[...])
    grad_middle_norm, grad_gain = norm_backward(grad_routed, middle, gains_ref[1:2])
    return (grad_out + grad_middle_norm, grad_gain, grad_logits)


def attention_back(
    grad_middle, inputs, gains_ref, held, projected_ref, probs_ref, grads_ref, table_ref
):
    weight_ref, copies = held
    copies[1].wait()
    grad_attended = dot_nt(grad_middle.astype(bf16), weight_ref[:, 3 * D :]).astype(bf16)
    low, first, second = lane_masks()
    width = 2 * HEAD_DIM
    scale_qk = HEAD_DIM ** (-0.5)
    places = [lax.broadcasted_iota(jnp.int32, (SLOT, SLOT), axis) for axis in range(2)]
    reverse = jnp.where(places[0] + places[1] == SLOT - 1, 1.0, 0.0).astype(bf16)
    for pair in range(HEADS // 2):
        columns = [
            slice(part * D + pair * width, part * D + (pair + 1) * width) for part in range(3)
        ]
        queries, keys, values = [projected_ref[:, part] for part in columns]
        grads = both_heads(grad_attended[:, pair * width : (pair + 1) * width], first, second)
        probs = probs_ref[pair]
        grad_probs = dot_nt(grads, values)
        grad_scores = (
            probs * (grad_probs - jnp.sum(probs * grad_probs, axis=-1, keepdims=True))
        ).astype(bf16)
        grads_ref[:, columns[0]] = (own_lanes(low, dot(grad_scores, keys)) * scale_qk).astype(bf16)
        grads_ref[:, columns[1]] = (
            dot_tn(grad_scores, both_heads(queries, first, second)) * scale_qk
        ).astype(bf16)
        grads_ref[:, columns[2]] = dot_tn(probs.astype(bf16), grads).astype(bf16)
        if table_ref is not None:
            for own in range(2):
                part = dot(reverse, grad_scores[own * SLOT : (own + 1) * SLOT])
                wide = jnp.concatenate([part, jnp.zeros_like(part)], axis=1)
                moved = pltpu.roll(wide, 1, 1, stride=1, stride_axis=0)
                head = 2 * pair + own
                table_ref[head : head + 1] = jnp.sum(moved, axis=0, keepdims=True)
    copies[0].wait()
    grad_normed = dot_nt(grads_ref[...], weight_ref[:, : 3 * D])
    grad_inputs_norm, grad_gain = norm_backward(grad_normed, inputs, gains_ref[0:1])
    return (grad_middle + grad_inputs_norm, grad_gain)


def start_weight(weight_ref, held_ref, sems):
    copies = load_weight(weight_ref, held_ref, sems)
    for copy in reversed(copies):
        copy.start()
    return (held_ref, copies)


def turn_kernel(
    cotangent_ref,
    returned_ref,
    target_ref,
    route_ref,
    inputs_ref,
    gains_ref,
    weight_ref,
    router_ref,
    projected_ref,
    probs_ref,
    middle_ref,
    route_probs_ref,
    gate_ref,
    outputs_ref,
    result_ref,
    grad_inputs_ref,
    grads_ref,
    held_ref,
    sems,
):
    held = start_weight(weight_ref, held_ref, sems)
    slots = lax.broadcasted_iota(jnp.int32, (1, returned_ref.shape[0]), 1)
    both = dot(placing_of(target_ref[...], slots), returned_ref[...])
    result = both[:, :D]
    result_ref[...] = result
    middle, gate = middle_ref[...], gate_ref[...]
    outputs_ref[...] = middle + gate * result
    grad_middle, _, _ = merge_back(
        cotangent_ref[...].astype(f32),
        result,
        both[:, D:],
        middle,
        gate,
        route_probs_ref[...],
        route_ref[...],
        router_ref,
        gains_ref,
    )
    grad_inputs, _ = attention_back(
        grad_middle,
        inputs_ref[...],
        gains_ref,
        held,
        projected_ref,
        probs_ref,
        grads_ref,
        None,
    )
    grad_inputs_ref[...] = grad_inputs.astype(bf16)


def merge_kernel(
    experts,
    grad_out_ref,
    returned_ref,
    target_ref,
    route_ref,
    gains_ref,
    router_ref,
    middle_ref,
    route_probs_ref,
    gate_ref,
    result_ref,
    grad_middle_ref,
    small_ref,
):
    slots = lax.broadcasted_iota(jnp.int32, (1, returned_ref.shape[0]), 1)
    middle = middle_ref[...]
    grad_middle, grad_gain, grad_logits = merge_back(
        grad_out_ref[...],
        result_ref[...],
        dot(placing_of(target_ref[...], slots), returned_ref[...]),
        middle,
        gate_ref[...],
        route_probs_ref[...],
        route_ref[...],
        router_ref,
        gains_ref,
    )
    grad_middle_ref[...] = grad_middle
    routed = (middle * rms_scale(middle) * gains_ref[1:2]).astype(bf16)
    small_ref[0:8] = jnp.broadcast_to(grad_gain[None], (8, D))
    small_ref[8:] = dot_tn(grad_logits, routed)[:experts]


def attention_back_kernel(
    grad_middle_ref,
    inputs_ref,
    gains_ref,
    weight_ref,
    projected_ref,
    probs_ref,
    grad_inputs_ref,
    grads_ref,
    gain_ref,
    table_ref,
    held_ref,
    sems,
):
    grad_inputs_ref[...], grad_gain = attention_back(
        grad_middle_ref[...],
        inputs_ref[...],
        gains_ref,
        start_weight(weight_ref, held_ref, sems),
        projected_ref,
        probs_ref,
        grads_ref,
        table_ref,
    )
    gain_ref[...] = grad_gain[None]


def owners_first(order_ref):
    return jnp.where(
        lax.broadcasted_iota(jnp.int32, (D, 1), 0) == order_ref[...], 1.0, 0.0
    ).astype(bf16)


def out_grad_kernel(blocks, order_ref, *refs):
    mine_ref, others_ref = refs[-2:]
    ordering = owners_first(order_ref)
    attended = jnp.concatenate([ref[...] for ref in refs[:blocks]], axis=0)
    grad_branch = jnp.concatenate([ref[...] for ref in refs[blocks : 2 * blocks]], axis=0)
    total = dot_tn(dot(attended, ordering).astype(bf16), grad_branch.astype(bf16)).astype(bf16)
    mine_ref[...] = total[: D // 2]
    others_ref[...] = total[D // 2 :]


def qkv_grad_kernel(blocks, experts, order_ref, gains_ref, spread_ref, owner_ref, *refs):
    mine_ref, others_ref, wide_ref = refs[-3:]
    inputs_refs, grads_refs, gain_refs, table_refs, small_refs = [
        refs[part * blocks : (part + 1) * blocks] for part in range(5)
    ]
    ordering = owners_first(order_ref)
    half = D // 2
    normed = []
    for inputs_ref in inputs_refs:
        inputs = inputs_ref[...]
        own = (inputs * rms_scale(inputs) * gains_ref[0:1]).astype(bf16)
        normed.append(dot(own, ordering).astype(bf16))
    normed = jnp.concatenate(normed, axis=0)
    for part in range(3):
        columns = slice(part * D, (part + 1) * D)
        grads = jnp.concatenate([grads_ref[:, columns] for grads_ref in grads_refs], axis=0)
        total = dot_tn(normed, grads).astype(bf16)
        mine_ref[:, columns] = total[:half]
        others_ref[:, columns] = total[half:]
    diagonals = sum([table_ref[...] for table_ref in table_refs])
    entries = jnp.sum(
        owner_ref[...]
        * jnp.dot(
            diagonals,
            spread_ref[...],
            preferred_element_type=f32,
            precision=lax.Precision.HIGHEST,
        ),
        axis=0,
        keepdims=True,
    )
    small = sum([small_ref[...] for small_ref in small_refs])
    wide_ref[...] = jnp.zeros_like(wide_ref)
    wide_ref[0:1] = sum([gain_ref[...] for gain_ref in gain_refs])
    wide_ref[1:2] = small[0:1]
    wide_ref[2:3] = entries
    wide_ref[8 : 8 + experts] = small[8:]
    columns = dot_tn(ordering, wide_ref[...].T.astype(bf16)).astype(bf16)
    mine_ref[:, 3 * D :] = columns[:half]
    others_ref[:, 3 * D :] = columns[half:]


def kernel_call(kernel, name, out_shape, operands, micros, scratch=(), **blocks):
    return pl.pallas_call(
        kernel,
        out_shape=tuple(jax.ShapeDtypeStruct(*pair) for pair in out_shape),
        scratch_shapes=list(scratch),
        compiler_params=pltpu.CompilerParams(vmem_limit_bytes=62 * 1024 * 1024),
        cost_estimate=pl.CostEstimate(
            flops=int(micros * 5e8), bytes_accessed=int(micros * 3e6), transcendentals=0
        ),
        name=name,
        **blocks,
    )(*operands)


def whole_blocks(operands, apart):
    spaces = {"hbm": pl.ANY, "scalar": pltpu.SMEM, "vmem": pltpu.VMEM}
    return [pl.BlockSpec(memory_space=spaces[apart.get(i, "vmem")]) for i in range(len(operands))]


def front_call(inputs, cotangent, dense, place):
    same_seq, route_ids, targets, slots = place
    operands = () if cotangent is None else (cotangent,)
    operands = operands + (inputs, same_seq, route_ids[:, None], targets[None, :])
    out_shape = (
        ((slots, D if cotangent is None else 2 * D), bf16),
        ((SLOT, 3 * D), bf16),
        ((HEADS // 2, 2 * SLOT, SLOT), f32),
        ((SLOT, D), bf16),
        ((SLOT, D), f32),
        ((SLOT, 128), f32),
        ((SLOT, 1), f32),
    )
    pieces, width, out_apart = 0, 4 * D, {}
    if isinstance(dense, tuple):
        gains, weight, router, diagonals = dense
        apart = {len(operands): "hbm"}
        operands = operands + (weight, gains, router, diagonals)
    else:
        offsets, spread, owner, *held = dense
        pieces, width = len(held), 4 * D + 128
        first = len(operands)
        apart = {first: "scalar", **{first + 3 + i: "hbm" for i in range(pieces)}}
        operands = operands + tuple(dense)
        out_apart = {len(out_shape): "hbm"}
        out_shape = out_shape + (
            ((D, 4 * D), bf16),
            ((8, D), f32),
            ((128, D), bf16),
            ((HEADS, 2 * SLOT), f32),
        )
    return kernel_call(
        functools.partial(
            front_kernel, lax.axis_size("dp") // 2, cotangent is not None, pieces
        ),
        "gathered_front" if pieces else "attention_front",
        out_shape,
        operands,
        5,
        (pltpu.VMEM((D, width), bf16), pltpu.SemaphoreType.DMA((max(2, pieces),))),
        in_specs=whole_blocks(operands, apart),
        out_specs=tuple(whole_blocks(out_shape, out_apart)),
    )


def expert_call(arrived, slope, experts_held, forward, backward, keep):
    own, other = arrived
    extent, units = own.shape[0], experts_held[0].shape[1]
    width = 2 * D if forward and backward else D
    kept = 0 if not keep else 2 if forward else 1
    step = 512
    replies = pl.BlockSpec((extent, width), lambda i: (0, 0))
    hidden = pl.BlockSpec((2 * extent, step), lambda i: (0, i))
    in_specs = [replies, replies] + ([] if slope is None else [hidden])
    in_specs = in_specs + [
        pl.BlockSpec((D, step), lambda i: (0, i)),
        pl.BlockSpec((step, D), lambda i: (i, 0)),
    ]
    return kernel_call(
        functools.partial(expert_kernel, forward, backward, keep),
        "experts_" + ("f" if forward else "") + ("b" if backward else ""),
        (((extent, width), bf16),) * 2 + (((2 * extent, units), bf16),) * kept,
        (own, other) + (() if slope is None else (slope,)) + experts_held,
        6 if width == D else 10,
        (pltpu.VMEM((2 * extent, width), f32),),
        grid=(units // step,),
        in_specs=in_specs,
        out_specs=(replies, replies) + (hidden,) * kept,
    )


def turn_call(cotangent, returned, inputs, kept, dense, place):
    gains, weight, router, _ = dense
    _, route_ids, targets, _ = place
    projected, probs, _, middle, route_probs, gate = kept
    rows = ((SLOT, D), f32)
    operands = (cotangent, returned, targets[:, None], route_ids[:, None], inputs, gains, weight)
    operands = operands + (router, projected, probs, middle, route_probs, gate)
    out_shape = (rows, rows, ((SLOT, D), bf16), ((SLOT, 3 * D), bf16))
    return kernel_call(
        turn_kernel,
        "turn_back",
        out_shape,
        operands,
        7,
        (pltpu.VMEM((D, 4 * D), bf16), pltpu.SemaphoreType.DMA((2,))),
        in_specs=whole_blocks(operands, {6: "hbm"}),
        out_specs=tuple(whole_blocks(out_shape, {})),
    )


def merge_call(grad_out, returned, result, kept, dense, place):
    gains, weight, router, _ = dense
    _, route_ids, targets, _ = place
    _, _, _, middle, route_probs, gate = kept
    experts = lax.axis_size("dp") // 2
    return kernel_call(
        functools.partial(merge_kernel, experts),
        "merge_back",
        (((SLOT, D), f32), ((8 + experts, D), f32)),
        (grad_out, returned, targets[:, None], route_ids[:, None], gains, router, middle)
        + (route_probs, gate, result),
        2,
    )


def attention_back_call(grad_middle, inputs, kept, dense):
    gains, weight, _, _ = dense
    projected, probs = kept[:2]
    operands = (grad_middle, inputs, gains, weight, projected, probs)
    out_shape = (
        ((SLOT, D), f32),
        ((SLOT, 3 * D), bf16),
        ((1, D), f32),
        ((HEADS, 2 * SLOT), f32),
    )
    return kernel_call(
        attention_back_kernel,
        "attention_back",
        out_shape,
        operands,
        7,
        (pltpu.VMEM((D, 4 * D), bf16), pltpu.SemaphoreType.DMA((2,))),
        in_specs=whole_blocks(operands, {3: "hbm"}),
        out_specs=tuple(whole_blocks(out_shape, {})),
    )


def pack_dense(gains, qkv, out, router, table):
    rows, kind = qkv.shape[0], qkv.dtype
    blank = jnp.zeros((rows, 128 - 8 - router.shape[1]), kind)
    entries = jnp.pad(table, (0, rows - table.shape[0]))[:, None]
    return jnp.concatenate(
        [qkv, out, gains.T, entries, jnp.zeros((rows, 5), kind), router, blank], axis=1
    )


def gather_pieces(piece):
    devices, extent = lax.axis_size("dp"), piece.shape[0]
    if devices != 16:
        gathered = lax.all_gather(piece, "dp", axis=0, tiled=True)
        return (jnp.zeros((1,), jnp.int32), [gathered])
    me = lax.axis_index("dp")
    z, y, core = me // 4, me // 2 % 2, me % 2

    def send(block, route):
        return lax.ppermute(block, "dp", route)

    upward = [(i, i + 4) for i in range(12)]
    downward = [(i + 4, i) for i in range(12)]
    rising, falling = [piece], [piece]
    for _ in range(3):
        rising.append(send(rising[-1], upward))
        falling.append(send(falling[-1], downward))
    line = [
        piece,
        jnp.where(z == 0, falling[1], rising[1]),
        jnp.where(z == 0, falling[2], jnp.where(z == 3, rising[2], falling[1])),
        jnp.where(
            z == 0,
            falling[3],
            jnp.where(z == 1, falling[2], jnp.where(z == 2, rising[2], rising[3])),
        ),
    ]
    from_z = [
        z,
        jnp.where(z == 0, 1, z - 1),
        jnp.where(z == 2, 3, jnp.where(z == 3, 1, 2)),
        jnp.where(z < 2, 3, 0),
    ]
    pieces, owners = [], []
    for block, z_of in zip(line, from_z):
        for other_y, column in enumerate((block, send(block, [(i, i ^ 2) for i in range(16)]))):
            for other_core, held in enumerate((column, pair_swap(column))):
                pieces.append(held)
                owners.append(4 * z_of + 2 * (y ^ other_y) + (core ^ other_core))
    return (jnp.stack(owners).astype(jnp.int32) * extent, pieces)


def by_chips(mine, others, devices):
    return join_halves(mine, others).reshape(devices // 2, D // devices, -1)


def total_of(came):
    return jnp.sum(came.astype(f32), axis=0)


def feature_order(devices):
    extent = D // devices
    places = jnp.arange(D, dtype=jnp.int32)
    chip, row = places % (D // 2) // extent, places % extent
    core = (places // (D // 2) + lax.axis_index("dp") % 2) % 2
    return ((2 * chip + core) * extent + row)[None]


def table_places(onehot, devices):
    extent, used = D // devices, BUCKETS * HEADS // devices
    places = np.arange(D)
    held = places % extent < used
    entry = np.where(held, places // extent * used + places % extent, 0)
    spread = onehot[:, entry // HEADS] * held
    owner = entry % HEADS == np.arange(HEADS)[:, None]
    return (spread.astype(np.float32), owner.astype(np.float32))


def shards(
    edge_rows,
    lengths,
    routes,
    norm_gains,
    qkv_weight,
    out_weight,
    router_weight,
    bias_table,
    expert_in,
    expert_out,
):
    devices = lax.axis_size("dp")
    experts = devices // 2
    first_section = lax.axis_index("section") == 0
    onehot = bucket_onehot()
    experts_held = (expert_in[0], expert_out[0])
    spread, owner = table_places(onehot, devices)
    offsets, pieces = gather_pieces(
        pack_dense(norm_gains[0], qkv_weight[0], out_weight[0], router_weight[0], bias_table[0])
    )
    gathering = [offsets, jnp.asarray(spread), jnp.asarray(owner), *pieces]
    dense = None
    same_seq = same_sequence(lengths)
    capacity = 4 * SLOT // devices
    blocks = range(edge_rows.shape[1] // SLOT)
    local_rows = [edge_rows[0, b * SLOT : (b + 1) * SLOT].astype(f32) for b in blocks]
    routes_of = [routes[0, b * SLOT : (b + 1) * SLOT, 0] for b in blocks]
    places = [
        (same_seq[b], routes_of[b], expert_places(routes_of[b], experts, capacity), experts * capacity)
        for b in blocks
    ]
    slot_ids = jnp.arange(experts * capacity, dtype=jnp.int32)
    placings = [
        (place[2][:, None] == slot_ids[None]).astype(bf16) for place in places
    ]

    def stream(b):
        nonlocal dense
        place, placing, local = places[b], placings[b], local_rows[b]
        packed, _, _, _, middle, _, gate, *made = front_call(
            local, None, dense or gathering, place
        )
        if dense is None:
            weight, *small = made
            dense = (small[0], weight, small[1], small[2])
        came = yield packed
        own, other = expert_call(arrive(came), None, experts_held, True, False, False)
        came = yield join_halves(own, other)
        outputs = middle + gate * dot(placing, came)
        carried = section_shift(outputs.astype(bf16), 1).astype(f32)
        inputs = jnp.where(first_section, local, carried)

        packed, *kept = front_call(inputs, local, dense, place)
        came = yield packed
        arrived = arrive(came)
        own, other, active, slope = expert_call(arrived, None, experts_held, True, True, True)
        came = yield join_halves(own, other)
        outputs, result, grad_inputs, _ = turn_call(local, came, inputs, kept, dense, place)
        carried = section_shift(grad_inputs.astype(bf16), -1).astype(f32)
        grad_out = jnp.where(first_section, carried, local)

        grad_result = (kept[5] * grad_out).astype(bf16)
        came = yield jnp.einsum(
            "ts,td->sd", placing, grad_result, preferred_element_type=f32
        ).astype(bf16)
        grad_rows = arrive(came)
        own, other, grad_hidden = expert_call(grad_rows, slope, experts_held, False, True, True)
        came = yield join_halves(own, other)
        grad_middle, small = merge_call(grad_out, came, result, kept, dense, place)
        last = b == len(blocks) - 1
        back = None if last else attention_back_call(grad_middle, inputs, kept, dense)
        return (
            (grad_middle, small, back),
            (inputs, outputs, kept, (arrived, active, grad_rows, grad_hidden)),
        )

    ends = in_turns([stream(b) for b in blocks])
    grad_middles, smalls, backs = [list(part) for part in zip(*[end[0] for end in ends])]
    inputs, outputs, kept, expert_rows = zip(*[end[1] for end in ends])
    order = feature_order(devices)
    mine, others = kernel_call(
        functools.partial(out_grad_kernel, len(blocks)),
        "out_gradient",
        (((D // 2, D), bf16),) * 2,
        (order,) + tuple(kept[b][2] for b in blocks) + tuple(grad_middles),
        2,
    )
    grad_first, grad_middles[-1] = lax.optimization_barrier(
        (by_chips(mine, others, devices), grad_middles[-1])
    )
    grad_out_w = chip_all_to_all(grad_first)
    backs[-1] = attention_back_call(grad_middles[-1], inputs[-1], kept[-1], dense)
    grad_inputs, grads, gain_ones, tables = zip(*backs)
    mine, others = kernel_call(
        functools.partial(qkv_grad_kernel, len(blocks), experts),
        "qkv_gradient",
        (((D // 2, 3 * D + 128), bf16),) * 2,
        (order, dense[0], spread, owner)
        + (*inputs, *grads, *gain_ones, *tables, *smalls),
        4,
        (pltpu.VMEM((128, D), f32),),
    )
    grad_out_w, grad_rest = lax.optimization_barrier(
        (grad_out_w, by_chips(mine, others, devices))
    )
    total = total_of(chip_all_to_all(grad_rest))
    grad_out_w = total_of(grad_out_w)
    arrived, active, grad_rows, grad_hidden = zip(*expert_rows)
    arrived = jnp.concatenate([rows[:, :D] for pair in arrived for rows in pair])
    grad_rows = jnp.concatenate([rows for pair in grad_rows for rows in pair])
    grad_expert_out = jnp.einsum(
        "rf,rd->fd", jnp.concatenate(active), grad_rows, preferred_element_type=f32
    )
    grad_expert_in = jnp.einsum(
        "rd,rf->df", arrived, jnp.concatenate(grad_hidden), preferred_element_type=f32
    )
    edge_results = jnp.concatenate(
        [jnp.where(first_section, grad_inputs[b], outputs[b]) for b in blocks]
    )
    extra = total[:, 3 * D :]
    return (
        edge_results[None],
        extra[None, :, 0:2].swapaxes(1, 2),
        total[None, :, : 3 * D],
        grad_out_w[None],
        extra[None, :, 8 : 8 + experts],
        extra[None, : BUCKETS * HEADS // devices, 2],
        grad_expert_in[None],
        grad_expert_out[None],
    )


def solution(mesh):
    return jax.shard_map(
        shards,
        mesh=mesh,
        in_specs=(
            P("section", "dp", None),
            P("dp", None),
            P("section", "dp", None),
            P("section", None, "dp"),
            P("section", "dp", None),
            P("section", "dp", None),
            P("section", "dp", None),
            P("section", "dp"),
            P("section", None, "dp"),
            P("section", "dp", None),
        ),
        out_specs=(
            P("section", "dp", None),
            P("section", None, "dp"),
            P("section", "dp", None),
            P("section", "dp", None),
            P("section", "dp", None),
            P("section", "dp"),
            P("section", None, "dp"),
            P("section", "dp", None),
        ),
        check_vma=False,
    )
```

```python
import functools

import jax
import jax.numpy as jnp
import numpy as np
from jax import lax
from jax.experimental import pallas as pl
from jax.experimental.pallas import tpu as pltpu
from jax.sharding import PartitionSpec as P

D = 768
HEADS = 12
HEAD_DIM = 64
BUCKETS = 32
SLOT = 128


norm_eps = 1e-06
masked_score = -1e30
bucket_edges = (1, 2, 3, 4, 5, 6, 7, 8, 12, 16, 23, 32, 46, 64, 91)
bf16 = jnp.bfloat16
f32 = jnp.float32


def dot(lhs, rhs):
    return jnp.dot(lhs, rhs, preferred_element_type=f32)


def section_shift(block, distance):
    devices = range(lax.axis_size("section"))
    route = [(i - distance, i) for i in devices if i - distance in devices]
    return lax.ppermute(block, "section", route)


def pair_swap(block):
    return lax.ppermute(block, "dp", [(i, i ^ 1) for i in range(lax.axis_size("dp"))])


def chip_all_to_all(block):
    devices = lax.axis_size("dp")
    groups = [list(range(core, devices, 2)) for core in range(2)]
    return lax.all_to_all(
        block, "dp", split_axis=0, concat_axis=0, tiled=True, axis_index_groups=groups
    )


def rms_scale(values):
    return lax.rsqrt(jnp.mean(values * values, axis=-1, keepdims=True) + norm_eps)


def norm_backward(grad_normed, values, gain_row):
    inv_rms = rms_scale(values)
    weighted = grad_normed * gain_row
    grad_gain = jnp.sum(grad_normed * values * inv_rms, axis=0)
    grad_values = inv_rms * weighted - values * inv_rms**3 * jnp.mean(
        weighted * values, axis=-1, keepdims=True
    )
    return (grad_values, grad_gain)


def bucket_onehot():
    offset = np.arange(2 * SLOT) - SLOT
    bucket = np.sum(np.abs(offset)[:, None] >= np.array(bucket_edges), axis=1)
    bucket = bucket + BUCKETS // 2 * (offset > 0)
    return (bucket[:, None] == np.arange(BUCKETS)).astype(np.float32)


def same_sequence(lengths):
    bounds = jnp.cumsum(lengths, axis=-1)
    places = jnp.arange(SLOT, dtype=jnp.int32)
    owners = jnp.sum((places[:, None] >= bounds[:, None, :]).astype(jnp.int32), axis=-1)
    return (owners[:, :, None] == owners[:, None, :]).astype(f32)


def expert_places(route_ids, experts, capacity):
    names = jnp.arange(experts, dtype=jnp.int32)
    choose = (route_ids[:, None] == names).astype(jnp.int32)
    places = jnp.arange(SLOT, dtype=jnp.int32)
    earlier = (places[:, None] > places[None, :]).astype(bf16)
    before = dot(earlier, choose.astype(bf16)).astype(jnp.int32)
    rank_ids = jnp.sum(before * choose, axis=-1)
    return route_ids * capacity + rank_ids


def arrive(block):
    return (block, pair_swap(block))


def join_halves(own, other):
    return (own.astype(f32) + pair_swap(other).astype(f32)).astype(bf16)


def in_turns(streams):
    ends, values = [None] * len(streams), [None] * len(streams)
    travelling = None
    running = list(range(len(streams)))
    while running:
        for turn in list(running):
            try:
                block = streams[turn].send(values[turn])
            except StopIteration as stop:
                ends[turn] = stop.value
                running.remove(turn)
                if travelling is not None and running:
                    last, held = travelling
                    held, first = lax.optimization_barrier((held, ends[turn][0]))
                    ends[turn] = (first,) + ends[turn][1:]
                    values[last], travelling = held, None
                continue
            if travelling is not None:
                last, held = travelling
                held, block = lax.optimization_barrier((held, block))
                values[last] = held
            experts, width = lax.axis_size("dp") // 2, block.shape[-1]
            came = chip_all_to_all(block.reshape(experts, -1, width)).reshape(-1, width)
            values[turn], travelling = came, (turn, came)
    return ends


def dot_nt(lhs, rhs):
    return lax.dot_general(lhs, rhs, (((1,), (1,)), ((), ())), preferred_element_type=f32)


def dot_tn(lhs, rhs):
    return lax.dot_general(lhs, rhs, (((0,), (0,)), ((), ())), preferred_element_type=f32)


def lane_masks():
    low = lax.broadcasted_iota(jnp.int32, (1, 2 * HEAD_DIM), 1) < HEAD_DIM
    first = jnp.where(low, 1.0, 0.0)
    return (low, first.astype(bf16), (1.0 - first).astype(bf16))


def both_heads(slab, first, second):
    return jnp.concatenate([slab * first, slab * second], axis=0)


def own_lanes(low, stacked):
    return jnp.where(low, stacked[:SLOT], stacked[SLOT:])


def gelu_parts(hidden):
    rate, cubic = 0.7978845608028654, 0.044715
    squared = hidden * hidden
    bend = jnp.tanh(rate * hidden * (1.0 + cubic * squared))
    active = 0.5 * hidden * (1.0 + bend)
    slope = 0.5 * (1.0 + bend) + 0.5 * hidden * (1.0 - bend * bend) * rate * (
        1.0 + 3.0 * cubic * squared
    )
    return (active.astype(bf16), slope.astype(bf16))


def placing_of(targets, slots, dtype=bf16):
    return jnp.where(slots == targets, 1.0, 0.0).astype(dtype)


def load_weight(weight_ref, held_ref, sems):
    parts = [slice(0, 3 * D), slice(3 * D, 4 * D)]
    copies = [
        pltpu.make_async_copy(weight_ref.at[:, part], held_ref.at[:, part], sems.at[i])
        for i, part in enumerate(parts)
    ]
    return copies


def place_pieces(offsets_ref, piece_refs, held_ref, sems):
    copies = []
    for i, piece_ref in enumerate(piece_refs):
        rows = piece_ref.shape[0]
        start = pl.multiple_of(offsets_ref[i], 16) if len(piece_refs) > 1 else 0
        copies.append(
            pltpu.make_async_copy(piece_ref, held_ref.at[pl.ds(start, rows)], sems.at[i])
        )
    return copies


def front_kernel(experts, cotangent, pieces, *refs):
    if cotangent:
        cotangent_ref, refs = refs[0], refs[1:]
    inputs_ref, same_ref, route_ref, target_ref = refs[:4]
    refs = refs[4:]
    held_ref, sems = refs[-2:]
    if pieces:
        offsets_ref, spread_ref, owner_ref = refs[:3]
        piece_refs = refs[3 : 3 + pieces]
        refs = refs[3 + pieces :]
        weight_ref, gains_ref, router_ref, diagonals_ref = refs[7:11]
        copies = place_pieces(offsets_ref, piece_refs, held_ref, sems)
        for copy in copies:
            copy.start()
    else:
        weight_ref, gains_ref, router_ref, diagonals_ref = refs[:4]
        refs = refs[4:]
        copies = load_weight(weight_ref, held_ref, sems)
        for copy in copies:
            copy.start()
    (
        packed_ref,
        projected_ref,
        probs_ref,
        attended_ref,
        middle_ref,
        route_probs_ref,
        gate_ref,
    ) = refs[:7]
    inputs = inputs_ref[...].astype(f32)
    inv_rms = rms_scale(inputs)
    if pieces:
        for copy in copies:
            copy.wait()
        keep = pltpu.make_async_copy(held_ref.at[:, : 4 * D], weight_ref, sems.at[0])
        keep.start()
        extra = held_ref[:, 4 * D :].astype(f32).T
        gains_ref[...] = extra[0:8]
        router_ref[0:120] = extra[8:128].astype(bf16)
        router_ref[120:128] = jnp.zeros((8, D), bf16)
        diagonals_ref[...] = lax.dot_general(
            owner_ref[...] * extra[2:3],
            spread_ref[...],
            (((1,), (1,)), ((), ())),
            preferred_element_type=f32,
            precision=lax.Precision.HIGHEST,
        )
    else:
        copies[0].wait()
    normed = (inputs * inv_rms * gains_ref[0:1]).astype(bf16)
    projected_ref[...] = dot(normed, held_ref[:, : 3 * D]).astype(bf16)
    low, first, second = lane_masks()
    width = 2 * HEAD_DIM
    same = same_ref[...]
    same = jnp.concatenate([same, same], axis=0) > 0
    for pair in range(HEADS // 2):
        relative = jnp.concatenate(
            [
                pltpu.roll(
                    jnp.broadcast_to(diagonals_ref[head : head + 1], (SLOT, 2 * SLOT)),
                    SLOT,
                    1,
                    stride=1,
                    stride_axis=0,
                )[:, :SLOT]
                for head in (2 * pair, 2 * pair + 1)
            ],
            axis=0,
        )
        queries, keys, values = [
            projected_ref[:, part * D + pair * width : part * D + (pair + 1) * width]
            for part in range(3)
        ]
        scores = dot_nt(both_heads(queries, first, second), keys) * HEAD_DIM ** (-0.5) + relative
        scores = jnp.where(same, scores, masked_score)
        raised = jnp.exp(scores - jnp.max(scores, axis=-1, keepdims=True))
        probs = raised / jnp.sum(raised, axis=-1, keepdims=True)
        probs_ref[pair] = probs
        attended_ref[:, pair * width : (pair + 1) * width] = own_lanes(
            low, dot(probs.astype(bf16), values)
        ).astype(bf16)
    if not pieces:
        copies[1].wait()
    middle = inputs + dot(attended_ref[...], held_ref[:, 3 * D : 4 * D])
    middle_ref[...] = middle
    routed = (middle * rms_scale(middle) * gains_ref[1:2]).astype(bf16)
    logits = dot_nt(routed, router_ref[...])
    names = lax.broadcasted_iota(jnp.int32, (1, logits.shape[1]), 1)
    logits = jnp.where(names < experts, logits, masked_score)
    raised = jnp.exp(logits - jnp.max(logits, axis=-1, keepdims=True))
    route_probs = raised / jnp.sum(raised, axis=-1, keepdims=True)
    route_probs_ref[...] = route_probs
    gate = jnp.sum(jnp.where(names == route_ref[...], route_probs, 0.0), axis=-1, keepdims=True)
    gate_ref[...] = gate
    slots = lax.broadcasted_iota(jnp.int32, (packed_ref.shape[0], 1), 0)
    placing = placing_of(target_ref[...], slots)
    packed_ref[:, :D] = dot(placing, routed).astype(bf16)
    if cotangent:
        grad_result = (gate * cotangent_ref[...].astype(f32)).astype(bf16)
        packed_ref[:, D:] = dot(placing, grad_result).astype(bf16)
    if pieces:
        keep.wait()


def expert_kernel(forward, backward, keep, own_ref, other_ref, *refs):
    if backward and not forward:
        slope_ref, refs = refs[0], refs[1:]
    weight_in_ref, weight_out_ref, own_out_ref, other_out_ref = refs[:4]
    kept_refs, total_ref = refs[4:-1], refs[-1]
    grad_at = slice(D, 2 * D) if forward else slice(0, D)
    extent = own_ref.shape[0]
    step = pl.program_id(0)

    @pl.when(step == 0)
    def _():
        total_ref[...] = jnp.zeros_like(total_ref)

    rows = jnp.concatenate([own_ref[...], other_ref[...]], axis=0)
    if forward:
        active, slope = gelu_parts(dot(rows[:, :D], weight_in_ref[...]))
        total_ref[:, :D] += dot(active, weight_out_ref[...])
        if keep:
            kept_refs[0][...] = active
            kept_refs[1][...] = slope
    else:
        slope = slope_ref[...]
    if backward:
        grad_hidden = (
            dot_nt(rows[:, grad_at], weight_out_ref[...]) * slope.astype(f32)
        ).astype(bf16)
        total_ref[:, grad_at] += dot_nt(grad_hidden, weight_in_ref[...])
        if not forward:
            kept_refs[0][...] = grad_hidden

    @pl.when(step == pl.num_programs(0) - 1)
    def _():
        own_out_ref[...] = total_ref[:extent].astype(bf16)
        other_out_ref[...] = total_ref[extent:].astype(bf16)


def merge_back(
    grad_out, result, grad_sent, middle, gate, route_probs, route, router_ref, gains_ref
):
    grad_gate = jnp.sum(grad_out * result, axis=-1, keepdims=True)
    names = lax.broadcasted_iota(jnp.int32, (1, router_ref.shape[0]), 1)
    choose = jnp.where(names == route, 1.0, 0.0)
    grad_logits = (grad_gate * gate * (choose - route_probs)).astype(bf16)
    grad_routed = grad_sent + dot(grad_logits, router_ref[...])
    grad_middle_norm, grad_gain = norm_backward(grad_routed, middle, gains_ref[1:2])
    return (grad_out + grad_middle_norm, grad_gain, grad_logits)


def attention_back(
    grad_middle, inputs, gains_ref, held, projected_ref, probs_ref, grads_ref, table_ref
):
    weight_ref, copies = held
    copies[1].wait()
    grad_attended = dot_nt(grad_middle.astype(bf16), weight_ref[:, 3 * D :]).astype(bf16)
    low, first, second = lane_masks()
    width = 2 * HEAD_DIM
    scale_qk = HEAD_DIM ** (-0.5)
    places = [lax.broadcasted_iota(jnp.int32, (SLOT, SLOT), axis) for axis in range(2)]
    reverse = jnp.where(places[0] + places[1] == SLOT - 1, 1.0, 0.0).astype(bf16)
    for pair in range(HEADS // 2):
        columns = [
            slice(part * D + pair * width, part * D + (pair + 1) * width) for part in range(3)
        ]
        queries, keys, values = [projected_ref[:, part] for part in columns]
        grads = both_heads(grad_attended[:, pair * width : (pair + 1) * width], first, second)
        probs = probs_ref[pair]
        grad_probs = dot_nt(grads, values)
        grad_scores = (
            probs * (grad_probs - jnp.sum(probs * grad_probs, axis=-1, keepdims=True))
        ).astype(bf16)
        grads_ref[:, columns[0]] = (own_lanes(low, dot(grad_scores, keys)) * scale_qk).astype(bf16)
        grads_ref[:, columns[1]] = (
            dot_tn(grad_scores, both_heads(queries, first, second)) * scale_qk
        ).astype(bf16)
        grads_ref[:, columns[2]] = dot_tn(probs.astype(bf16), grads).astype(bf16)
        if table_ref is not None:
            for own in range(2):
                part = dot(reverse, grad_scores[own * SLOT : (own + 1) * SLOT])
                wide = jnp.concatenate([part, jnp.zeros_like(part)], axis=1)
                moved = pltpu.roll(wide, 1, 1, stride=1, stride_axis=0)
                head = 2 * pair + own
                table_ref[head : head + 1] = jnp.sum(moved, axis=0, keepdims=True)
    copies[0].wait()
    grad_normed = dot_nt(grads_ref[...], weight_ref[:, : 3 * D])
    grad_inputs_norm, grad_gain = norm_backward(grad_normed, inputs, gains_ref[0:1])
    return (grad_middle + grad_inputs_norm, grad_gain)


def start_weight(weight_ref, held_ref, sems):
    copies = load_weight(weight_ref, held_ref, sems)
    for copy in reversed(copies):
        copy.start()
    return (held_ref, copies)


def turn_kernel(
    cotangent_ref,
    returned_ref,
    target_ref,
    route_ref,
    inputs_ref,
    gains_ref,
    weight_ref,
    router_ref,
    projected_ref,
    probs_ref,
    middle_ref,
    route_probs_ref,
    gate_ref,
    outputs_ref,
    result_ref,
    grad_inputs_ref,
    grads_ref,
    held_ref,
    sems,
):
    held = start_weight(weight_ref, held_ref, sems)
    slots = lax.broadcasted_iota(jnp.int32, (1, returned_ref.shape[0]), 1)
    both = dot(placing_of(target_ref[...], slots), returned_ref[...])
    result = both[:, :D]
    result_ref[...] = result
    middle, gate = middle_ref[...], gate_ref[...]
    outputs_ref[...] = middle + gate * result
    grad_middle, _, _ = merge_back(
        cotangent_ref[...].astype(f32),
        result,
        both[:, D:],
        middle,
        gate,
        route_probs_ref[...],
        route_ref[...],
        router_ref,
        gains_ref,
    )
    grad_inputs, _ = attention_back(
        grad_middle,
        inputs_ref[...].astype(f32),
        gains_ref,
        held,
        projected_ref,
        probs_ref,
        grads_ref,
        None,
    )
    grad_inputs_ref[...] = grad_inputs.astype(bf16)


def merge_kernel(
    experts,
    grad_out_ref,
    returned_ref,
    target_ref,
    route_ref,
    gains_ref,
    router_ref,
    middle_ref,
    route_probs_ref,
    gate_ref,
    result_ref,
    grad_middle_ref,
    small_ref,
):
    slots = lax.broadcasted_iota(jnp.int32, (1, returned_ref.shape[0]), 1)
    middle = middle_ref[...]
    grad_middle, grad_gain, grad_logits = merge_back(
        grad_out_ref[...].astype(f32),
        result_ref[...],
        dot(placing_of(target_ref[...], slots), returned_ref[...]),
        middle,
        gate_ref[...],
        route_probs_ref[...],
        route_ref[...],
        router_ref,
        gains_ref,
    )
    grad_middle_ref[...] = grad_middle
    routed = (middle * rms_scale(middle) * gains_ref[1:2]).astype(bf16)
    small_ref[0:8] = jnp.broadcast_to(grad_gain[None], (8, D))
    small_ref[8:] = dot_tn(grad_logits, routed)[:experts]


def attention_back_kernel(
    grad_middle_ref,
    inputs_ref,
    gains_ref,
    weight_ref,
    projected_ref,
    probs_ref,
    grad_inputs_ref,
    grads_ref,
    gain_ref,
    table_ref,
    held_ref,
    sems,
):
    grad_inputs_ref[...], grad_gain = attention_back(
        grad_middle_ref[...],
        inputs_ref[...].astype(f32),
        gains_ref,
        start_weight(weight_ref, held_ref, sems),
        projected_ref,
        probs_ref,
        grads_ref,
        table_ref,
    )
    gain_ref[...] = grad_gain[None]


def owners_first(order_ref):
    return jnp.where(
        lax.broadcasted_iota(jnp.int32, (D, 1), 0) == order_ref[...], 1.0, 0.0
    ).astype(bf16)


def out_grad_kernel(blocks, order_ref, *refs):
    mine_ref, others_ref = refs[-2:]
    ordering = owners_first(order_ref)
    attended = jnp.concatenate([ref[...] for ref in refs[:blocks]], axis=0)
    grad_branch = jnp.concatenate([ref[...] for ref in refs[blocks : 2 * blocks]], axis=0)
    total = dot_tn(dot(attended, ordering).astype(bf16), grad_branch.astype(bf16)).astype(bf16)
    mine_ref[...] = total[: D // 2]
    others_ref[...] = total[D // 2 :]


def qkv_grad_kernel(blocks, experts, order_ref, gains_ref, spread_ref, owner_ref, *refs):
    mine_ref, others_ref, wide_ref = refs[-3:]
    inputs_refs, grads_refs, gain_refs, table_refs, small_refs = [
        refs[part * blocks : (part + 1) * blocks] for part in range(5)
    ]
    ordering = owners_first(order_ref)
    half = D // 2
    normed = []
    for inputs_ref in inputs_refs:
        inputs = inputs_ref[...].astype(f32)
        own = (inputs * rms_scale(inputs) * gains_ref[0:1]).astype(bf16)
        normed.append(dot(own, ordering).astype(bf16))
    normed = jnp.concatenate(normed, axis=0)
    for part in range(3):
        columns = slice(part * D, (part + 1) * D)
        grads = jnp.concatenate([grads_ref[:, columns] for grads_ref in grads_refs], axis=0)
        total = dot_tn(normed, grads).astype(bf16)
        mine_ref[:, columns] = total[:half]
        others_ref[:, columns] = total[half:]
    diagonals = sum([table_ref[...] for table_ref in table_refs])
    entries = jnp.sum(
        owner_ref[...]
        * jnp.dot(
            diagonals,
            spread_ref[...],
            preferred_element_type=f32,
            precision=lax.Precision.HIGHEST,
        ),
        axis=0,
        keepdims=True,
    )
    small = sum([small_ref[...] for small_ref in small_refs])
    wide_ref[...] = jnp.zeros_like(wide_ref)
    wide_ref[0:1] = sum([gain_ref[...] for gain_ref in gain_refs])
    wide_ref[1:2] = small[0:1]
    wide_ref[2:3] = entries
    wide_ref[8 : 8 + experts] = small[8:]
    columns = dot_tn(ordering, wide_ref[...].T.astype(bf16)).astype(bf16)
    mine_ref[:, 3 * D :] = columns[:half]
    others_ref[:, 3 * D :] = columns[half:]


def kernel_call(kernel, name, out_shape, operands, micros, scratch=(), **blocks):
    return pl.pallas_call(
        kernel,
        out_shape=tuple(jax.ShapeDtypeStruct(*pair) for pair in out_shape),
        scratch_shapes=list(scratch),
        compiler_params=pltpu.CompilerParams(vmem_limit_bytes=62 * 1024 * 1024),
        cost_estimate=pl.CostEstimate(
            flops=int(micros * 5e8), bytes_accessed=int(micros * 3e6), transcendentals=0
        ),
        name=name,
        **blocks,
    )(*operands)


def whole_blocks(operands, apart):
    spaces = {"hbm": pl.ANY, "scalar": pltpu.SMEM, "vmem": pltpu.VMEM}
    return [pl.BlockSpec(memory_space=spaces[apart.get(i, "vmem")]) for i in range(len(operands))]


def front_call(inputs, cotangent, dense, place):
    same_seq, route_ids, targets, slots = place
    operands = () if cotangent is None else (cotangent,)
    operands = operands + (inputs, same_seq, route_ids[:, None], targets[None, :])
    out_shape = (
        ((slots, D if cotangent is None else 2 * D), bf16),
        ((SLOT, 3 * D), bf16),
        ((HEADS // 2, 2 * SLOT, SLOT), f32),
        ((SLOT, D), bf16),
        ((SLOT, D), f32),
        ((SLOT, 128), f32),
        ((SLOT, 1), f32),
    )
    pieces, width, out_apart = 0, 4 * D, {}
    if isinstance(dense, tuple):
        gains, weight, router, diagonals = dense
        apart = {len(operands): "hbm"}
        operands = operands + (weight, gains, router, diagonals)
    else:
        offsets, spread, owner, *held = dense
        pieces, width = len(held), 4 * D + 128
        first = len(operands)
        apart = {first: "scalar", **{first + 3 + i: "hbm" for i in range(pieces)}}
        operands = operands + tuple(dense)
        out_apart = {len(out_shape): "hbm"}
        out_shape = out_shape + (
            ((D, 4 * D), bf16),
            ((8, D), f32),
            ((128, D), bf16),
            ((HEADS, 2 * SLOT), f32),
        )
    return kernel_call(
        functools.partial(
            front_kernel, lax.axis_size("dp") // 2, cotangent is not None, pieces
        ),
        "gathered_front" if pieces else "attention_front",
        out_shape,
        operands,
        5,
        (pltpu.VMEM((D, width), bf16), pltpu.SemaphoreType.DMA((max(2, pieces),))),
        in_specs=whole_blocks(operands, apart),
        out_specs=tuple(whole_blocks(out_shape, out_apart)),
    )


def expert_call(arrived, slope, experts_held, forward, backward, keep):
    own, other = arrived
    extent, units = own.shape[0], experts_held[0].shape[1]
    width = 2 * D if forward and backward else D
    kept = 0 if not keep else 2 if forward else 1
    step = 512
    replies = pl.BlockSpec((extent, width), lambda i: (0, 0))
    hidden = pl.BlockSpec((2 * extent, step), lambda i: (0, i))
    in_specs = [replies, replies] + ([] if slope is None else [hidden])
    in_specs = in_specs + [
        pl.BlockSpec((D, step), lambda i: (0, i)),
        pl.BlockSpec((step, D), lambda i: (i, 0)),
    ]
    return kernel_call(
        functools.partial(expert_kernel, forward, backward, keep),
        "experts_" + ("f" if forward else "") + ("b" if backward else ""),
        (((extent, width), bf16),) * 2 + (((2 * extent, units), bf16),) * kept,
        (own, other) + (() if slope is None else (slope,)) + experts_held,
        6 if width == D else 10,
        (pltpu.VMEM((2 * extent, width), f32),),
        grid=(units // step,),
        in_specs=in_specs,
        out_specs=(replies, replies) + (hidden,) * kept,
    )


def turn_call(cotangent, returned, inputs, kept, dense, place):
    gains, weight, router, _ = dense
    _, route_ids, targets, _ = place
    projected, probs, _, middle, route_probs, gate = kept
    rows = ((SLOT, D), f32)
    operands = (cotangent, returned, targets[:, None], route_ids[:, None], inputs, gains, weight)
    operands = operands + (router, projected, probs, middle, route_probs, gate)
    out_shape = (rows, rows, ((SLOT, D), bf16), ((SLOT, 3 * D), bf16))
    return kernel_call(
        turn_kernel,
        "turn_back",
        out_shape,
        operands,
        7,
        (pltpu.VMEM((D, 4 * D), bf16), pltpu.SemaphoreType.DMA((2,))),
        in_specs=whole_blocks(operands, {6: "hbm"}),
        out_specs=tuple(whole_blocks(out_shape, {})),
    )


def merge_call(grad_out, returned, result, kept, dense, place):
    gains, weight, router, _ = dense
    _, route_ids, targets, _ = place
    _, _, _, middle, route_probs, gate = kept
    experts = lax.axis_size("dp") // 2
    return kernel_call(
        functools.partial(merge_kernel, experts),
        "merge_back",
        (((SLOT, D), f32), ((8 + experts, D), f32)),
        (grad_out, returned, targets[:, None], route_ids[:, None], gains, router, middle)
        + (route_probs, gate, result),
        2,
    )


def attention_back_call(grad_middle, inputs, kept, dense):
    gains, weight, _, _ = dense
    projected, probs = kept[:2]
    operands = (grad_middle, inputs, gains, weight, projected, probs)
    out_shape = (
        ((SLOT, D), f32),
        ((SLOT, 3 * D), bf16),
        ((1, D), f32),
        ((HEADS, 2 * SLOT), f32),
    )
    return kernel_call(
        attention_back_kernel,
        "attention_back",
        out_shape,
        operands,
        7,
        (pltpu.VMEM((D, 4 * D), bf16), pltpu.SemaphoreType.DMA((2,))),
        in_specs=whole_blocks(operands, {3: "hbm"}),
        out_specs=tuple(whole_blocks(out_shape, {})),
    )


def pack_dense(gains, qkv, out, router, table):
    rows, kind = qkv.shape[0], qkv.dtype
    blank = jnp.zeros((rows, 128 - 8 - router.shape[1]), kind)
    entries = jnp.pad(table, (0, rows - table.shape[0]))[:, None]
    return jnp.concatenate(
        [qkv, out, gains.T, entries, jnp.zeros((rows, 5), kind), router, blank], axis=1
    )


def gather_pieces(piece):
    devices, extent = lax.axis_size("dp"), piece.shape[0]
    if devices != 16:
        gathered = lax.all_gather(piece, "dp", axis=0, tiled=True)
        return (jnp.zeros((1,), jnp.int32), [gathered])
    me = lax.axis_index("dp")
    z, y, core = me // 4, me // 2 % 2, me % 2

    def send(block, route):
        return lax.ppermute(block, "dp", route)

    upward = [(i, i + 4) for i in range(12)]
    downward = [(i + 4, i) for i in range(12)]
    ends = [(i, i + 12) for i in range(4)] + [(i + 12, i) for i in range(4)]
    rising, falling, far = send(piece, upward), send(piece, downward), send(piece, ends)
    at_end = (z == 0) | (z == 3)
    line = [
        piece,
        jnp.where(z == 0, falling, rising),
        jnp.where(at_end, far, falling),
        jnp.where(z < 2, send(falling, downward), send(rising, upward)),
    ]
    from_z = [z, jnp.where(z == 0, 1, z - 1), jnp.where(at_end, 3 - z, z + 1), (z + 2) % 4]
    pieces, owners = [], []
    for block, z_of in zip(line, from_z):
        for other_y, column in enumerate((block, send(block, [(i, i ^ 2) for i in range(16)]))):
            for other_core, held in enumerate((column, pair_swap(column))):
                pieces.append(held)
                owners.append(4 * z_of + 2 * (y ^ other_y) + (core ^ other_core))
    return (jnp.stack(owners).astype(jnp.int32) * extent, pieces)


def by_chips(mine, others, devices):
    return join_halves(mine, others).reshape(devices // 2, D // devices, -1)


def total_of(came):
    return jnp.sum(came.astype(f32), axis=0)


def feature_order(devices):
    extent = D // devices
    places = jnp.arange(D, dtype=jnp.int32)
    chip, row = places % (D // 2) // extent, places % extent
    core = (places // (D // 2) + lax.axis_index("dp") % 2) % 2
    return ((2 * chip + core) * extent + row)[None]


def table_places(onehot, devices):
    extent, used = D // devices, BUCKETS * HEADS // devices
    places = np.arange(D)
    held = places % extent < used
    entry = np.where(held, places // extent * used + places % extent, 0)
    spread = onehot[:, entry // HEADS] * held
    owner = entry % HEADS == np.arange(HEADS)[:, None]
    return (spread.astype(np.float32), owner.astype(np.float32))


def shards(
    edge_rows,
    lengths,
    routes,
    norm_gains,
    qkv_weight,
    out_weight,
    router_weight,
    bias_table,
    expert_in,
    expert_out,
):
    devices = lax.axis_size("dp")
    experts = devices // 2
    first_section = lax.axis_index("section") == 0
    onehot = bucket_onehot()
    experts_held = (expert_in[0], expert_out[0])
    spread, owner = table_places(onehot, devices)
    offsets, pieces = gather_pieces(
        pack_dense(norm_gains[0], qkv_weight[0], out_weight[0], router_weight[0], bias_table[0])
    )
    gathering = [offsets, jnp.asarray(spread), jnp.asarray(owner), *pieces]
    dense = None
    same_seq = same_sequence(lengths)
    capacity = 4 * SLOT // devices
    blocks = range(edge_rows.shape[1] // SLOT)
    local_rows = [edge_rows[0, b * SLOT : (b + 1) * SLOT] for b in blocks]
    routes_of = [routes[0, b * SLOT : (b + 1) * SLOT, 0] for b in blocks]
    places = [
        (same_seq[b], routes_of[b], expert_places(routes_of[b], experts, capacity), experts * capacity)
        for b in blocks
    ]
    slot_ids = jnp.arange(experts * capacity, dtype=jnp.int32)
    placings = [
        (place[2][:, None] == slot_ids[None]).astype(bf16) for place in places
    ]

    def stream(b):
        nonlocal dense
        place, placing, local = places[b], placings[b], local_rows[b]
        packed, _, _, _, middle, _, gate, *made = front_call(
            local, None, dense or gathering, place
        )
        if dense is None:
            weight, *small = made
            dense = (small[0], weight, small[1], small[2])
        came = yield packed
        own, other = expert_call(arrive(came), None, experts_held, True, False, False)
        came = yield join_halves(own, other)
        outputs = middle + gate * dot(placing, came)
        carried = section_shift(outputs.astype(bf16), 1)
        inputs = jnp.where(first_section, local, carried)

        packed, *kept = front_call(inputs, local, dense, place)
        came = yield packed
        arrived = arrive(came)
        own, other, active, slope = expert_call(arrived, None, experts_held, True, True, True)
        came = yield join_halves(own, other)
        outputs, result, grad_inputs, _ = turn_call(local, came, inputs, kept, dense, place)
        carried = section_shift(grad_inputs, -1)
        grad_out = jnp.where(first_section, carried, local)

        grad_result = (kept[5] * grad_out).astype(bf16)
        came = yield jnp.einsum(
            "ts,td->sd", placing, grad_result, preferred_element_type=f32
        ).astype(bf16)
        grad_rows = arrive(came)
        own, other, grad_hidden = expert_call(grad_rows, slope, experts_held, False, True, True)
        came = yield join_halves(own, other)
        grad_middle, small = merge_call(grad_out, came, result, kept, dense, place)
        last = b == len(blocks) - 1
        back = None if last else attention_back_call(grad_middle, inputs, kept, dense)
        return (
            (grad_middle, small, back),
            (inputs, outputs, kept, (arrived, active, grad_rows, grad_hidden)),
        )

    ends = in_turns([stream(b) for b in blocks])
    grad_middles, smalls, backs = [list(part) for part in zip(*[end[0] for end in ends])]
    inputs, outputs, kept, expert_rows = zip(*[end[1] for end in ends])
    order = feature_order(devices)
    mine, others = kernel_call(
        functools.partial(out_grad_kernel, len(blocks)),
        "out_gradient",
        (((D // 2, D), bf16),) * 2,
        (order,) + tuple(kept[b][2] for b in blocks) + tuple(grad_middles),
        2,
    )
    grad_first, grad_middles[-1] = lax.optimization_barrier(
        (by_chips(mine, others, devices), grad_middles[-1])
    )
    grad_out_w = chip_all_to_all(grad_first)
    backs[-1] = attention_back_call(grad_middles[-1], inputs[-1], kept[-1], dense)
    grad_inputs, grads, gain_ones, tables = zip(*backs)
    mine, others = kernel_call(
        functools.partial(qkv_grad_kernel, len(blocks), experts),
        "qkv_gradient",
        (((D // 2, 3 * D + 128), bf16),) * 2,
        (order, dense[0], spread, owner)
        + (*inputs, *grads, *gain_ones, *tables, *smalls),
        4,
        (pltpu.VMEM((128, D), f32),),
    )
    grad_out_w, others = lax.optimization_barrier((grad_out_w, others))
    total = total_of(chip_all_to_all(by_chips(mine, others, devices)))
    grad_out_w = total_of(grad_out_w)
    arrived, active, grad_rows, grad_hidden = zip(*expert_rows)
    arrived = jnp.concatenate([rows[:, :D] for pair in arrived for rows in pair])
    grad_rows = jnp.concatenate([rows for pair in grad_rows for rows in pair])
    grad_expert_out = jnp.einsum(
        "rf,rd->fd", jnp.concatenate(active), grad_rows, preferred_element_type=f32
    )
    grad_expert_in = jnp.einsum(
        "rd,rf->df", arrived, jnp.concatenate(grad_hidden), preferred_element_type=f32
    )
    edge_results = jnp.concatenate(
        [jnp.where(first_section, grad_inputs[b], outputs[b]) for b in blocks]
    )
    extra = total[:, 3 * D :]
    return (
        edge_results[None],
        extra[None, :, 0:2].swapaxes(1, 2),
        total[None, :, : 3 * D],
        grad_out_w[None],
        extra[None, :, 8 : 8 + experts],
        extra[None, : BUCKETS * HEADS // devices, 2],
        grad_expert_in[None],
        grad_expert_out[None],
    )


def solution(mesh):
    return jax.shard_map(
        shards,
        mesh=mesh,
        in_specs=(
            P("section", "dp", None),
            P("dp", None),
            P("section", "dp", None),
            P("section", None, "dp"),
            P("section", "dp", None),
            P("section", "dp", None),
            P("section", "dp", None),
            P("section", "dp"),
            P("section", None, "dp"),
            P("section", "dp", None),
        ),
        out_specs=(
            P("section", "dp", None),
            P("section", None, "dp"),
            P("section", "dp", None),
            P("section", "dp", None),
            P("section", "dp", None),
            P("section", "dp"),
            P("section", None, "dp"),
            P("section", "dp", None),
        ),
        check_vma=False,
    )
```

```python
import functools

import jax
import jax.numpy as jnp
import numpy as np
from jax import lax
from jax.experimental import pallas as pl
from jax.experimental.pallas import tpu as pltpu
from jax.sharding import PartitionSpec as P

D = 768
HEADS = 12
HEAD_DIM = 64
BUCKETS = 32
SLOT = 128


norm_eps = 1e-06
masked_score = -1e30
bucket_edges = (1, 2, 3, 4, 5, 6, 7, 8, 12, 16, 23, 32, 46, 64, 91)
bf16 = jnp.bfloat16
f32 = jnp.float32


def dot(lhs, rhs):
    return jnp.dot(lhs, rhs, preferred_element_type=f32)


def section_shift(block, distance):
    devices = range(lax.axis_size("section"))
    route = [(i - distance, i) for i in devices if i - distance in devices]
    return lax.ppermute(block, "section", route)


def pair_swap(block):
    return lax.ppermute(block, "dp", [(i, i ^ 1) for i in range(lax.axis_size("dp"))])


def chip_all_to_all(block):
    devices = lax.axis_size("dp")
    groups = [list(range(core, devices, 2)) for core in range(2)]
    return lax.all_to_all(
        block, "dp", split_axis=0, concat_axis=0, tiled=True, axis_index_groups=groups
    )


def rms_scale(values):
    return lax.rsqrt(jnp.mean(values * values, axis=-1, keepdims=True) + norm_eps)


def norm_backward(grad_normed, values, gain_row):
    inv_rms = rms_scale(values)
    weighted = grad_normed * gain_row
    grad_gain = jnp.sum(grad_normed * values * inv_rms, axis=0)
    grad_values = inv_rms * weighted - values * inv_rms**3 * jnp.mean(
        weighted * values, axis=-1, keepdims=True
    )
    return (grad_values, grad_gain)


def bucket_onehot():
    offset = np.arange(2 * SLOT) - SLOT
    bucket = np.sum(np.abs(offset)[:, None] >= np.array(bucket_edges), axis=1)
    bucket = bucket + BUCKETS // 2 * (offset > 0)
    return (bucket[:, None] == np.arange(BUCKETS)).astype(np.float32)


def same_sequence(lengths):
    bounds = jnp.cumsum(lengths, axis=-1)
    places = jnp.arange(SLOT, dtype=jnp.int32)
    owners = jnp.sum((places[:, None] >= bounds[:, None, :]).astype(jnp.int32), axis=-1)
    return (owners[:, :, None] == owners[:, None, :]).astype(f32)


def expert_places(route_ids, experts, capacity):
    names = jnp.arange(experts, dtype=jnp.int32)
    choose = (route_ids[:, None] == names).astype(jnp.int32)
    places = jnp.arange(SLOT, dtype=jnp.int32)
    earlier = (places[:, None] > places[None, :]).astype(bf16)
    before = dot(earlier, choose.astype(bf16)).astype(jnp.int32)
    rank_ids = jnp.sum(before * choose, axis=-1)
    return route_ids * capacity + rank_ids


def arrive(block):
    return (block, pair_swap(block))


def join_halves(own, other):
    return (own.astype(f32) + pair_swap(other).astype(f32)).astype(bf16)


def in_turns(streams):
    ends, values = [None] * len(streams), [None] * len(streams)
    travelling = None
    running = list(range(len(streams)))
    while running:
        for turn in list(running):
            try:
                block = streams[turn].send(values[turn])
            except StopIteration as stop:
                ends[turn] = stop.value
                running.remove(turn)
                if travelling is not None and running:
                    last, held = travelling
                    held, first = lax.optimization_barrier((held, ends[turn][0]))
                    ends[turn] = (first,) + ends[turn][1:]
                    values[last], travelling = held, None
                continue
            if travelling is not None:
                last, held = travelling
                held, block = lax.optimization_barrier((held, block))
                values[last] = held
            experts, width = lax.axis_size("dp") // 2, block.shape[-1]
            came = chip_all_to_all(block.reshape(experts, -1, width)).reshape(-1, width)
            values[turn], travelling = came, (turn, came)
    return ends


def dot_nt(lhs, rhs):
    return lax.dot_general(lhs, rhs, (((1,), (1,)), ((), ())), preferred_element_type=f32)


def dot_tn(lhs, rhs):
    return lax.dot_general(lhs, rhs, (((0,), (0,)), ((), ())), preferred_element_type=f32)


def lane_masks():
    low = lax.broadcasted_iota(jnp.int32, (1, 2 * HEAD_DIM), 1) < HEAD_DIM
    first = jnp.where(low, 1.0, 0.0)
    return (low, first.astype(bf16), (1.0 - first).astype(bf16))


def both_heads(slab, first, second):
    return jnp.concatenate([slab * first, slab * second], axis=0)


def own_lanes(low, stacked):
    return jnp.where(low, stacked[:SLOT], stacked[SLOT:])


def gelu_parts(hidden):
    rate, cubic = 0.7978845608028654, 0.044715
    squared = hidden * hidden
    bend = jnp.tanh(rate * hidden * (1.0 + cubic * squared))
    active = 0.5 * hidden * (1.0 + bend)
    slope = 0.5 * (1.0 + bend) + 0.5 * hidden * (1.0 - bend * bend) * rate * (
        1.0 + 3.0 * cubic * squared
    )
    return (active.astype(bf16), slope.astype(bf16))


def placing_of(targets, slots, dtype=bf16):
    return jnp.where(slots == targets, 1.0, 0.0).astype(dtype)


def load_weight(weight_ref, held_ref, sems):
    parts = [slice(0, 3 * D), slice(3 * D, 4 * D)]
    copies = [
        pltpu.make_async_copy(weight_ref.at[:, part], held_ref.at[:, part], sems.at[i])
        for i, part in enumerate(parts)
    ]
    return copies


def place_pieces(offsets_ref, piece_refs, held_ref, sems):
    copies = []
    for i, piece_ref in enumerate(piece_refs):
        rows = piece_ref.shape[0]
        start = pl.multiple_of(offsets_ref[i], 16) if len(piece_refs) > 1 else 0
        copies.append(
            pltpu.make_async_copy(piece_ref, held_ref.at[pl.ds(start, rows)], sems.at[i])
        )
    return copies


def front_kernel(experts, cotangent, pieces, *refs):
    if cotangent:
        first_ref, cotangent_ref, refs = refs[0], refs[1], refs[2:]
    inputs_ref, same_ref, route_ref, target_ref = refs[:4]
    refs = refs[4:]
    held_ref, sems = refs[-2:]
    if pieces:
        offsets_ref, spread_ref, owner_ref = refs[:3]
        piece_refs = refs[3 : 3 + pieces]
        refs = refs[3 + pieces :]
        weight_ref, gains_ref, router_ref, diagonals_ref = refs[7:11]
        copies = place_pieces(offsets_ref, piece_refs, held_ref, sems)
        for copy in copies:
            copy.start()
    else:
        weight_ref, gains_ref, router_ref, diagonals_ref = refs[:4]
        refs = refs[4:]
        copies = load_weight(weight_ref, held_ref, sems)
        for copy in copies:
            copy.start()
    (
        packed_ref,
        projected_ref,
        probs_ref,
        attended_ref,
        middle_ref,
        route_probs_ref,
        gate_ref,
    ) = refs[:7]
    inputs = inputs_ref[...].astype(f32)
    if cotangent:
        inputs = jnp.where(first_ref[0] > 0, cotangent_ref[...].astype(f32), inputs)
        refs[7][...] = inputs.astype(bf16)
    inv_rms = rms_scale(inputs)
    if pieces:
        for copy in copies:
            copy.wait()
        keep = pltpu.make_async_copy(held_ref.at[:, : 4 * D], weight_ref, sems.at[0])
        keep.start()
        extra = held_ref[:, 4 * D :].astype(f32).T
        gains_ref[...] = extra[0:8]
        router_ref[0:120] = extra[8:128].astype(bf16)
        router_ref[120:128] = jnp.zeros((8, D), bf16)
        diagonals_ref[...] = lax.dot_general(
            owner_ref[...] * extra[2:3],
            spread_ref[...],
            (((1,), (1,)), ((), ())),
            preferred_element_type=f32,
            precision=lax.Precision.HIGHEST,
        )
    else:
        copies[0].wait()
    normed = (inputs * inv_rms * gains_ref[0:1]).astype(bf16)
    projected_ref[...] = dot(normed, held_ref[:, : 3 * D]).astype(bf16)
    low, first, second = lane_masks()
    width = 2 * HEAD_DIM
    same = same_ref[...]
    same = jnp.concatenate([same, same], axis=0) > 0
    for pair in range(HEADS // 2):
        relative = jnp.concatenate(
            [
                pltpu.roll(
                    jnp.broadcast_to(diagonals_ref[head : head + 1], (SLOT, 2 * SLOT)),
                    SLOT,
                    1,
                    stride=1,
                    stride_axis=0,
                )[:, :SLOT]
                for head in (2 * pair, 2 * pair + 1)
            ],
            axis=0,
        )
        queries, keys, values = [
            projected_ref[:, part * D + pair * width : part * D + (pair + 1) * width]
            for part in range(3)
        ]
        scores = dot_nt(both_heads(queries, first, second), keys) * HEAD_DIM ** (-0.5) + relative
        scores = jnp.where(same, scores, masked_score)
        raised = jnp.exp(scores - jnp.max(scores, axis=-1, keepdims=True))
        probs = raised / jnp.sum(raised, axis=-1, keepdims=True)
        probs_ref[pair] = probs
        attended_ref[:, pair * width : (pair + 1) * width] = own_lanes(
            low, dot(probs.astype(bf16), values)
        ).astype(bf16)
    if not pieces:
        copies[1].wait()
    middle = inputs + dot(attended_ref[...], held_ref[:, 3 * D : 4 * D])
    middle_ref[...] = middle
    routed = (middle * rms_scale(middle) * gains_ref[1:2]).astype(bf16)
    logits = dot_nt(routed, router_ref[...])
    names = lax.broadcasted_iota(jnp.int32, (1, logits.shape[1]), 1)
    logits = jnp.where(names < experts, logits, masked_score)
    raised = jnp.exp(logits - jnp.max(logits, axis=-1, keepdims=True))
    route_probs = raised / jnp.sum(raised, axis=-1, keepdims=True)
    route_probs_ref[...] = route_probs
    gate = jnp.sum(jnp.where(names == route_ref[...], route_probs, 0.0), axis=-1, keepdims=True)
    gate_ref[...] = gate
    slots = lax.broadcasted_iota(jnp.int32, (packed_ref.shape[0], 1), 0)
    placing = placing_of(target_ref[...], slots)
    packed_ref[:, :D] = dot(placing, routed).astype(bf16)
    if cotangent:
        grad_result = (gate * cotangent_ref[...].astype(f32)).astype(bf16)
        packed_ref[:, D:] = dot(placing, grad_result).astype(bf16)
    if pieces:
        keep.wait()


def expert_kernel(forward, backward, keep, own_ref, other_ref, *refs):
    if backward and not forward:
        slope_ref, refs = refs[0], refs[1:]
    weight_in_ref, weight_out_ref, own_out_ref, other_out_ref = refs[:4]
    kept_refs, total_ref = refs[4:-1], refs[-1]
    grad_at = slice(D, 2 * D) if forward else slice(0, D)
    extent = own_ref.shape[0]
    step = pl.program_id(0)

    @pl.when(step == 0)
    def _():
        total_ref[...] = jnp.zeros_like(total_ref)

    rows = jnp.concatenate([own_ref[...], other_ref[...]], axis=0)
    if forward:
        active, slope = gelu_parts(dot(rows[:, :D], weight_in_ref[...]))
        total_ref[:, :D] += dot(active, weight_out_ref[...])
        if keep:
            kept_refs[0][...] = active
            kept_refs[1][...] = slope
    else:
        slope = slope_ref[...]
    if backward:
        grad_hidden = (
            dot_nt(rows[:, grad_at], weight_out_ref[...]) * slope.astype(f32)
        ).astype(bf16)
        total_ref[:, grad_at] += dot_nt(grad_hidden, weight_in_ref[...])
        if not forward:
            kept_refs[0][...] = grad_hidden

    @pl.when(step == pl.num_programs(0) - 1)
    def _():
        own_out_ref[...] = total_ref[:extent].astype(bf16)
        other_out_ref[...] = total_ref[extent:].astype(bf16)


def merge_back(
    grad_out, result, grad_sent, middle, gate, route_probs, route, router_ref, gains_ref
):
    grad_gate = jnp.sum(grad_out * result, axis=-1, keepdims=True)
    names = lax.broadcasted_iota(jnp.int32, (1, router_ref.shape[0]), 1)
    choose = jnp.where(names == route, 1.0, 0.0)
    grad_logits = (grad_gate * gate * (choose - route_probs)).astype(bf16)
    grad_routed = grad_sent + dot(grad_logits, router_ref[...])
    grad_middle_norm, grad_gain = norm_backward(grad_routed, middle, gains_ref[1:2])
    return (grad_out + grad_middle_norm, grad_gain, grad_logits)


def attention_back(
    grad_middle, inputs, gains_ref, held, projected_ref, probs_ref, grads_ref, table_ref
):
    weight_ref, copies = held
    copies[1].wait()
    grad_attended = dot_nt(grad_middle.astype(bf16), weight_ref[:, 3 * D :]).astype(bf16)
    low, first, second = lane_masks()
    width = 2 * HEAD_DIM
    scale_qk = HEAD_DIM ** (-0.5)
    places = [lax.broadcasted_iota(jnp.int32, (SLOT, SLOT), axis) for axis in range(2)]
    reverse = jnp.where(places[0] + places[1] == SLOT - 1, 1.0, 0.0).astype(bf16)
    for pair in range(HEADS // 2):
        columns = [
            slice(part * D + pair * width, part * D + (pair + 1) * width) for part in range(3)
        ]
        queries, keys, values = [projected_ref[:, part] for part in columns]
        grads = both_heads(grad_attended[:, pair * width : (pair + 1) * width], first, second)
        probs = probs_ref[pair]
        grad_probs = dot_nt(grads, values)
        grad_scores = (
            probs * (grad_probs - jnp.sum(probs * grad_probs, axis=-1, keepdims=True))
        ).astype(bf16)
        grads_ref[:, columns[0]] = (own_lanes(low, dot(grad_scores, keys)) * scale_qk).astype(bf16)
        grads_ref[:, columns[1]] = (
            dot_tn(grad_scores, both_heads(queries, first, second)) * scale_qk
        ).astype(bf16)
        grads_ref[:, columns[2]] = dot_tn(probs.astype(bf16), grads).astype(bf16)
        if table_ref is not None:
            for own in range(2):
                part = dot(reverse, grad_scores[own * SLOT : (own + 1) * SLOT])
                wide = jnp.concatenate([part, jnp.zeros_like(part)], axis=1)
                moved = pltpu.roll(wide, 1, 1, stride=1, stride_axis=0)
                head = 2 * pair + own
                table_ref[head : head + 1] = jnp.sum(moved, axis=0, keepdims=True)
    copies[0].wait()
    grad_normed = dot_nt(grads_ref[...], weight_ref[:, : 3 * D])
    grad_inputs_norm, grad_gain = norm_backward(grad_normed, inputs, gains_ref[0:1])
    return (grad_middle + grad_inputs_norm, grad_gain)


def start_weight(weight_ref, held_ref, sems):
    copies = load_weight(weight_ref, held_ref, sems)
    for copy in reversed(copies):
        copy.start()
    return (held_ref, copies)


def turn_kernel(
    cotangent_ref,
    returned_ref,
    target_ref,
    route_ref,
    inputs_ref,
    gains_ref,
    weight_ref,
    router_ref,
    projected_ref,
    probs_ref,
    middle_ref,
    route_probs_ref,
    gate_ref,
    outputs_ref,
    result_ref,
    grad_inputs_ref,
    grads_ref,
    held_ref,
    sems,
):
    held = start_weight(weight_ref, held_ref, sems)
    slots = lax.broadcasted_iota(jnp.int32, (1, returned_ref.shape[0]), 1)
    both = dot(placing_of(target_ref[...], slots), returned_ref[...])
    result = both[:, :D]
    result_ref[...] = result
    middle, gate = middle_ref[...], gate_ref[...]
    outputs_ref[...] = middle + gate * result
    grad_middle, _, _ = merge_back(
        cotangent_ref[...].astype(f32),
        result,
        both[:, D:],
        middle,
        gate,
        route_probs_ref[...],
        route_ref[...],
        router_ref,
        gains_ref,
    )
    grad_inputs, _ = attention_back(
        grad_middle,
        inputs_ref[...].astype(f32),
        gains_ref,
        held,
        projected_ref,
        probs_ref,
        grads_ref,
        None,
    )
    grad_inputs_ref[...] = grad_inputs.astype(bf16)


def back_kernel(
    experts,
    last,
    grad_out_ref,
    returned_ref,
    target_ref,
    route_ref,
    inputs_ref,
    gains_ref,
    weight_ref,
    router_ref,
    projected_ref,
    probs_ref,
    attended_ref,
    middle_ref,
    route_probs_ref,
    gate_ref,
    result_ref,
    *refs,
):
    if last:
        earlier = len(refs) - 9
        order_ref, earlier_refs, refs = refs[0], refs[1:earlier], refs[earlier:]
        mine_ref, others_ref, refs = refs[0], refs[1], refs[2:]
    else:
        grad_middle_ref, refs = refs[0], refs[1:]
    grad_inputs_ref, grads_ref, gain_ref, table_ref, small_ref, held_ref, sems = refs[-7:]
    held = start_weight(weight_ref, held_ref, sems)
    slots = lax.broadcasted_iota(jnp.int32, (1, returned_ref.shape[0]), 1)
    middle = middle_ref[...]
    grad_middle, grad_gain, grad_logits = merge_back(
        grad_out_ref[...].astype(f32),
        result_ref[...],
        dot(placing_of(target_ref[...], slots), returned_ref[...]),
        middle,
        gate_ref[...],
        route_probs_ref[...],
        route_ref[...],
        router_ref,
        gains_ref,
    )
    routed = (middle * rms_scale(middle) * gains_ref[1:2]).astype(bf16)
    small_ref[0:8] = jnp.broadcast_to(grad_gain[None], (8, D))
    small_ref[8:] = dot_tn(grad_logits, routed)[:experts]
    if last:
        half = len(earlier_refs) // 2
        attended = [ref[...] for ref in earlier_refs[:half]] + [attended_ref[...]]
        grads = [ref[...] for ref in earlier_refs[half:]] + [grad_middle]
        ordered = dot(jnp.concatenate(attended, axis=0), order_ref[...]).astype(bf16)
        total = dot_tn(ordered, jnp.concatenate(grads, axis=0).astype(bf16)).astype(bf16)
        mine_ref[...] = total[: D // 2]
        others_ref[...] = total[D // 2 :]
    else:
        grad_middle_ref[...] = grad_middle
    grad_inputs_ref[...], grad_gain = attention_back(
        grad_middle,
        inputs_ref[...].astype(f32),
        gains_ref,
        held,
        projected_ref,
        probs_ref,
        grads_ref,
        table_ref,
    )
    gain_ref[...] = grad_gain[None]


def qkv_grad_kernel(blocks, experts, order_ref, gains_ref, spread_ref, owner_ref, *refs):
    mine_ref, others_ref, wide_ref = refs[-3:]
    inputs_refs, grads_refs, gain_refs, table_refs, small_refs = [
        refs[part * blocks : (part + 1) * blocks] for part in range(5)
    ]
    ordering = order_ref[...]
    inputs = jnp.concatenate([ref[...] for ref in inputs_refs], axis=0).astype(f32)
    normed = (inputs * rms_scale(inputs) * gains_ref[0:1]).astype(bf16)
    normed = dot(normed, ordering).astype(bf16)
    for part in range(3):
        columns = slice(part * D, (part + 1) * D)
        grads = jnp.concatenate([grads_ref[:, columns] for grads_ref in grads_refs], axis=0)
        total = dot_tn(normed, grads).astype(bf16)
        mine_ref[:, columns] = total[: D // 2]
        others_ref[:, columns] = total[D // 2 :]
    diagonals = sum([table_ref[...] for table_ref in table_refs])
    entries = jnp.sum(
        owner_ref[...]
        * jnp.dot(
            diagonals,
            spread_ref[...],
            preferred_element_type=f32,
            precision=lax.Precision.HIGHEST,
        ),
        axis=0,
        keepdims=True,
    )
    small = sum([small_ref[...] for small_ref in small_refs])
    wide_ref[...] = jnp.zeros_like(wide_ref)
    wide_ref[0:1] = sum([gain_ref[...] for gain_ref in gain_refs])
    wide_ref[1:2] = small[0:1]
    wide_ref[2:3] = entries
    wide_ref[8 : 8 + experts] = small[8:]
    total = dot_tn(ordering, wide_ref[...].T.astype(bf16)).astype(bf16)
    mine_ref[:, 3 * D :] = total[: D // 2]
    others_ref[:, 3 * D :] = total[D // 2 :]


def kernel_call(kernel, name, out_shape, operands, micros, scratch=(), **blocks):
    return pl.pallas_call(
        kernel,
        out_shape=tuple(jax.ShapeDtypeStruct(*pair) for pair in out_shape),
        scratch_shapes=list(scratch),
        compiler_params=pltpu.CompilerParams(vmem_limit_bytes=62 * 1024 * 1024),
        cost_estimate=pl.CostEstimate(
            flops=int(micros * 5e8), bytes_accessed=int(micros * 3e6), transcendentals=0
        ),
        name=name,
        **blocks,
    )(*operands)


def whole_blocks(operands, apart):
    spaces = {"hbm": pl.ANY, "scalar": pltpu.SMEM, "vmem": pltpu.VMEM}
    return [pl.BlockSpec(memory_space=spaces[apart.get(i, "vmem")]) for i in range(len(operands))]


def front_call(inputs, own, dense, place):
    same_seq, route_column, _, target_row = place
    slots = 4 * SLOT // lax.axis_size("dp") * (lax.axis_size("dp") // 2)
    operands = () if own is None else own
    operands = operands + (inputs, same_seq, route_column, target_row)
    out_shape = (
        ((slots, D if own is None else 2 * D), bf16),
        ((SLOT, 3 * D), bf16),
        ((HEADS // 2, 2 * SLOT, SLOT), f32),
        ((SLOT, D), bf16),
        ((SLOT, D), f32),
        ((SLOT, 128), f32),
        ((SLOT, 1), f32),
    )
    pieces, width, out_apart = 0, 4 * D, {}
    if own is not None:
        out_shape = out_shape + (((SLOT, D), bf16),)
    if isinstance(dense, tuple):
        gains, weight, router, diagonals = dense
        apart = {len(operands): "hbm"} if own is None else {0: "scalar", len(operands): "hbm"}
        operands = operands + (weight, gains, router, diagonals)
    else:
        offsets, spread, owner, *held = dense
        pieces, width = len(held), 4 * D + 128
        first = len(operands)
        apart = {first: "scalar", **{first + 3 + i: "hbm" for i in range(pieces)}}
        operands = operands + tuple(dense)
        out_apart = {len(out_shape): "hbm"}
        out_shape = out_shape + (
            ((D, 4 * D), bf16),
            ((8, D), f32),
            ((128, D), bf16),
            ((HEADS, 2 * SLOT), f32),
        )
    return kernel_call(
        functools.partial(
            front_kernel, lax.axis_size("dp") // 2, own is not None, pieces
        ),
        "gathered_front" if pieces else "attention_front",
        out_shape,
        operands,
        5,
        (pltpu.VMEM((D, width), bf16), pltpu.SemaphoreType.DMA((max(2, pieces),))),
        in_specs=whole_blocks(operands, apart),
        out_specs=tuple(whole_blocks(out_shape, out_apart)),
    )


def expert_call(arrived, slope, experts_held, forward, backward, keep):
    own, other = arrived
    extent, units = own.shape[0], experts_held[0].shape[1]
    width = 2 * D if forward and backward else D
    kept = 0 if not keep else 2 if forward else 1
    step = 512
    replies = pl.BlockSpec((extent, width), lambda i: (0, 0))
    hidden = pl.BlockSpec((2 * extent, step), lambda i: (0, i))
    in_specs = [replies, replies] + ([] if slope is None else [hidden])
    in_specs = in_specs + [
        pl.BlockSpec((D, step), lambda i: (0, i)),
        pl.BlockSpec((step, D), lambda i: (i, 0)),
    ]
    return kernel_call(
        functools.partial(expert_kernel, forward, backward, keep),
        "experts_" + ("f" if forward else "") + ("b" if backward else ""),
        (((extent, width), bf16),) * 2 + (((2 * extent, units), bf16),) * kept,
        (own, other) + (() if slope is None else (slope,)) + experts_held,
        6 if width == D else 10,
        (pltpu.VMEM((2 * extent, width), f32),),
        grid=(units // step,),
        in_specs=in_specs,
        out_specs=(replies, replies) + (hidden,) * kept,
    )


def turn_call(cotangent, returned, inputs, kept, dense, place):
    gains, weight, router, _ = dense
    _, route_column, target_column, _ = place
    projected, probs, _, middle, route_probs, gate = kept
    rows = ((SLOT, D), f32)
    operands = (cotangent, returned, target_column, route_column, inputs, gains, weight)
    operands = operands + (router, projected, probs, middle, route_probs, gate)
    out_shape = (rows, rows, ((SLOT, D), bf16), ((SLOT, 3 * D), bf16))
    return kernel_call(
        turn_kernel,
        "turn_back",
        out_shape,
        operands,
        7,
        (pltpu.VMEM((D, 4 * D), bf16), pltpu.SemaphoreType.DMA((2,))),
        in_specs=whole_blocks(operands, {6: "hbm"}),
        out_specs=tuple(whole_blocks(out_shape, {})),
    )


def back_call(grad_out, returned, inputs, kept, result, dense, place, earlier):
    gains, weight, router, _ = dense
    _, route_column, target_column, _ = place
    experts = lax.axis_size("dp") // 2
    operands = (grad_out, returned, target_column, route_column, inputs, gains, weight, router)
    operands = operands + tuple(kept) + (result,) + earlier
    out_shape = (
        ((SLOT, D), f32),
        ((SLOT, 3 * D), bf16),
        ((1, D), f32),
        ((HEADS, 2 * SLOT), f32),
        ((8 + experts, D), f32),
    )
    first = (((D // 2, D), bf16),) * 2 if earlier else (((SLOT, D), f32),)
    out_shape = first + out_shape
    return kernel_call(
        functools.partial(back_kernel, experts, len(earlier) > 0),
        "back_and_out_gradient" if earlier else "back",
        out_shape,
        operands,
        9,
        (pltpu.VMEM((D, 4 * D), bf16), pltpu.SemaphoreType.DMA((2,))),
        in_specs=whole_blocks(operands, {6: "hbm"}),
        out_specs=tuple(whole_blocks(out_shape, {})),
    )


def pack_dense(gains, qkv, out, router, table):
    rows, kind = qkv.shape[0], qkv.dtype
    blank = jnp.zeros((rows, 128 - 8 - router.shape[1]), kind)
    entries = jnp.pad(table, (0, rows - table.shape[0]))[:, None]
    return jnp.concatenate(
        [qkv, out, gains.T, entries, jnp.zeros((rows, 5), kind), router, blank], axis=1
    )


def gather_pieces(piece, early):
    devices, extent = lax.axis_size("dp"), piece.shape[0]
    if devices != 16:
        gathered = lax.all_gather(piece, "dp", axis=0, tiled=True)
        return (jnp.zeros((1,), jnp.int32), [gathered], early)
    me = lax.axis_index("dp")

    def send(block, distance):
        return lax.ppermute(block, "dp", [(i, i ^ distance) for i in range(devices)])

    near, far = send(piece, 4), send(piece, 12)
    far, early = lax.optimization_barrier((far, early))
    pieces, owners = [], []
    for distance, block in ((0, piece), (4, near), (12, far), (8, send(far, 4))):
        for other_y, column in enumerate((block, send(block, 2))):
            for other_core, held in enumerate((column, send(column, 1))):
                pieces.append(held)
                owners.append(me ^ (distance + 2 * other_y + other_core))
    return (jnp.stack(owners).astype(jnp.int32) * extent, pieces, early)


def by_chips(mine, came, devices):
    summed = (mine.astype(f32) + came.astype(f32)).astype(bf16)
    return summed.reshape(devices // 2, D // devices, -1)


def total_of(came):
    return jnp.sum(came.astype(f32), axis=0)


def feature_order(devices):
    extent = D // devices
    places = np.arange(D)
    core = (places // (D // 2) + lax.axis_index("dp") % 2) % 2
    features = (2 * (places % (D // 2) // extent) + core) * extent + places % extent
    return (jnp.arange(D)[:, None] == features[None]).astype(bf16)


def table_places(onehot, devices):
    extent, used = D // devices, BUCKETS * HEADS // devices
    places = np.arange(D)
    held = places % extent < used
    entry = np.where(held, places // extent * used + places % extent, 0)
    spread = onehot[:, entry // HEADS] * held
    owner = entry % HEADS == np.arange(HEADS)[:, None]
    return (spread.astype(np.float32), owner.astype(np.float32))


def shards(
    edge_rows,
    lengths,
    routes,
    norm_gains,
    qkv_weight,
    out_weight,
    router_weight,
    bias_table,
    expert_in,
    expert_out,
):
    devices = lax.axis_size("dp")
    experts = devices // 2
    first_section = lax.axis_index("section") == 0
    onehot = bucket_onehot()
    experts_held = (expert_in[0], expert_out[0])
    spread, owner = table_places(onehot, devices)
    same_seq = same_sequence(lengths)
    capacity = 4 * SLOT // devices
    blocks = range(edge_rows.shape[1] // SLOT)
    local_rows = [edge_rows[0, b * SLOT : (b + 1) * SLOT] for b in blocks]
    slot_ids = jnp.arange(experts * capacity, dtype=jnp.int32)
    places, placings = [], []
    for b in blocks:
        route_ids = routes[0, b * SLOT : (b + 1) * SLOT, 0]
        targets = expert_places(route_ids, experts, capacity)
        places.append((same_seq[b], route_ids[:, None], targets[:, None], targets[None, :]))
        placings.append((targets[:, None] == slot_ids[None]).astype(bf16))
    early = (local_rows, places, placings, feature_order(devices))
    offsets, pieces, early = gather_pieces(
        pack_dense(norm_gains[0], qkv_weight[0], out_weight[0], router_weight[0], bias_table[0]),
        early,
    )
    local_rows, places, placings, order = early
    gathering = [offsets, jnp.asarray(spread), jnp.asarray(owner), *pieces]
    dense = None
    first_flag = first_section.astype(jnp.int32).reshape(1)

    def stream(b):
        nonlocal dense
        place, placing, local = places[b], placings[b], local_rows[b]
        packed, _, _, _, middle, _, gate, *made = front_call(
            local, None, dense or gathering, place
        )
        if dense is None:
            weight, *small = made
            dense = (small[0], weight, small[1], small[2])
        came = yield packed
        own, other = expert_call(arrive(came), None, experts_held, True, False, False)
        came = yield join_halves(own, other)
        outputs = middle + gate * dot(placing, came)
        carried = section_shift(outputs.astype(bf16), 1)
        packed, *kept, inputs = front_call(carried, (first_flag, local), dense, place)
        came = yield packed
        arrived = arrive(came)
        own, other, active, slope = expert_call(arrived, None, experts_held, True, True, True)
        came = yield join_halves(own, other)
        outputs, result, grad_inputs, _ = turn_call(local, came, inputs, kept, dense, place)
        carried = section_shift(grad_inputs, -1)
        grad_out = jnp.where(first_section, carried, local)

        grad_result = (kept[5] * grad_out).astype(bf16)
        came = yield jnp.einsum(
            "ts,td->sd", placing, grad_result, preferred_element_type=f32
        ).astype(bf16)
        grad_rows = arrive(came)
        own, other, grad_hidden = expert_call(grad_rows, slope, experts_held, False, True, True)
        came = yield join_halves(own, other)
        rest = (inputs, outputs, kept, (arrived, active, grad_rows, grad_hidden))
        if b == len(blocks) - 1:
            return (came, rest, (grad_out, result))
        return (back_call(grad_out, came, inputs, kept, result, dense, place, ()), rest)

    ends = in_turns([stream(b) for b in blocks])
    inputs, outputs, kept, expert_rows = zip(*[end[1] for end in ends])
    backs = [end[0] for end in ends[:-1]]
    earlier = (order, *[now[2] for now in kept[:-1]], *[back[0] for back in backs])
    returned, _, (grad_out, result) = ends[-1]
    mine, others, *back = back_call(
        grad_out, returned, inputs[-1], kept[-1], result, dense, places[-1], earlier
    )
    grad_out_w = chip_all_to_all(by_chips(mine, pair_swap(others), devices))
    grad_inputs, grads, gain_ones, tables, smalls = zip(*[now[1:] for now in backs], back)
    mine, others = kernel_call(
        functools.partial(qkv_grad_kernel, len(blocks), experts),
        "qkv_gradient",
        (((D // 2, 3 * D + 128), bf16),) * 2,
        (order, dense[0], spread, owner)
        + (*inputs, *grads, *gain_ones, *tables, *smalls),
        4,
        (pltpu.VMEM((128, D), f32),),
    )
    grad_out_w, others = lax.optimization_barrier((grad_out_w, pair_swap(others)))
    total = total_of(chip_all_to_all(by_chips(mine, others, devices)))
    grad_out_w = total_of(grad_out_w)
    arrived, active, grad_rows, grad_hidden = zip(*expert_rows)
    arrived = jnp.concatenate([rows[:, :D] for pair in arrived for rows in pair])
    grad_rows = jnp.concatenate([rows for pair in grad_rows for rows in pair])
    grad_expert_out = jnp.einsum(
        "rf,rd->fd", jnp.concatenate(active), grad_rows, preferred_element_type=f32
    )
    grad_expert_in = jnp.einsum(
        "rd,rf->df", arrived, jnp.concatenate(grad_hidden), preferred_element_type=f32
    )
    edge_results = jnp.concatenate(
        [jnp.where(first_section, grad_inputs[b], outputs[b]) for b in blocks]
    )
    extra = total[:, 3 * D :]
    return (
        edge_results[None],
        extra[None, :, 0:2].swapaxes(1, 2),
        total[None, :, : 3 * D],
        grad_out_w[None],
        extra[None, :, 8 : 8 + experts],
        extra[None, : BUCKETS * HEADS // devices, 2],
        grad_expert_in[None],
        grad_expert_out[None],
    )


def solution(mesh):
    return jax.shard_map(
        shards,
        mesh=mesh,
        in_specs=(
            P("section", "dp", None),
            P("dp", None),
            P("section", "dp", None),
            P("section", None, "dp"),
            P("section", "dp", None),
            P("section", "dp", None),
            P("section", "dp", None),
            P("section", "dp"),
            P("section", None, "dp"),
            P("section", "dp", None),
        ),
        out_specs=(
            P("section", "dp", None),
            P("section", None, "dp"),
            P("section", "dp", None),
            P("section", "dp", None),
            P("section", "dp", None),
            P("section", "dp"),
            P("section", None, "dp"),
            P("section", "dp", None),
        ),
        check_vma=False,
    )
```

```python
import functools

import jax
import jax.numpy as jnp
import numpy as np
from jax import lax
from jax.experimental import pallas as pl
from jax.experimental.pallas import tpu as pltpu
from jax.sharding import PartitionSpec as P

D = 768
HEADS = 12
HEAD_DIM = 64
BUCKETS = 32
SLOT = 128


norm_eps = 1e-06
masked_score = -1e30
bucket_edges = (1, 2, 3, 4, 5, 6, 7, 8, 12, 16, 23, 32, 46, 64, 91)
bf16 = jnp.bfloat16
f32 = jnp.float32


def dot(lhs, rhs):
    return jnp.dot(lhs, rhs, preferred_element_type=f32)


def section_shift(block, distance):
    devices = range(lax.axis_size("section"))
    route = [(i - distance, i) for i in devices if i - distance in devices]
    return lax.ppermute(block, "section", route)


def pair_swap(block):
    return lax.ppermute(block, "dp", [(i, i ^ 1) for i in range(lax.axis_size("dp"))])


def chip_all_to_all(block):
    devices = lax.axis_size("dp")
    groups = [list(range(core, devices, 2)) for core in range(2)]
    return lax.all_to_all(
        block, "dp", split_axis=0, concat_axis=0, tiled=True, axis_index_groups=groups
    )


def rms_scale(values):
    return lax.rsqrt(jnp.mean(values * values, axis=-1, keepdims=True) + norm_eps)


def norm_backward(grad_normed, values, gain_row):
    inv_rms = rms_scale(values)
    weighted = grad_normed * gain_row
    grad_gain = jnp.sum(grad_normed * values * inv_rms, axis=0)
    grad_values = inv_rms * weighted - values * inv_rms**3 * jnp.mean(
        weighted * values, axis=-1, keepdims=True
    )
    return (grad_values, grad_gain)


def bucket_onehot():
    offset = np.arange(2 * SLOT) - SLOT
    bucket = np.sum(np.abs(offset)[:, None] >= np.array(bucket_edges), axis=1)
    bucket = bucket + BUCKETS // 2 * (offset > 0)
    return (bucket[:, None] == np.arange(BUCKETS)).astype(np.float32)


def same_sequence(lengths):
    bounds = jnp.cumsum(lengths, axis=-1)
    places = jnp.arange(SLOT, dtype=jnp.int32)
    owners = jnp.sum((places[:, None] >= bounds[:, None, :]).astype(jnp.int32), axis=-1)
    return (owners[:, :, None] == owners[:, None, :]).astype(f32)


def expert_places(route_ids, experts, capacity):
    names = jnp.arange(experts, dtype=jnp.int32)
    choose = (route_ids[:, None] == names).astype(jnp.int32)
    places = jnp.arange(SLOT, dtype=jnp.int32)
    earlier = (places[:, None] > places[None, :]).astype(bf16)
    before = dot(earlier, choose.astype(bf16)).astype(jnp.int32)
    rank_ids = jnp.sum(before * choose, axis=-1)
    return route_ids * capacity + rank_ids


def arrive(block):
    return (block, pair_swap(block))


def join_halves(own, other):
    return (own.astype(f32) + pair_swap(other).astype(f32)).astype(bf16)


def in_turns(streams):
    ends, values = [None] * len(streams), [None] * len(streams)
    travelling = None
    running = list(range(len(streams)))
    while running:
        for turn in list(running):
            try:
                block = streams[turn].send(values[turn])
            except StopIteration as stop:
                ends[turn] = stop.value
                running.remove(turn)
                if travelling is not None and running:
                    last, held = travelling
                    held, first = lax.optimization_barrier((held, ends[turn][0]))
                    ends[turn] = (first,) + ends[turn][1:]
                    values[last], travelling = held, None
                continue
            if travelling is not None:
                last, held = travelling
                held, block = lax.optimization_barrier((held, block))
                values[last] = held
            experts, width = lax.axis_size("dp") // 2, block.shape[-1]
            came = chip_all_to_all(block.reshape(experts, -1, width)).reshape(-1, width)
            values[turn], travelling = came, (turn, came)
    return ends


def dot_nt(lhs, rhs):
    return lax.dot_general(lhs, rhs, (((1,), (1,)), ((), ())), preferred_element_type=f32)


def dot_tn(lhs, rhs):
    return lax.dot_general(lhs, rhs, (((0,), (0,)), ((), ())), preferred_element_type=f32)


def lane_masks():
    low = lax.broadcasted_iota(jnp.int32, (1, 2 * HEAD_DIM), 1) < HEAD_DIM
    first = jnp.where(low, 1.0, 0.0)
    return (low, first.astype(bf16), (1.0 - first).astype(bf16))


def both_heads(slab, first, second):
    return jnp.concatenate([slab * first, slab * second], axis=0)


def own_lanes(low, stacked):
    return jnp.where(low, stacked[:SLOT], stacked[SLOT:])


def gelu_parts(hidden):
    rate, cubic = 0.7978845608028654, 0.044715
    squared = hidden * hidden
    bend = jnp.tanh(rate * hidden * (1.0 + cubic * squared))
    active = 0.5 * hidden * (1.0 + bend)
    slope = 0.5 * (1.0 + bend) + 0.5 * hidden * (1.0 - bend * bend) * rate * (
        1.0 + 3.0 * cubic * squared
    )
    return (active.astype(bf16), slope.astype(bf16))


def placing_of(targets, slots, dtype=bf16):
    return jnp.where(slots == targets, 1.0, 0.0).astype(dtype)


def load_weight(weight_ref, held_ref, sems):
    parts = [slice(0, 3 * D), slice(3 * D, 4 * D)]
    copies = [
        pltpu.make_async_copy(weight_ref.at[:, part], held_ref.at[:, part], sems.at[i])
        for i, part in enumerate(parts)
    ]
    return copies


def place_pieces(offsets_ref, piece_refs, held_ref, sems):
    copies = []
    for i, piece_ref in enumerate(piece_refs):
        rows = piece_ref.shape[0]
        start = pl.multiple_of(offsets_ref[i], 16) if len(piece_refs) > 1 else 0
        copies.append(
            pltpu.make_async_copy(piece_ref, held_ref.at[pl.ds(start, rows)], sems.at[i])
        )
    return copies


def front_kernel(experts, cotangent, pieces, *refs):
    if cotangent:
        first_ref, cotangent_ref, refs = refs[0], refs[1], refs[2:]
    inputs_ref, same_ref, route_ref, target_ref = refs[:4]
    refs = refs[4:]
    held_ref, sems = refs[-2:]
    if pieces:
        offsets_ref, spread_ref, owner_ref = refs[:3]
        piece_refs = refs[3 : 3 + pieces]
        refs = refs[3 + pieces :]
        weight_ref, gains_ref, router_ref, diagonals_ref = refs[7:11]
        copies = place_pieces(offsets_ref, piece_refs, held_ref, sems)
        for copy in copies:
            copy.start()
    else:
        weight_ref, gains_ref, router_ref, diagonals_ref = refs[:4]
        refs = refs[4:]
        copies = load_weight(weight_ref, held_ref, sems)
        for copy in copies:
            copy.start()
    (
        packed_ref,
        projected_ref,
        probs_ref,
        attended_ref,
        middle_ref,
        route_probs_ref,
        gate_ref,
    ) = refs[:7]
    inputs = inputs_ref[...].astype(f32)
    if cotangent:
        inputs = jnp.where(first_ref[0] > 0, cotangent_ref[...].astype(f32), inputs)
        refs[7][...] = inputs.astype(bf16)
    inv_rms = rms_scale(inputs)
    if pieces:
        for copy in copies:
            copy.wait()
        keep = pltpu.make_async_copy(held_ref.at[:, : 4 * D], weight_ref, sems.at[0])
        keep.start()
        extra = held_ref[:, 4 * D :].astype(f32).T
        gains_ref[...] = extra[0:8]
        router_ref[0:120] = extra[8:128].astype(bf16)
        router_ref[120:128] = jnp.zeros((8, D), bf16)
        diagonals_ref[...] = lax.dot_general(
            owner_ref[...] * extra[2:3],
            spread_ref[...],
            (((1,), (1,)), ((), ())),
            preferred_element_type=f32,
            precision=lax.Precision.HIGHEST,
        )
    else:
        copies[0].wait()
    normed = (inputs * inv_rms * gains_ref[0:1]).astype(bf16)
    projected_ref[...] = dot(normed, held_ref[:, : 3 * D]).astype(bf16)
    low, first, second = lane_masks()
    width = 2 * HEAD_DIM
    same = same_ref[...]
    same = jnp.concatenate([same, same], axis=0) > 0
    for pair in range(HEADS // 2):
        relative = jnp.concatenate(
            [
                pltpu.roll(
                    jnp.broadcast_to(diagonals_ref[head : head + 1], (SLOT, 2 * SLOT)),
                    SLOT,
                    1,
                    stride=1,
                    stride_axis=0,
                )[:, :SLOT]
                for head in (2 * pair, 2 * pair + 1)
            ],
            axis=0,
        )
        queries, keys, values = [
            projected_ref[:, part * D + pair * width : part * D + (pair + 1) * width]
            for part in range(3)
        ]
        scores = dot_nt(both_heads(queries, first, second), keys) * HEAD_DIM ** (-0.5) + relative
        scores = jnp.where(same, scores, masked_score)
        raised = jnp.exp(scores - jnp.max(scores, axis=-1, keepdims=True))
        probs = raised / jnp.sum(raised, axis=-1, keepdims=True)
        probs_ref[pair] = probs
        attended_ref[:, pair * width : (pair + 1) * width] = own_lanes(
            low, dot(probs.astype(bf16), values)
        ).astype(bf16)
    if not pieces:
        copies[1].wait()
    middle = inputs + dot(attended_ref[...], held_ref[:, 3 * D : 4 * D])
    middle_ref[...] = middle
    routed = (middle * rms_scale(middle) * gains_ref[1:2]).astype(bf16)
    logits = dot_nt(routed, router_ref[...])
    names = lax.broadcasted_iota(jnp.int32, (1, logits.shape[1]), 1)
    logits = jnp.where(names < experts, logits, masked_score)
    raised = jnp.exp(logits - jnp.max(logits, axis=-1, keepdims=True))
    route_probs = raised / jnp.sum(raised, axis=-1, keepdims=True)
    route_probs_ref[...] = route_probs
    gate = jnp.sum(jnp.where(names == route_ref[...], route_probs, 0.0), axis=-1, keepdims=True)
    gate_ref[...] = gate
    slots = lax.broadcasted_iota(jnp.int32, (packed_ref.shape[0], 1), 0)
    placing = placing_of(target_ref[...], slots)
    packed_ref[:, :D] = dot(placing, routed).astype(bf16)
    if cotangent:
        grad_result = (gate * cotangent_ref[...].astype(f32)).astype(bf16)
        packed_ref[:, D:] = dot(placing, grad_result).astype(bf16)
    if pieces:
        keep.wait()


def expert_kernel(forward, backward, keep, own_ref, other_ref, *refs):
    if backward and not forward:
        slope_ref, refs = refs[0], refs[1:]
    weight_in_ref, weight_out_ref, own_out_ref, other_out_ref = refs[:4]
    kept_refs, total_ref = refs[4:-1], refs[-1]
    grad_at = slice(D, 2 * D) if forward else slice(0, D)
    extent = own_ref.shape[0]
    step = pl.program_id(0)

    @pl.when(step == 0)
    def _():
        total_ref[...] = jnp.zeros_like(total_ref)

    rows = jnp.concatenate([own_ref[...], other_ref[...]], axis=0)
    if forward:
        active, slope = gelu_parts(dot(rows[:, :D], weight_in_ref[...]))
        total_ref[:, :D] += dot(active, weight_out_ref[...])
        if keep:
            kept_refs[0][...] = active
            kept_refs[1][...] = slope
    else:
        slope = slope_ref[...]
    if backward:
        grad_hidden = (
            dot_nt(rows[:, grad_at], weight_out_ref[...]) * slope.astype(f32)
        ).astype(bf16)
        total_ref[:, grad_at] += dot_nt(grad_hidden, weight_in_ref[...])
        if not forward:
            kept_refs[0][...] = grad_hidden

    @pl.when(step == pl.num_programs(0) - 1)
    def _():
        own_out_ref[...] = total_ref[:extent].astype(bf16)
        other_out_ref[...] = total_ref[extent:].astype(bf16)


def merge_back(
    grad_out, result, grad_sent, middle, gate, route_probs, route, router_ref, gains_ref
):
    grad_gate = jnp.sum(grad_out * result, axis=-1, keepdims=True)
    names = lax.broadcasted_iota(jnp.int32, (1, router_ref.shape[0]), 1)
    choose = jnp.where(names == route, 1.0, 0.0)
    grad_logits = (grad_gate * gate * (choose - route_probs)).astype(bf16)
    grad_routed = grad_sent + dot(grad_logits, router_ref[...])
    grad_middle_norm, grad_gain = norm_backward(grad_routed, middle, gains_ref[1:2])
    return (grad_out + grad_middle_norm, grad_gain, grad_logits)


def attention_back(
    grad_middle, inputs, gains_ref, held, projected_ref, probs_ref, grads_ref, table_ref
):
    weight_ref, copies = held
    copies[1].wait()
    grad_attended = dot_nt(grad_middle.astype(bf16), weight_ref[:, 3 * D :]).astype(bf16)
    low, first, second = lane_masks()
    width = 2 * HEAD_DIM
    scale_qk = HEAD_DIM ** (-0.5)
    places = [lax.broadcasted_iota(jnp.int32, (SLOT, SLOT), axis) for axis in range(2)]
    reverse = jnp.where(places[0] + places[1] == SLOT - 1, 1.0, 0.0).astype(bf16)
    for pair in range(HEADS // 2):
        columns = [
            slice(part * D + pair * width, part * D + (pair + 1) * width) for part in range(3)
        ]
        queries, keys, values = [projected_ref[:, part] for part in columns]
        grads = both_heads(grad_attended[:, pair * width : (pair + 1) * width], first, second)
        probs = probs_ref[pair]
        grad_probs = dot_nt(grads, values)
        grad_scores = (
            probs * (grad_probs - jnp.sum(probs * grad_probs, axis=-1, keepdims=True))
        ).astype(bf16)
        grads_ref[:, columns[0]] = (own_lanes(low, dot(grad_scores, keys)) * scale_qk).astype(bf16)
        grads_ref[:, columns[1]] = (
            dot_tn(grad_scores, both_heads(queries, first, second)) * scale_qk
        ).astype(bf16)
        grads_ref[:, columns[2]] = dot_tn(probs.astype(bf16), grads).astype(bf16)
        if table_ref is not None:
            for own in range(2):
                part = dot(reverse, grad_scores[own * SLOT : (own + 1) * SLOT])
                wide = jnp.concatenate([part, jnp.zeros_like(part)], axis=1)
                moved = pltpu.roll(wide, 1, 1, stride=1, stride_axis=0)
                head = 2 * pair + own
                table_ref[head : head + 1] = jnp.sum(moved, axis=0, keepdims=True)
    copies[0].wait()
    grad_normed = dot_nt(grads_ref[...], weight_ref[:, : 3 * D])
    grad_inputs_norm, grad_gain = norm_backward(grad_normed, inputs, gains_ref[0:1])
    return (grad_middle + grad_inputs_norm, grad_gain)


def start_weight(weight_ref, held_ref, sems):
    copies = load_weight(weight_ref, held_ref, sems)
    for copy in reversed(copies):
        copy.start()
    return (held_ref, copies)


def turn_kernel(
    cotangent_ref,
    returned_ref,
    target_ref,
    route_ref,
    inputs_ref,
    gains_ref,
    weight_ref,
    router_ref,
    projected_ref,
    probs_ref,
    middle_ref,
    route_probs_ref,
    gate_ref,
    outputs_ref,
    result_ref,
    grad_inputs_ref,
    grads_ref,
    held_ref,
    sems,
):
    held = start_weight(weight_ref, held_ref, sems)
    slots = lax.broadcasted_iota(jnp.int32, (1, returned_ref.shape[0]), 1)
    both = dot(placing_of(target_ref[...], slots), returned_ref[...])
    result = both[:, :D]
    result_ref[...] = result
    middle, gate = middle_ref[...], gate_ref[...]
    outputs_ref[...] = middle + gate * result
    grad_middle, _, _ = merge_back(
        cotangent_ref[...].astype(f32),
        result,
        both[:, D:],
        middle,
        gate,
        route_probs_ref[...],
        route_ref[...],
        router_ref,
        gains_ref,
    )
    grad_inputs, _ = attention_back(
        grad_middle,
        inputs_ref[...].astype(f32),
        gains_ref,
        held,
        projected_ref,
        probs_ref,
        grads_ref,
        None,
    )
    grad_inputs_ref[...] = grad_inputs.astype(bf16)


def back_kernel(
    experts,
    last,
    grad_out_ref,
    returned_ref,
    target_ref,
    route_ref,
    inputs_ref,
    gains_ref,
    weight_ref,
    router_ref,
    projected_ref,
    probs_ref,
    attended_ref,
    middle_ref,
    route_probs_ref,
    gate_ref,
    result_ref,
    *refs,
):
    if last:
        earlier = len(refs) - 9
        order_ref, earlier_refs, refs = refs[0], refs[1:earlier], refs[earlier:]
        mine_ref, others_ref, refs = refs[0], refs[1], refs[2:]
    else:
        grad_middle_ref, refs = refs[0], refs[1:]
    grad_inputs_ref, grads_ref, gain_ref, table_ref, small_ref, held_ref, sems = refs[-7:]
    held = start_weight(weight_ref, held_ref, sems)
    slots = lax.broadcasted_iota(jnp.int32, (1, returned_ref.shape[0]), 1)
    middle = middle_ref[...]
    grad_middle, grad_gain, grad_logits = merge_back(
        grad_out_ref[...].astype(f32),
        result_ref[...],
        dot(placing_of(target_ref[...], slots), returned_ref[...]),
        middle,
        gate_ref[...],
        route_probs_ref[...],
        route_ref[...],
        router_ref,
        gains_ref,
    )
    routed = (middle * rms_scale(middle) * gains_ref[1:2]).astype(bf16)
    small_ref[0:8] = jnp.broadcast_to(grad_gain[None], (8, D))
    small_ref[8:] = dot_tn(grad_logits, routed)[:experts]
    if last:
        half = len(earlier_refs) // 2
        attended = [ref[...] for ref in earlier_refs[:half]] + [attended_ref[...]]
        grads = [ref[...] for ref in earlier_refs[half:]] + [grad_middle]
        ordered = dot(jnp.concatenate(attended, axis=0), order_ref[...]).astype(bf16)
        total = dot_tn(ordered, jnp.concatenate(grads, axis=0).astype(bf16)).astype(bf16)
        mine_ref[...] = total[: D // 2]
        others_ref[...] = total[D // 2 :]
    else:
        grad_middle_ref[...] = grad_middle
    grad_inputs_ref[...], grad_gain = attention_back(
        grad_middle,
        inputs_ref[...].astype(f32),
        gains_ref,
        held,
        projected_ref,
        probs_ref,
        grads_ref,
        table_ref,
    )
    gain_ref[...] = grad_gain[None]


def qkv_grad_kernel(blocks, experts, order_ref, gains_ref, spread_ref, owner_ref, *refs):
    mine_ref, others_ref, wide_ref = refs[-3:]
    inputs_refs, grads_refs, gain_refs, table_refs, small_refs = [
        refs[part * blocks : (part + 1) * blocks] for part in range(5)
    ]
    ordering = order_ref[...]
    inputs = jnp.concatenate([ref[...] for ref in inputs_refs], axis=0).astype(f32)
    normed = (inputs * rms_scale(inputs) * gains_ref[0:1]).astype(bf16)
    normed = dot(normed, ordering).astype(bf16)
    for part in range(3):
        columns = slice(part * D, (part + 1) * D)
        grads = jnp.concatenate([grads_ref[:, columns] for grads_ref in grads_refs], axis=0)
        total = dot_tn(normed, grads).astype(bf16)
        mine_ref[:, columns] = total[: D // 2]
        others_ref[:, columns] = total[D // 2 :]
    diagonals = sum([table_ref[...] for table_ref in table_refs])
    entries = jnp.sum(
        owner_ref[...]
        * jnp.dot(
            diagonals,
            spread_ref[...],
            preferred_element_type=f32,
            precision=lax.Precision.HIGHEST,
        ),
        axis=0,
        keepdims=True,
    )
    small = sum([small_ref[...] for small_ref in small_refs])
    wide_ref[...] = jnp.zeros_like(wide_ref)
    wide_ref[0:1] = sum([gain_ref[...] for gain_ref in gain_refs])
    wide_ref[1:2] = small[0:1]
    wide_ref[2:3] = entries
    wide_ref[8 : 8 + experts] = small[8:]
    total = dot_tn(ordering, wide_ref[...].T.astype(bf16)).astype(bf16)
    mine_ref[:, 3 * D :] = total[: D // 2]
    others_ref[:, 3 * D :] = total[D // 2 :]


def kernel_call(kernel, name, out_shape, operands, micros, scratch=(), **blocks):
    return pl.pallas_call(
        kernel,
        out_shape=tuple(jax.ShapeDtypeStruct(*pair) for pair in out_shape),
        scratch_shapes=list(scratch),
        compiler_params=pltpu.CompilerParams(vmem_limit_bytes=62 * 1024 * 1024),
        cost_estimate=pl.CostEstimate(
            flops=int(micros * 5e8), bytes_accessed=int(micros * 3e6), transcendentals=0
        ),
        name=name,
        **blocks,
    )(*operands)


def whole_blocks(operands, apart):
    spaces = {"hbm": pl.ANY, "scalar": pltpu.SMEM, "vmem": pltpu.VMEM}
    return [pl.BlockSpec(memory_space=spaces[apart.get(i, "vmem")]) for i in range(len(operands))]


def front_call(inputs, own, dense, place):
    same_seq, route_column, _, target_row = place
    slots = 4 * SLOT // lax.axis_size("dp") * (lax.axis_size("dp") // 2)
    operands = () if own is None else own
    operands = operands + (inputs, same_seq, route_column, target_row)
    out_shape = (
        ((slots, D if own is None else 2 * D), bf16),
        ((SLOT, 3 * D), bf16),
        ((HEADS // 2, 2 * SLOT, SLOT), f32),
        ((SLOT, D), bf16),
        ((SLOT, D), f32),
        ((SLOT, 128), f32),
        ((SLOT, 1), f32),
    )
    pieces, width, out_apart = 0, 4 * D, {}
    if own is not None:
        out_shape = out_shape + (((SLOT, D), bf16),)
    if isinstance(dense, tuple):
        gains, weight, router, diagonals = dense
        apart = {len(operands): "hbm"} if own is None else {0: "scalar", len(operands): "hbm"}
        operands = operands + (weight, gains, router, diagonals)
    else:
        offsets, spread, owner, *held = dense
        pieces, width = len(held), 4 * D + 128
        first = len(operands)
        apart = {first: "scalar", **{first + 3 + i: "hbm" for i in range(pieces)}}
        operands = operands + tuple(dense)
        out_apart = {len(out_shape): "hbm"}
        out_shape = out_shape + (
            ((D, 4 * D), bf16),
            ((8, D), f32),
            ((128, D), bf16),
            ((HEADS, 2 * SLOT), f32),
        )
    return kernel_call(
        functools.partial(
            front_kernel, lax.axis_size("dp") // 2, own is not None, pieces
        ),
        "gathered_front" if pieces else "attention_front",
        out_shape,
        operands,
        5,
        (pltpu.VMEM((D, width), bf16), pltpu.SemaphoreType.DMA((max(2, pieces),))),
        in_specs=whole_blocks(operands, apart),
        out_specs=tuple(whole_blocks(out_shape, out_apart)),
    )


def expert_call(arrived, slope, experts_held, forward, backward, keep):
    own, other = arrived
    extent, units = own.shape[0], experts_held[0].shape[1]
    width = 2 * D if forward and backward else D
    kept = 0 if not keep else 2 if forward else 1
    step = 512
    replies = pl.BlockSpec((extent, width), lambda i: (0, 0))
    hidden = pl.BlockSpec((2 * extent, step), lambda i: (0, i))
    in_specs = [replies, replies] + ([] if slope is None else [hidden])
    in_specs = in_specs + [
        pl.BlockSpec((D, step), lambda i: (0, i)),
        pl.BlockSpec((step, D), lambda i: (i, 0)),
    ]
    return kernel_call(
        functools.partial(expert_kernel, forward, backward, keep),
        "experts_" + ("f" if forward else "") + ("b" if backward else ""),
        (((extent, width), bf16),) * 2 + (((2 * extent, units), bf16),) * kept,
        (own, other) + (() if slope is None else (slope,)) + experts_held,
        6 if width == D else 10,
        (pltpu.VMEM((2 * extent, width), f32),),
        grid=(units // step,),
        in_specs=in_specs,
        out_specs=(replies, replies) + (hidden,) * kept,
    )


def turn_call(cotangent, returned, inputs, kept, dense, place):
    gains, weight, router, _ = dense
    _, route_column, target_column, _ = place
    projected, probs, _, middle, route_probs, gate = kept
    rows = ((SLOT, D), f32)
    operands = (cotangent, returned, target_column, route_column, inputs, gains, weight)
    operands = operands + (router, projected, probs, middle, route_probs, gate)
    out_shape = (rows, rows, ((SLOT, D), bf16), ((SLOT, 3 * D), bf16))
    return kernel_call(
        turn_kernel,
        "turn_back",
        out_shape,
        operands,
        7,
        (pltpu.VMEM((D, 4 * D), bf16), pltpu.SemaphoreType.DMA((2,))),
        in_specs=whole_blocks(operands, {6: "hbm"}),
        out_specs=tuple(whole_blocks(out_shape, {})),
    )


def back_call(grad_out, returned, inputs, kept, result, dense, place, earlier):
    gains, weight, router, _ = dense
    _, route_column, target_column, _ = place
    experts = lax.axis_size("dp") // 2
    operands = (grad_out, returned, target_column, route_column, inputs, gains, weight, router)
    operands = operands + tuple(kept) + (result,) + earlier
    out_shape = (
        ((SLOT, D), f32),
        ((SLOT, 3 * D), bf16),
        ((1, D), f32),
        ((HEADS, 2 * SLOT), f32),
        ((8 + experts, D), f32),
    )
    first = (((D // 2, D), bf16),) * 2 if earlier else (((SLOT, D), f32),)
    out_shape = first + out_shape
    return kernel_call(
        functools.partial(back_kernel, experts, len(earlier) > 0),
        "back_and_out_gradient" if earlier else "back",
        out_shape,
        operands,
        9,
        (pltpu.VMEM((D, 4 * D), bf16), pltpu.SemaphoreType.DMA((2,))),
        in_specs=whole_blocks(operands, {6: "hbm"}),
        out_specs=tuple(whole_blocks(out_shape, {})),
    )


def pack_dense(gains, qkv, out, router, table):
    rows, kind = qkv.shape[0], qkv.dtype
    blank = jnp.zeros((rows, 128 - 8 - router.shape[1]), kind)
    entries = jnp.pad(table, (0, rows - table.shape[0]))[:, None]
    return jnp.concatenate(
        [qkv, out, gains.T, entries, jnp.zeros((rows, 5), kind), router, blank], axis=1
    )


def gather_pieces(piece, early):
    devices, extent = lax.axis_size("dp"), piece.shape[0]
    if devices != 16:
        gathered = lax.all_gather(piece, "dp", axis=0, tiled=True)
        return (jnp.zeros((1,), jnp.int32), [gathered], early)
    me = lax.axis_index("dp")

    def send(block, distance):
        return lax.ppermute(block, "dp", [(i, i ^ distance) for i in range(devices)])

    near, far = send(piece, 4), send(piece, 12)
    far, early = lax.optimization_barrier((far, early))
    pieces, owners = [], []
    for distance, block in ((0, piece), (4, near), (12, far), (8, send(far, 4))):
        for other_y, column in enumerate((block, send(block, 2))):
            for other_core, held in enumerate((column, send(column, 1))):
                pieces.append(held)
                owners.append(me ^ (distance + 2 * other_y + other_core))
    return (jnp.stack(owners).astype(jnp.int32) * extent, pieces, early)


def swap(block, distance):
    route = [(i, i ^ distance) for i in range(lax.axis_size("dp"))]
    return lax.ppermute(block, "dp", route)


def sum_of_four(mine, came):
    half = mine.shape[0] // 2
    far = (mine[half:].astype(f32) + came[half:].astype(f32)).astype(bf16)
    near = mine[:half].astype(f32) + came[:half].astype(f32)
    return (near + swap(far, 2).astype(f32)).astype(bf16)


def total_of(summed):
    devices = lax.axis_size("dp")
    groups = [list(range(first, devices, 4)) for first in range(4)]
    came = lax.all_to_all(
        summed.reshape(devices // 4, D // devices, -1),
        "dp",
        split_axis=0,
        concat_axis=0,
        tiled=True,
        axis_index_groups=groups,
    )
    return jnp.sum(came.astype(f32), axis=0)


def feature_order(devices):
    extent = D // devices
    places = np.arange(D)
    quarter, rest = places // (D // 4), places % (D // 4)
    place = (quarter // 2 + 2 * (quarter % 2)) ^ (lax.axis_index("dp") % 4)
    features = (4 * (rest // extent) + place) * extent + rest % extent
    return (jnp.arange(D)[:, None] == features[None]).astype(bf16)


def table_places(onehot, devices):
    extent, used = D // devices, BUCKETS * HEADS // devices
    places = np.arange(D)
    held = places % extent < used
    entry = np.where(held, places // extent * used + places % extent, 0)
    spread = onehot[:, entry // HEADS] * held
    owner = entry % HEADS == np.arange(HEADS)[:, None]
    return (spread.astype(np.float32), owner.astype(np.float32))


def shards(
    edge_rows,
    lengths,
    routes,
    norm_gains,
    qkv_weight,
    out_weight,
    router_weight,
    bias_table,
    expert_in,
    expert_out,
):
    devices = lax.axis_size("dp")
    experts = devices // 2
    first_section = lax.axis_index("section") == 0
    onehot = bucket_onehot()
    experts_held = (expert_in[0], expert_out[0])
    spread, owner = table_places(onehot, devices)
    same_seq = same_sequence(lengths)
    capacity = 4 * SLOT // devices
    blocks = range(edge_rows.shape[1] // SLOT)
    local_rows = [edge_rows[0, b * SLOT : (b + 1) * SLOT] for b in blocks]
    slot_ids = jnp.arange(experts * capacity, dtype=jnp.int32)
    places, placings = [], []
    for b in blocks:
        route_ids = routes[0, b * SLOT : (b + 1) * SLOT, 0]
        targets = expert_places(route_ids, experts, capacity)
        places.append((same_seq[b], route_ids[:, None], targets[:, None], targets[None, :]))
        placings.append((targets[:, None] == slot_ids[None]).astype(bf16))
    early = (local_rows, places, placings, feature_order(devices))
    offsets, pieces, early = gather_pieces(
        pack_dense(norm_gains[0], qkv_weight[0], out_weight[0], router_weight[0], bias_table[0]),
        early,
    )
    local_rows, places, placings, order = early
    gathering = [offsets, jnp.asarray(spread), jnp.asarray(owner), *pieces]
    dense = None
    first_flag = first_section.astype(jnp.int32).reshape(1)

    def stream(b):
        nonlocal dense
        place, placing, local = places[b], placings[b], local_rows[b]
        packed, _, _, _, middle, _, gate, *made = front_call(
            local, None, dense or gathering, place
        )
        if dense is None:
            weight, *small = made
            dense = (small[0], weight, small[1], small[2])
        came = yield packed
        own, other = expert_call(arrive(came), None, experts_held, True, False, False)
        came = yield join_halves(own, other)
        outputs = middle + gate * dot(placing, came)
        carried = section_shift(outputs.astype(bf16), 1)
        packed, *kept, inputs = front_call(carried, (first_flag, local), dense, place)
        came = yield packed
        arrived = arrive(came)
        own, other, active, slope = expert_call(arrived, None, experts_held, True, True, True)
        came = yield join_halves(own, other)
        outputs, result, grad_inputs, _ = turn_call(local, came, inputs, kept, dense, place)
        carried = section_shift(grad_inputs, -1)
        grad_out = jnp.where(first_section, carried, local)

        grad_result = (kept[5] * grad_out).astype(bf16)
        came = yield jnp.einsum(
            "ts,td->sd", placing, grad_result, preferred_element_type=f32
        ).astype(bf16)
        grad_rows = arrive(came)
        own, other, grad_hidden = expert_call(grad_rows, slope, experts_held, False, True, True)
        came = yield join_halves(own, other)
        rest = (inputs, outputs, kept, (arrived, active, grad_rows, grad_hidden))
        if b == len(blocks) - 1:
            return (came, rest, (grad_out, result))
        return (back_call(grad_out, came, inputs, kept, result, dense, place, ()), rest)

    ends = in_turns([stream(b) for b in blocks])
    inputs, outputs, kept, expert_rows = zip(*[end[1] for end in ends])
    backs = [end[0] for end in ends[:-1]]
    earlier = (order, *[now[2] for now in kept[:-1]], *[back[0] for back in backs])
    returned, _, (grad_out, result) = ends[-1]
    mine, others, *back = back_call(
        grad_out, returned, inputs[-1], kept[-1], result, dense, places[-1], earlier
    )
    grad_first = sum_of_four(mine, pair_swap(others))
    grad_inputs, grads, gain_ones, tables, smalls = zip(*[now[1:] for now in backs], back)
    mine, others = kernel_call(
        functools.partial(qkv_grad_kernel, len(blocks), experts),
        "qkv_gradient",
        (((D // 2, 3 * D + 128), bf16),) * 2,
        (order, dense[0], spread, owner)
        + (*inputs, *grads, *gain_ones, *tables, *smalls),
        4,
        (pltpu.VMEM((128, D), f32),),
    )
    grad_rest = sum_of_four(mine, pair_swap(others))
    grad_out_w = total_of(grad_first)
    grad_out_w, grad_rest = lax.optimization_barrier((grad_out_w, grad_rest))
    total = total_of(grad_rest)
    arrived, active, grad_rows, grad_hidden = zip(*expert_rows)
    arrived = jnp.concatenate([rows[:, :D] for pair in arrived for rows in pair])
    grad_rows = jnp.concatenate([rows for pair in grad_rows for rows in pair])
    grad_expert_out = jnp.einsum(
        "rf,rd->fd", jnp.concatenate(active), grad_rows, preferred_element_type=f32
    )
    grad_expert_in = jnp.einsum(
        "rd,rf->df", arrived, jnp.concatenate(grad_hidden), preferred_element_type=f32
    )
    edge_results = jnp.concatenate(
        [jnp.where(first_section, grad_inputs[b], outputs[b]) for b in blocks]
    )
    extra = total[:, 3 * D :]
    return (
        edge_results[None],
        extra[None, :, 0:2].swapaxes(1, 2),
        total[None, :, : 3 * D],
        grad_out_w[None],
        extra[None, :, 8 : 8 + experts],
        extra[None, : BUCKETS * HEADS // devices, 2],
        grad_expert_in[None],
        grad_expert_out[None],
    )


def solution(mesh):
    return jax.shard_map(
        shards,
        mesh=mesh,
        in_specs=(
            P("section", "dp", None),
            P("dp", None),
            P("section", "dp", None),
            P("section", None, "dp"),
            P("section", "dp", None),
            P("section", "dp", None),
            P("section", "dp", None),
            P("section", "dp"),
            P("section", None, "dp"),
            P("section", "dp", None),
        ),
        out_specs=(
            P("section", "dp", None),
            P("section", None, "dp"),
            P("section", "dp", None),
            P("section", "dp", None),
            P("section", "dp", None),
            P("section", "dp"),
            P("section", None, "dp"),
            P("section", "dp", None),
        ),
        check_vma=False,
    )
```

```python
import functools

import jax
import jax.numpy as jnp
import numpy as np
from jax import lax
from jax.experimental import pallas as pl
from jax.experimental.pallas import tpu as pltpu
from jax.sharding import PartitionSpec as P

D = 768
HEADS = 12
HEAD_DIM = 64
BUCKETS = 32
SLOT = 128


norm_eps = 1e-06
masked_score = -1e30
bucket_edges = (1, 2, 3, 4, 5, 6, 7, 8, 12, 16, 23, 32, 46, 64, 91)
bf16 = jnp.bfloat16
f32 = jnp.float32


def dot(lhs, rhs):
    return jnp.dot(lhs, rhs, preferred_element_type=f32)


def section_shift(block, distance):
    devices = range(lax.axis_size("section"))
    route = [(i - distance, i) for i in devices if i - distance in devices]
    return lax.ppermute(block, "section", route)


def pair_swap(block):
    return lax.ppermute(block, "dp", [(i, i ^ 1) for i in range(lax.axis_size("dp"))])


def chip_all_to_all(block):
    devices = lax.axis_size("dp")
    groups = [list(range(core, devices, 2)) for core in range(2)]
    return lax.all_to_all(
        block, "dp", split_axis=0, concat_axis=0, tiled=True, axis_index_groups=groups
    )


def rms_scale(values):
    return lax.rsqrt(jnp.mean(values * values, axis=-1, keepdims=True) + norm_eps)


def norm_backward(grad_normed, values, gain_row):
    inv_rms = rms_scale(values)
    weighted = grad_normed * gain_row
    grad_gain = jnp.sum(grad_normed * values * inv_rms, axis=0)
    grad_values = inv_rms * weighted - values * inv_rms**3 * jnp.mean(
        weighted * values, axis=-1, keepdims=True
    )
    return (grad_values, grad_gain)


def bucket_onehot():
    offset = np.arange(2 * SLOT) - SLOT
    bucket = np.sum(np.abs(offset)[:, None] >= np.array(bucket_edges), axis=1)
    bucket = bucket + BUCKETS // 2 * (offset > 0)
    return (bucket[:, None] == np.arange(BUCKETS)).astype(np.float32)


def same_sequence(lengths):
    bounds = jnp.cumsum(lengths, axis=-1)
    places = jnp.arange(SLOT, dtype=jnp.int32)
    owners = jnp.sum((places[:, None] >= bounds[:, None, :]).astype(jnp.int32), axis=-1)
    return (owners[:, :, None] == owners[:, None, :]).astype(f32)


def expert_places(route_ids, experts, capacity):
    names = jnp.arange(experts, dtype=jnp.int32)
    choose = (route_ids[:, None] == names).astype(jnp.int32)
    places = jnp.arange(SLOT, dtype=jnp.int32)
    earlier = (places[:, None] > places[None, :]).astype(bf16)
    before = dot(earlier, choose.astype(bf16)).astype(jnp.int32)
    rank_ids = jnp.sum(before * choose, axis=-1)
    return route_ids * capacity + rank_ids


def arrive(block):
    return (block, pair_swap(block))


def join_halves(own, other):
    return (own.astype(f32) + pair_swap(other).astype(f32)).astype(bf16)


def in_turns(streams):
    ends, values = [None] * len(streams), [None] * len(streams)
    travelling = None
    running = list(range(len(streams)))
    while running:
        for turn in list(running):
            try:
                block = streams[turn].send(values[turn])
            except StopIteration as stop:
                ends[turn] = stop.value
                running.remove(turn)
                if travelling is not None and running:
                    last, held = travelling
                    held, first = lax.optimization_barrier((held, ends[turn][0]))
                    ends[turn] = (first,) + ends[turn][1:]
                    values[last], travelling = held, None
                continue
            if travelling is not None:
                last, held = travelling
                held, block = lax.optimization_barrier((held, block))
                values[last] = held
            experts, width = lax.axis_size("dp") // 2, block.shape[-1]
            came = chip_all_to_all(block.reshape(experts, -1, width)).reshape(-1, width)
            values[turn], travelling = came, (turn, came)
    return ends


def dot_nt(lhs, rhs):
    return lax.dot_general(lhs, rhs, (((1,), (1,)), ((), ())), preferred_element_type=f32)


def dot_tn(lhs, rhs):
    return lax.dot_general(lhs, rhs, (((0,), (0,)), ((), ())), preferred_element_type=f32)


def lane_masks():
    low = lax.broadcasted_iota(jnp.int32, (1, 2 * HEAD_DIM), 1) < HEAD_DIM
    first = jnp.where(low, 1.0, 0.0)
    return (low, first.astype(bf16), (1.0 - first).astype(bf16))


def both_heads(slab, first, second):
    return jnp.concatenate([slab * first, slab * second], axis=0)


def own_lanes(low, stacked):
    return jnp.where(low, stacked[:SLOT], stacked[SLOT:])


def gelu_parts(hidden):
    rate, cubic = 0.7978845608028654, 0.044715
    squared = hidden * hidden
    bend = jnp.tanh(rate * hidden * (1.0 + cubic * squared))
    active = 0.5 * hidden * (1.0 + bend)
    slope = 0.5 * (1.0 + bend) + 0.5 * hidden * (1.0 - bend * bend) * rate * (
        1.0 + 3.0 * cubic * squared
    )
    return (active.astype(bf16), slope.astype(bf16))


def placing_of(targets, slots, dtype=bf16):
    return jnp.where(slots == targets, 1.0, 0.0).astype(dtype)


def load_weight(weight_ref, held_ref, sems):
    parts = [slice(0, 3 * D), slice(3 * D, 4 * D)]
    copies = [
        pltpu.make_async_copy(weight_ref.at[:, part], held_ref.at[:, part], sems.at[i])
        for i, part in enumerate(parts)
    ]
    return copies


def place_pieces(offsets_ref, piece_refs, held_ref, sems):
    copies = []
    for i, piece_ref in enumerate(piece_refs):
        rows = piece_ref.shape[0]
        start = pl.multiple_of(offsets_ref[i], 16) if len(piece_refs) > 1 else 0
        copies.append(
            pltpu.make_async_copy(piece_ref, held_ref.at[pl.ds(start, rows)], sems.at[i])
        )
    return copies


def front_kernel(experts, cotangent, pieces, *refs):
    if cotangent:
        first_ref, cotangent_ref, refs = refs[0], refs[1], refs[2:]
    inputs_ref, same_ref, route_ref, target_ref = refs[:4]
    refs = refs[4:]
    held_ref, sems = refs[-2:]
    if pieces:
        offsets_ref, spread_ref, owner_ref = refs[:3]
        piece_refs = refs[3 : 3 + pieces]
        refs = refs[3 + pieces :]
        weight_ref, gains_ref, router_ref, diagonals_ref = refs[7:11]
        copies = place_pieces(offsets_ref, piece_refs, held_ref, sems)
        for copy in copies:
            copy.start()
    else:
        weight_ref, gains_ref, router_ref, diagonals_ref = refs[:4]
        refs = refs[4:]
        copies = load_weight(weight_ref, held_ref, sems)
        for copy in copies:
            copy.start()
    (
        packed_ref,
        projected_ref,
        probs_ref,
        attended_ref,
        middle_ref,
        route_probs_ref,
        gate_ref,
    ) = refs[:7]
    inputs = inputs_ref[...].astype(f32)
    if cotangent:
        inputs = jnp.where(first_ref[0] > 0, cotangent_ref[...].astype(f32), inputs)
        refs[7][...] = inputs.astype(bf16)
    inv_rms = rms_scale(inputs)
    if pieces:
        for copy in copies:
            copy.wait()
        keep = pltpu.make_async_copy(held_ref.at[:, : 4 * D], weight_ref, sems.at[0])
        keep.start()
        extra = held_ref[:, 4 * D :].astype(f32).T
        gains_ref[...] = extra[0:8]
        router_ref[0:120] = extra[8:128].astype(bf16)
        router_ref[120:128] = jnp.zeros((8, D), bf16)
        diagonals_ref[...] = lax.dot_general(
            owner_ref[...] * extra[2:3],
            spread_ref[...],
            (((1,), (1,)), ((), ())),
            preferred_element_type=f32,
            precision=lax.Precision.HIGHEST,
        )
    else:
        copies[0].wait()
    normed = (inputs * inv_rms * gains_ref[0:1]).astype(bf16)
    projected_ref[...] = dot(normed, held_ref[:, : 3 * D]).astype(bf16)
    low, first, second = lane_masks()
    width = 2 * HEAD_DIM
    same = same_ref[...]
    same = jnp.concatenate([same, same], axis=0) > 0
    for pair in range(HEADS // 2):
        relative = jnp.concatenate(
            [
                pltpu.roll(
                    jnp.broadcast_to(diagonals_ref[head : head + 1], (SLOT, 2 * SLOT)),
                    SLOT,
                    1,
                    stride=1,
                    stride_axis=0,
                )[:, :SLOT]
                for head in (2 * pair, 2 * pair + 1)
            ],
            axis=0,
        )
        queries, keys, values = [
            projected_ref[:, part * D + pair * width : part * D + (pair + 1) * width]
            for part in range(3)
        ]
        scores = dot_nt(both_heads(queries, first, second), keys) * HEAD_DIM ** (-0.5) + relative
        scores = jnp.where(same, scores, masked_score)
        raised = jnp.exp(scores - jnp.max(scores, axis=-1, keepdims=True))
        probs = raised / jnp.sum(raised, axis=-1, keepdims=True)
        probs_ref[pair] = probs
        attended_ref[:, pair * width : (pair + 1) * width] = own_lanes(
            low, dot(probs.astype(bf16), values)
        ).astype(bf16)
    if not pieces:
        copies[1].wait()
    middle = inputs + dot(attended_ref[...], held_ref[:, 3 * D : 4 * D])
    middle_ref[...] = middle
    routed = (middle * rms_scale(middle) * gains_ref[1:2]).astype(bf16)
    logits = dot_nt(routed, router_ref[...])
    names = lax.broadcasted_iota(jnp.int32, (1, logits.shape[1]), 1)
    logits = jnp.where(names < experts, logits, masked_score)
    raised = jnp.exp(logits - jnp.max(logits, axis=-1, keepdims=True))
    route_probs = raised / jnp.sum(raised, axis=-1, keepdims=True)
    route_probs_ref[...] = route_probs
    gate = jnp.sum(jnp.where(names == route_ref[...], route_probs, 0.0), axis=-1, keepdims=True)
    gate_ref[...] = gate
    slots = lax.broadcasted_iota(jnp.int32, (packed_ref.shape[0], 1), 0)
    placing = placing_of(target_ref[...], slots)
    packed_ref[:, :D] = dot(placing, routed).astype(bf16)
    if cotangent:
        grad_result = (gate * cotangent_ref[...].astype(f32)).astype(bf16)
        packed_ref[:, D:] = dot(placing, grad_result).astype(bf16)
    if pieces:
        keep.wait()


def expert_kernel(forward, backward, keep, own_ref, other_ref, *refs):
    if backward and not forward:
        slope_ref, refs = refs[0], refs[1:]
    weight_in_ref, weight_out_ref, own_out_ref, other_out_ref = refs[:4]
    kept_refs, total_ref = refs[4:-1], refs[-1]
    grad_at = slice(D, 2 * D) if forward else slice(0, D)
    extent = own_ref.shape[0]
    step = pl.program_id(0)

    @pl.when(step == 0)
    def _():
        total_ref[...] = jnp.zeros_like(total_ref)

    rows = jnp.concatenate([own_ref[...], other_ref[...]], axis=0)
    if keep:
        kept_refs[-1][...] = rows[:, :D]
    if forward:
        active, slope = gelu_parts(dot(rows[:, :D], weight_in_ref[...]))
        total_ref[:, :D] += dot(active, weight_out_ref[...])
        if keep:
            kept_refs[0][...] = active
            kept_refs[1][...] = slope
    else:
        slope = slope_ref[...]
    if backward:
        grad_hidden = (
            dot_nt(rows[:, grad_at], weight_out_ref[...]) * slope.astype(f32)
        ).astype(bf16)
        total_ref[:, grad_at] += dot_nt(grad_hidden, weight_in_ref[...])
        if not forward:
            kept_refs[0][...] = grad_hidden

    @pl.when(step == pl.num_programs(0) - 1)
    def _():
        own_out_ref[...] = total_ref[:extent].astype(bf16)
        other_out_ref[...] = total_ref[extent:].astype(bf16)


def merge_back(
    grad_out, result, grad_sent, middle, gate, route_probs, route, router_ref, gains_ref
):
    grad_gate = jnp.sum(grad_out * result, axis=-1, keepdims=True)
    names = lax.broadcasted_iota(jnp.int32, (1, router_ref.shape[0]), 1)
    choose = jnp.where(names == route, 1.0, 0.0)
    grad_logits = (grad_gate * gate * (choose - route_probs)).astype(bf16)
    grad_routed = grad_sent + dot(grad_logits, router_ref[...])
    grad_middle_norm, grad_gain = norm_backward(grad_routed, middle, gains_ref[1:2])
    return (grad_out + grad_middle_norm, grad_gain, grad_logits)


def attention_back(
    grad_middle, inputs, gains_ref, held, projected_ref, probs_ref, grads_ref, table_ref
):
    weight_ref, copies = held
    copies[1].wait()
    grad_attended = dot_nt(grad_middle.astype(bf16), weight_ref[:, 3 * D :]).astype(bf16)
    low, first, second = lane_masks()
    width = 2 * HEAD_DIM
    scale_qk = HEAD_DIM ** (-0.5)
    places = [lax.broadcasted_iota(jnp.int32, (SLOT, SLOT), axis) for axis in range(2)]
    reverse = jnp.where(places[0] + places[1] == SLOT - 1, 1.0, 0.0).astype(bf16)
    for pair in range(HEADS // 2):
        columns = [
            slice(part * D + pair * width, part * D + (pair + 1) * width) for part in range(3)
        ]
        queries, keys, values = [projected_ref[:, part] for part in columns]
        grads = both_heads(grad_attended[:, pair * width : (pair + 1) * width], first, second)
        probs = probs_ref[pair]
        grad_probs = dot_nt(grads, values)
        grad_scores = (
            probs * (grad_probs - jnp.sum(probs * grad_probs, axis=-1, keepdims=True))
        ).astype(bf16)
        grads_ref[:, columns[0]] = (own_lanes(low, dot(grad_scores, keys)) * scale_qk).astype(bf16)
        grads_ref[:, columns[1]] = (
            dot_tn(grad_scores, both_heads(queries, first, second)) * scale_qk
        ).astype(bf16)
        grads_ref[:, columns[2]] = dot_tn(probs.astype(bf16), grads).astype(bf16)
        if table_ref is not None:
            for own in range(2):
                part = dot(reverse, grad_scores[own * SLOT : (own + 1) * SLOT])
                wide = jnp.concatenate([part, jnp.zeros_like(part)], axis=1)
                moved = pltpu.roll(wide, 1, 1, stride=1, stride_axis=0)
                head = 2 * pair + own
                table_ref[head : head + 1] = jnp.sum(moved, axis=0, keepdims=True)
    copies[0].wait()
    grad_normed = dot_nt(grads_ref[...], weight_ref[:, : 3 * D])
    grad_inputs_norm, grad_gain = norm_backward(grad_normed, inputs, gains_ref[0:1])
    return (grad_middle + grad_inputs_norm, grad_gain)


def start_weight(weight_ref, held_ref, sems):
    copies = load_weight(weight_ref, held_ref, sems)
    for copy in reversed(copies):
        copy.start()
    return (held_ref, copies)


def turn_kernel(
    cotangent_ref,
    returned_ref,
    target_ref,
    route_ref,
    inputs_ref,
    gains_ref,
    weight_ref,
    router_ref,
    projected_ref,
    probs_ref,
    middle_ref,
    route_probs_ref,
    gate_ref,
    outputs_ref,
    result_ref,
    grad_inputs_ref,
    grads_ref,
    held_ref,
    sems,
):
    held = start_weight(weight_ref, held_ref, sems)
    slots = lax.broadcasted_iota(jnp.int32, (1, returned_ref.shape[0]), 1)
    both = dot(placing_of(target_ref[...], slots), returned_ref[...])
    result = both[:, :D]
    result_ref[...] = result
    middle, gate = middle_ref[...], gate_ref[...]
    outputs_ref[...] = middle + gate * result
    grad_middle, _, _ = merge_back(
        cotangent_ref[...].astype(f32),
        result,
        both[:, D:],
        middle,
        gate,
        route_probs_ref[...],
        route_ref[...],
        router_ref,
        gains_ref,
    )
    grad_inputs, _ = attention_back(
        grad_middle,
        inputs_ref[...].astype(f32),
        gains_ref,
        held,
        projected_ref,
        probs_ref,
        grads_ref,
        None,
    )
    grad_inputs_ref[...] = grad_inputs.astype(bf16)


def back_kernel(
    experts,
    last,
    grad_out_ref,
    returned_ref,
    target_ref,
    route_ref,
    inputs_ref,
    gains_ref,
    weight_ref,
    router_ref,
    projected_ref,
    probs_ref,
    attended_ref,
    middle_ref,
    route_probs_ref,
    gate_ref,
    result_ref,
    *refs,
):
    if last:
        earlier = len(refs) - 11
        order_ref, earlier_refs, refs = refs[0], refs[1:earlier], refs[earlier:]
        quarter_refs, refs = refs[:4], refs[4:]
    else:
        grad_middle_ref, refs = refs[0], refs[1:]
    grad_inputs_ref, grads_ref, gain_ref, table_ref, small_ref, held_ref, sems = refs[-7:]
    held = start_weight(weight_ref, held_ref, sems)
    slots = lax.broadcasted_iota(jnp.int32, (1, returned_ref.shape[0]), 1)
    middle = middle_ref[...]
    grad_middle, grad_gain, grad_logits = merge_back(
        grad_out_ref[...].astype(f32),
        result_ref[...],
        dot(placing_of(target_ref[...], slots), returned_ref[...]),
        middle,
        gate_ref[...],
        route_probs_ref[...],
        route_ref[...],
        router_ref,
        gains_ref,
    )
    routed = (middle * rms_scale(middle) * gains_ref[1:2]).astype(bf16)
    small_ref[0:8] = jnp.broadcast_to(grad_gain[None], (8, D))
    small_ref[8:] = dot_tn(grad_logits, routed)[:experts]
    if last:
        half = len(earlier_refs) // 2
        attended = [ref[...] for ref in earlier_refs[:half]] + [attended_ref[...]]
        grads = [ref[...] for ref in earlier_refs[half:]] + [grad_middle]
        ordered = dot(jnp.concatenate(attended, axis=0), order_ref[...]).astype(bf16)
        total = dot_tn(ordered, jnp.concatenate(grads, axis=0).astype(bf16)).astype(bf16)
        for i, quarter_ref in enumerate(quarter_refs):
            quarter_ref[...] = total[i * D // 4 : (i + 1) * D // 4]
    else:
        grad_middle_ref[...] = grad_middle
    grad_inputs_ref[...], grad_gain = attention_back(
        grad_middle,
        inputs_ref[...].astype(f32),
        gains_ref,
        held,
        projected_ref,
        probs_ref,
        grads_ref,
        table_ref,
    )
    gain_ref[...] = grad_gain[None]


def qkv_grad_kernel(blocks, experts, order_ref, gains_ref, spread_ref, owner_ref, *refs):
    chunks, wide_ref = refs[-9:-1], refs[-1]
    inputs_refs, grads_refs, gain_refs, table_refs, small_refs = [
        refs[part * blocks : (part + 1) * blocks] for part in range(5)
    ]
    ordering = order_ref[...]
    inputs = jnp.concatenate([ref[...] for ref in inputs_refs], axis=0).astype(f32)
    normed = (inputs * rms_scale(inputs) * gains_ref[0:1]).astype(bf16)
    normed = dot(normed, ordering).astype(bf16)
    cut = chunks[0].shape[1]

    def keep(start, total):
        first = start if start < cut else start - cut
        columns = slice(first, first + total.shape[1])
        for i, quarter_ref in enumerate(chunks[:4] if start < cut else chunks[4:]):
            quarter_ref[:, columns] = total[i * D // 4 : (i + 1) * D // 4]

    for start, stop in ((0, D), (D, cut), (cut, 2 * D), (2 * D, 3 * D)):
        grads = jnp.concatenate([grads_ref[:, start:stop] for grads_ref in grads_refs], axis=0)
        keep(start, dot_tn(normed, grads).astype(bf16))
    diagonals = sum([table_ref[...] for table_ref in table_refs])
    entries = jnp.sum(
        owner_ref[...]
        * jnp.dot(
            diagonals,
            spread_ref[...],
            preferred_element_type=f32,
            precision=lax.Precision.HIGHEST,
        ),
        axis=0,
        keepdims=True,
    )
    small = sum([small_ref[...] for small_ref in small_refs])
    wide_ref[...] = jnp.zeros_like(wide_ref)
    wide_ref[0:1] = sum([gain_ref[...] for gain_ref in gain_refs])
    wide_ref[1:2] = small[0:1]
    wide_ref[2:3] = entries
    wide_ref[8 : 8 + experts] = small[8:]
    keep(3 * D, dot_tn(ordering, wide_ref[...].T.astype(bf16)).astype(bf16))


def kernel_call(kernel, name, out_shape, operands, micros, scratch=(), **blocks):
    return pl.pallas_call(
        kernel,
        out_shape=tuple(jax.ShapeDtypeStruct(*pair) for pair in out_shape),
        scratch_shapes=list(scratch),
        compiler_params=pltpu.CompilerParams(vmem_limit_bytes=62 * 1024 * 1024),
        cost_estimate=pl.CostEstimate(
            flops=int(micros * 5e8), bytes_accessed=int(micros * 3e6), transcendentals=0
        ),
        name=name,
        **blocks,
    )(*operands)


def whole_blocks(operands, apart):
    spaces = {"hbm": pl.ANY, "scalar": pltpu.SMEM, "vmem": pltpu.VMEM}
    return [pl.BlockSpec(memory_space=spaces[apart.get(i, "vmem")]) for i in range(len(operands))]


def front_call(inputs, own, dense, place):
    same_seq, route_column, _, target_row = place
    slots = 4 * SLOT // lax.axis_size("dp") * (lax.axis_size("dp") // 2)
    operands = () if own is None else own
    operands = operands + (inputs, same_seq, route_column, target_row)
    out_shape = (
        ((slots, D if own is None else 2 * D), bf16),
        ((SLOT, 3 * D), bf16),
        ((HEADS // 2, 2 * SLOT, SLOT), f32),
        ((SLOT, D), bf16),
        ((SLOT, D), f32),
        ((SLOT, 128), f32),
        ((SLOT, 1), f32),
    )
    pieces, width, out_apart = 0, 4 * D, {}
    if own is not None:
        out_shape = out_shape + (((SLOT, D), bf16),)
    if isinstance(dense, tuple):
        gains, weight, router, diagonals = dense
        apart = {len(operands): "hbm"} if own is None else {0: "scalar", len(operands): "hbm"}
        operands = operands + (weight, gains, router, diagonals)
    else:
        offsets, spread, owner, *held = dense
        pieces, width = len(held), 4 * D + 128
        first = len(operands)
        apart = {first: "scalar", **{first + 3 + i: "hbm" for i in range(pieces)}}
        operands = operands + tuple(dense)
        out_apart = {len(out_shape): "hbm"}
        out_shape = out_shape + (
            ((D, 4 * D), bf16),
            ((8, D), f32),
            ((128, D), bf16),
            ((HEADS, 2 * SLOT), f32),
        )
    return kernel_call(
        functools.partial(
            front_kernel, lax.axis_size("dp") // 2, own is not None, pieces
        ),
        "gathered_front" if pieces else "attention_front",
        out_shape,
        operands,
        5,
        (pltpu.VMEM((D, width), bf16), pltpu.SemaphoreType.DMA((max(2, pieces),))),
        in_specs=whole_blocks(operands, apart),
        out_specs=tuple(whole_blocks(out_shape, out_apart)),
    )


def expert_call(arrived, slope, experts_held, forward, backward, keep):
    own, other = arrived
    extent, units = own.shape[0], experts_held[0].shape[1]
    width = 2 * D if forward and backward else D
    kept = 0 if not keep else 2 if forward else 1
    row_kept = 1 if keep else 0
    step = 512
    replies = pl.BlockSpec((extent, width), lambda i: (0, 0))
    hidden = pl.BlockSpec((2 * extent, step), lambda i: (0, i))
    in_specs = [replies, replies] + ([] if slope is None else [hidden])
    in_specs = in_specs + [
        pl.BlockSpec((D, step), lambda i: (0, i)),
        pl.BlockSpec((step, D), lambda i: (i, 0)),
    ]
    return kernel_call(
        functools.partial(expert_kernel, forward, backward, keep),
        "experts_" + ("f" if forward else "") + ("b" if backward else ""),
        (((extent, width), bf16),) * 2
        + (((2 * extent, units), bf16),) * kept
        + (((2 * extent, D), bf16),) * row_kept,
        (own, other) + (() if slope is None else (slope,)) + experts_held,
        6 if width == D else 10,
        (pltpu.VMEM((2 * extent, width), f32),),
        grid=(units // step,),
        in_specs=in_specs,
        out_specs=(replies, replies)
        + (hidden,) * kept
        + (pl.BlockSpec((2 * extent, D), lambda i: (0, 0)),) * row_kept,
    )


def turn_call(cotangent, returned, inputs, kept, dense, place):
    gains, weight, router, _ = dense
    _, route_column, target_column, _ = place
    projected, probs, _, middle, route_probs, gate = kept
    rows = ((SLOT, D), f32)
    operands = (cotangent, returned, target_column, route_column, inputs, gains, weight)
    operands = operands + (router, projected, probs, middle, route_probs, gate)
    out_shape = (rows, rows, ((SLOT, D), bf16), ((SLOT, 3 * D), bf16))
    return kernel_call(
        turn_kernel,
        "turn_back",
        out_shape,
        operands,
        7,
        (pltpu.VMEM((D, 4 * D), bf16), pltpu.SemaphoreType.DMA((2,))),
        in_specs=whole_blocks(operands, {6: "hbm"}),
        out_specs=tuple(whole_blocks(out_shape, {})),
    )


def back_call(grad_out, returned, inputs, kept, result, dense, place, earlier):
    gains, weight, router, _ = dense
    _, route_column, target_column, _ = place
    experts = lax.axis_size("dp") // 2
    operands = (grad_out, returned, target_column, route_column, inputs, gains, weight, router)
    operands = operands + tuple(kept) + (result,) + earlier
    out_shape = (
        ((SLOT, D), f32),
        ((SLOT, 3 * D), bf16),
        ((1, D), f32),
        ((HEADS, 2 * SLOT), f32),
        ((8 + experts, D), f32),
    )
    first = (((D // 4, D), bf16),) * 4 if earlier else (((SLOT, D), f32),)
    out_shape = first + out_shape
    return kernel_call(
        functools.partial(back_kernel, experts, len(earlier) > 0),
        "back_and_out_gradient" if earlier else "back",
        out_shape,
        operands,
        9,
        (pltpu.VMEM((D, 4 * D), bf16), pltpu.SemaphoreType.DMA((2,))),
        in_specs=whole_blocks(operands, {6: "hbm"}),
        out_specs=tuple(whole_blocks(out_shape, {})),
    )


def pack_dense(gains, qkv, out, router, table):
    rows, kind = qkv.shape[0], qkv.dtype
    blank = jnp.zeros((rows, 128 - 8 - router.shape[1]), kind)
    entries = jnp.pad(table, (0, rows - table.shape[0]))[:, None]
    return jnp.concatenate(
        [qkv, out, gains.T, entries, jnp.zeros((rows, 5), kind), router, blank], axis=1
    )


def gather_pieces(piece, early):
    devices, extent = lax.axis_size("dp"), piece.shape[0]
    if devices != 16:
        gathered = lax.all_gather(piece, "dp", axis=0, tiled=True)
        return (jnp.zeros((1,), jnp.int32), [gathered], early)
    me = lax.axis_index("dp")

    def send(block, distance):
        return lax.ppermute(block, "dp", [(i, i ^ distance) for i in range(devices)])

    near, far = send(piece, 4), send(piece, 12)
    far, early = lax.optimization_barrier((far, early))
    pieces, owners = [], []
    for distance, block in ((0, piece), (4, near), (12, far), (8, send(far, 4))):
        for other_y, column in enumerate((block, send(block, 2))):
            for other_core, held in enumerate((column, send(column, 1))):
                pieces.append(held)
                owners.append(me ^ (distance + 2 * other_y + other_core))
    return (jnp.stack(owners).astype(jnp.int32) * extent, pieces, early)


def swap(block, distance):
    route = [(i, i ^ distance) for i in range(lax.axis_size("dp"))]
    return lax.ppermute(block, "dp", route)


def sum_of_four(near, far, near_there, far_there):
    far = (far.astype(f32) + swap(far_there, 1).astype(f32)).astype(bf16)
    near = near.astype(f32) + swap(near_there, 1).astype(f32)
    return (near + swap(far, 2).astype(f32)).astype(bf16)


def total_of(summed):
    devices = lax.axis_size("dp")
    groups = [list(range(first, devices, 4)) for first in range(4)]
    came = lax.all_to_all(
        summed.reshape(devices // 4, D // devices, -1),
        "dp",
        split_axis=0,
        concat_axis=0,
        tiled=True,
        axis_index_groups=groups,
    )
    return jnp.sum(came.astype(f32), axis=0)


def feature_order(devices):
    extent = D // devices
    places = np.arange(D)
    quarter, rest = places // (D // 4), places % (D // 4)
    place = (quarter // 2 + 2 * (quarter % 2)) ^ (lax.axis_index("dp") % 4)
    features = (4 * (rest // extent) + place) * extent + rest % extent
    return (jnp.arange(D)[:, None] == features[None]).astype(bf16)


def table_places(onehot, devices):
    extent, used = D // devices, BUCKETS * HEADS // devices
    places = np.arange(D)
    held = places % extent < used
    entry = np.where(held, places // extent * used + places % extent, 0)
    spread = onehot[:, entry // HEADS] * held
    owner = entry % HEADS == np.arange(HEADS)[:, None]
    return (spread.astype(np.float32), owner.astype(np.float32))


def shards(
    edge_rows,
    lengths,
    routes,
    norm_gains,
    qkv_weight,
    out_weight,
    router_weight,
    bias_table,
    expert_in,
    expert_out,
):
    devices = lax.axis_size("dp")
    experts = devices // 2
    first_section = lax.axis_index("section") == 0
    onehot = bucket_onehot()
    experts_held = (expert_in[0], expert_out[0])
    spread, owner = table_places(onehot, devices)
    same_seq = same_sequence(lengths)
    capacity = 4 * SLOT // devices
    blocks = range(edge_rows.shape[1] // SLOT)
    local_rows = [edge_rows[0, b * SLOT : (b + 1) * SLOT] for b in blocks]
    slot_ids = jnp.arange(experts * capacity, dtype=jnp.int32)
    places, placings = [], []
    for b in blocks:
        route_ids = routes[0, b * SLOT : (b + 1) * SLOT, 0]
        targets = expert_places(route_ids, experts, capacity)
        places.append((same_seq[b], route_ids[:, None], targets[:, None], targets[None, :]))
        placings.append((targets[:, None] == slot_ids[None]).astype(bf16))
    early = (local_rows, places, placings, feature_order(devices))
    offsets, pieces, early = gather_pieces(
        pack_dense(norm_gains[0], qkv_weight[0], out_weight[0], router_weight[0], bias_table[0]),
        early,
    )
    local_rows, places, placings, order = early
    gathering = [offsets, jnp.asarray(spread), jnp.asarray(owner), *pieces]
    dense = None
    first_flag = first_section.astype(jnp.int32).reshape(1)

    def stream(b):
        nonlocal dense
        place, placing, local = places[b], placings[b], local_rows[b]
        packed, _, _, _, middle, _, gate, *made = front_call(
            local, None, dense or gathering, place
        )
        if dense is None:
            weight, *small = made
            dense = (small[0], weight, small[1], small[2])
        came = yield packed
        own, other = expert_call(arrive(came), None, experts_held, True, False, False)
        came = yield join_halves(own, other)
        outputs = middle + gate * dot(placing, came)
        carried = section_shift(outputs.astype(bf16), 1)
        packed, *kept, inputs = front_call(carried, (first_flag, local), dense, place)
        came = yield packed
        own, other, active, slope, arrived = expert_call(
            arrive(came), None, experts_held, True, True, True
        )
        came = yield join_halves(own, other)
        outputs, result, grad_inputs, _ = turn_call(local, came, inputs, kept, dense, place)
        carried = section_shift(grad_inputs, -1)
        grad_out = jnp.where(first_section, carried, local)

        grad_result = (kept[5] * grad_out).astype(bf16)
        came = yield jnp.einsum(
            "ts,td->sd", placing, grad_result, preferred_element_type=f32
        ).astype(bf16)
        own, other, grad_hidden, grad_rows = expert_call(
            arrive(came), slope, experts_held, False, True, True
        )
        came = yield join_halves(own, other)
        rest = (inputs, outputs, kept, (arrived, active, grad_rows, grad_hidden))
        if b == len(blocks) - 1:
            return (came, rest, (grad_out, result))
        return (back_call(grad_out, came, inputs, kept, result, dense, place, ()), rest)

    ends = in_turns([stream(b) for b in blocks])
    inputs, outputs, kept, expert_rows = zip(*[end[1] for end in ends])
    backs = [end[0] for end in ends[:-1]]
    earlier = (order, *[now[2] for now in kept[:-1]], *[back[0] for back in backs])
    returned, _, (grad_out, result) = ends[-1]
    made = back_call(
        grad_out, returned, inputs[-1], kept[-1], result, dense, places[-1], earlier
    )
    back = made[4:]
    grad_first = sum_of_four(*made[:4])
    grad_inputs, grads, gain_ones, tables, smalls = zip(*[now[1:] for now in backs], back)
    cut = D + D // 2
    quarters = kernel_call(
        functools.partial(qkv_grad_kernel, len(blocks), experts),
        "qkv_gradient",
        (((D // 4, cut), bf16),) * 4 + (((D // 4, 3 * D - cut + 128), bf16),) * 4,
        (order, dense[0], spread, owner)
        + (*inputs, *grads, *gain_ones, *tables, *smalls),
        4,
        (pltpu.VMEM((128, D), f32),),
    )
    grad_qkv = sum_of_four(*quarters[:4])
    grad_last = sum_of_four(*quarters[4:])
    total_out = total_of(grad_first)
    total_out, grad_qkv = lax.optimization_barrier((total_out, grad_qkv))
    total_qkv = total_of(grad_qkv)
    total_qkv, grad_last = lax.optimization_barrier((total_qkv, grad_last))
    total_last = total_of(grad_last)
    arrived, active, grad_rows, grad_hidden = zip(*expert_rows)
    grad_expert_out = jnp.einsum(
        "rf,rd->fd",
        jnp.concatenate(active),
        jnp.concatenate(grad_rows),
        preferred_element_type=f32,
    )
    grad_expert_in = jnp.einsum(
        "rd,rf->df",
        jnp.concatenate(arrived),
        jnp.concatenate(grad_hidden),
        preferred_element_type=f32,
    )
    edge_results = jnp.concatenate(
        [jnp.where(first_section, grad_inputs[b], outputs[b]) for b in blocks]
    )
    extra = total_last[:, 3 * D - cut :]
    grad_qkv = jnp.concatenate([total_qkv, total_last[:, : 3 * D - cut]], axis=1)
    return (
        edge_results[None],
        extra[None, :, 0:2].swapaxes(1, 2),
        grad_qkv[None],
        total_out[None],
        extra[None, :, 8 : 8 + experts],
        extra[None, : BUCKETS * HEADS // devices, 2],
        grad_expert_in[None],
        grad_expert_out[None],
    )


def solution(mesh):
    return jax.shard_map(
        shards,
        mesh=mesh,
        in_specs=(
            P("section", "dp", None),
            P("dp", None),
            P("section", "dp", None),
            P("section", None, "dp"),
            P("section", "dp", None),
            P("section", "dp", None),
            P("section", "dp", None),
            P("section", "dp"),
            P("section", None, "dp"),
            P("section", "dp", None),
        ),
        out_specs=(
            P("section", "dp", None),
            P("section", None, "dp"),
            P("section", "dp", None),
            P("section", "dp", None),
            P("section", "dp", None),
            P("section", "dp"),
            P("section", None, "dp"),
            P("section", "dp", None),
        ),
        check_vma=False,
    )
```

```python
import functools

import jax
import jax.numpy as jnp
import numpy as np
from jax import lax
from jax.experimental import pallas as pl
from jax.experimental.pallas import tpu as pltpu
from jax.sharding import PartitionSpec as P

D = 768
HEADS = 12
HEAD_DIM = 64
BUCKETS = 32
SLOT = 128


norm_eps = 1e-06
masked_score = -1e30
bucket_edges = (1, 2, 3, 4, 5, 6, 7, 8, 12, 16, 23, 32, 46, 64, 91)
bf16 = jnp.bfloat16
f32 = jnp.float32


def dot(lhs, rhs):
    return jnp.dot(lhs, rhs, preferred_element_type=f32)


def section_shift(block, distance):
    devices = range(lax.axis_size("section"))
    route = [(i - distance, i) for i in devices if i - distance in devices]
    return lax.ppermute(block, "section", route)


def pair_swap(block):
    return lax.ppermute(block, "dp", [(i, i ^ 1) for i in range(lax.axis_size("dp"))])


def chip_all_to_all(block):
    devices = lax.axis_size("dp")
    groups = [list(range(core, devices, 2)) for core in range(2)]
    return lax.all_to_all(
        block, "dp", split_axis=0, concat_axis=0, tiled=True, axis_index_groups=groups
    )


def rms_scale(values):
    return lax.rsqrt(jnp.mean(values * values, axis=-1, keepdims=True) + norm_eps)


def norm_backward(grad_normed, values, gain_row):
    inv_rms = rms_scale(values)
    weighted = grad_normed * gain_row
    grad_gain = jnp.sum(grad_normed * values * inv_rms, axis=0)
    grad_values = inv_rms * weighted - values * inv_rms**3 * jnp.mean(
        weighted * values, axis=-1, keepdims=True
    )
    return (grad_values, grad_gain)


def bucket_onehot():
    offset = np.arange(2 * SLOT) - SLOT
    bucket = np.sum(np.abs(offset)[:, None] >= np.array(bucket_edges), axis=1)
    bucket = bucket + BUCKETS // 2 * (offset > 0)
    return (bucket[:, None] == np.arange(BUCKETS)).astype(np.float32)


def same_sequence(lengths):
    bounds = jnp.cumsum(lengths, axis=-1)
    places = jnp.arange(SLOT, dtype=jnp.int32)
    owners = jnp.sum((places[:, None] >= bounds[:, None, :]).astype(jnp.int32), axis=-1)
    return (owners[:, :, None] == owners[:, None, :]).astype(f32)


def expert_places(route_ids, experts, capacity):
    names = jnp.arange(experts, dtype=jnp.int32)
    choose = (route_ids[:, None] == names).astype(jnp.int32)
    places = jnp.arange(SLOT, dtype=jnp.int32)
    earlier = (places[:, None] > places[None, :]).astype(bf16)
    before = dot(earlier, choose.astype(bf16)).astype(jnp.int32)
    rank_ids = jnp.sum(before * choose, axis=-1)
    return route_ids * capacity + rank_ids


def arrive(block):
    return (block, pair_swap(block))


def join_halves(own, other):
    return (own.astype(f32) + pair_swap(other).astype(f32)).astype(bf16)


def in_turns(streams):
    ends, values = [None] * len(streams), [None] * len(streams)
    travelling = None
    running = list(range(len(streams)))
    while running:
        for turn in list(running):
            try:
                block = streams[turn].send(values[turn])
            except StopIteration as stop:
                ends[turn] = stop.value
                running.remove(turn)
                if travelling is not None and running:
                    last, held = travelling
                    held, first = lax.optimization_barrier((held, ends[turn][0]))
                    ends[turn] = (first,) + ends[turn][1:]
                    values[last], travelling = held, None
                continue
            if travelling is not None:
                last, held = travelling
                held, block = lax.optimization_barrier((held, block))
                values[last] = held
            experts, width = lax.axis_size("dp") // 2, block.shape[-1]
            came = chip_all_to_all(block.reshape(experts, -1, width)).reshape(-1, width)
            values[turn], travelling = came, (turn, came)
    return ends


def dot_nt(lhs, rhs):
    return lax.dot_general(lhs, rhs, (((1,), (1,)), ((), ())), preferred_element_type=f32)


def dot_tn(lhs, rhs):
    return lax.dot_general(lhs, rhs, (((0,), (0,)), ((), ())), preferred_element_type=f32)


def lane_masks():
    low = lax.broadcasted_iota(jnp.int32, (1, 2 * HEAD_DIM), 1) < HEAD_DIM
    first = jnp.where(low, 1.0, 0.0)
    return (low, first.astype(bf16), (1.0 - first).astype(bf16))


def both_heads(slab, first, second):
    return jnp.concatenate([slab * first, slab * second], axis=0)


def own_lanes(low, stacked):
    return jnp.where(low, stacked[:SLOT], stacked[SLOT:])


def gelu_parts(hidden):
    rate, cubic = 0.7978845608028654, 0.044715
    squared = hidden * hidden
    bend = jnp.tanh(rate * hidden * (1.0 + cubic * squared))
    active = 0.5 * hidden * (1.0 + bend)
    slope = 0.5 * (1.0 + bend) + 0.5 * hidden * (1.0 - bend * bend) * rate * (
        1.0 + 3.0 * cubic * squared
    )
    return (active.astype(bf16), slope.astype(bf16))


def placing_of(targets, slots, dtype=bf16):
    return jnp.where(slots == targets, 1.0, 0.0).astype(dtype)


def load_weight(weight_ref, held_ref, sems):
    parts = [slice(0, 3 * D), slice(3 * D, 4 * D)]
    copies = [
        pltpu.make_async_copy(weight_ref.at[:, part], held_ref.at[:, part], sems.at[i])
        for i, part in enumerate(parts)
    ]
    return copies


def place_pieces(offsets_ref, piece_refs, held_ref, sems):
    copies = []
    for i, piece_ref in enumerate(piece_refs):
        rows = piece_ref.shape[0]
        start = pl.multiple_of(offsets_ref[i], 16) if len(piece_refs) > 1 else 0
        copies.append(
            pltpu.make_async_copy(piece_ref, held_ref.at[pl.ds(start, rows)], sems.at[i])
        )
    return copies


def front_kernel(experts, cotangent, pieces, *refs):
    if cotangent:
        first_ref, cotangent_ref, refs = refs[0], refs[1], refs[2:]
    inputs_ref, same_ref, choose_ref, target_ref = refs[:4]
    refs = refs[4:]
    held_ref, sems = refs[-2:]
    if pieces:
        offsets_ref, spread_ref, owner_ref = refs[:3]
        piece_refs = refs[3 : 3 + pieces]
        refs = refs[3 + pieces :]
        weight_ref, gains_ref, router_ref, diagonals_ref = refs[7:11]
        copies = place_pieces(offsets_ref, piece_refs, held_ref, sems)
        for copy in copies:
            copy.start()
    else:
        weight_ref, gains_ref, router_ref, diagonals_ref = refs[:4]
        refs = refs[4:]
        copies = load_weight(weight_ref, held_ref, sems)
        for copy in copies:
            copy.start()
    (
        packed_ref,
        projected_ref,
        probs_ref,
        attended_ref,
        middle_ref,
        route_probs_ref,
        gate_ref,
    ) = refs[:7]
    inputs = inputs_ref[...].astype(f32)
    if cotangent:
        inputs = jnp.where(first_ref[0] > 0, cotangent_ref[...].astype(f32), inputs)
        refs[7][...] = inputs.astype(bf16)
    inv_rms = rms_scale(inputs)
    if pieces:
        for copy in copies:
            copy.wait()
        keep = pltpu.make_async_copy(held_ref.at[:, : 4 * D], weight_ref, sems.at[0])
        keep.start()
        extra = held_ref[:, 4 * D :].astype(f32).T
        gains_ref[...] = extra[0:8]
        router_ref[0:120] = extra[8:128].astype(bf16)
        router_ref[120:128] = jnp.zeros((8, D), bf16)
        diagonals_ref[...] = lax.dot_general(
            owner_ref[...] * extra[2:3],
            spread_ref[...],
            (((1,), (1,)), ((), ())),
            preferred_element_type=f32,
            precision=lax.Precision.HIGHEST,
        )
    else:
        copies[0].wait()
    normed = (inputs * inv_rms * gains_ref[0:1]).astype(bf16)
    projected_ref[...] = dot(normed, held_ref[:, : 3 * D]).astype(bf16)
    low, first, second = lane_masks()
    width = 2 * HEAD_DIM
    same = same_ref[...]
    same = jnp.concatenate([same, same], axis=0) > 0
    for pair in range(HEADS // 2):
        relative = jnp.concatenate(
            [
                pltpu.roll(
                    jnp.broadcast_to(diagonals_ref[head : head + 1], (SLOT, 2 * SLOT)),
                    SLOT,
                    1,
                    stride=1,
                    stride_axis=0,
                )[:, :SLOT]
                for head in (2 * pair, 2 * pair + 1)
            ],
            axis=0,
        )
        queries, keys, values = [
            projected_ref[:, part * D + pair * width : part * D + (pair + 1) * width]
            for part in range(3)
        ]
        scores = dot_nt(both_heads(queries, first, second), keys) * HEAD_DIM ** (-0.5) + relative
        scores = jnp.where(same, scores, masked_score)
        raised = jnp.exp(scores - jnp.max(scores, axis=-1, keepdims=True))
        probs = raised / jnp.sum(raised, axis=-1, keepdims=True)
        probs_ref[pair] = probs
        attended_ref[:, pair * width : (pair + 1) * width] = own_lanes(
            low, dot(probs.astype(bf16), values)
        ).astype(bf16)
    if not pieces:
        copies[1].wait()
    middle = inputs + dot(attended_ref[...], held_ref[:, 3 * D : 4 * D])
    middle_ref[...] = middle
    routed = (middle * rms_scale(middle) * gains_ref[1:2]).astype(bf16)
    logits = dot_nt(routed, router_ref[...])
    names = lax.broadcasted_iota(jnp.int32, (1, logits.shape[1]), 1)
    logits = jnp.where(names < experts, logits, masked_score)
    raised = jnp.exp(logits - jnp.max(logits, axis=-1, keepdims=True))
    route_probs = raised / jnp.sum(raised, axis=-1, keepdims=True)
    route_probs_ref[...] = route_probs
    gate = jnp.sum(choose_ref[...] * route_probs, axis=-1, keepdims=True)
    gate_ref[...] = gate
    slots = lax.broadcasted_iota(jnp.int32, (packed_ref.shape[0], 1), 0)
    placing = placing_of(target_ref[...], slots)
    packed_ref[:, :D] = dot(placing, routed).astype(bf16)
    if cotangent:
        grad_result = (gate * cotangent_ref[...].astype(f32)).astype(bf16)
        packed_ref[:, D:] = dot(placing, grad_result).astype(bf16)
    if pieces:
        keep.wait()


def expert_kernel(forward, backward, keep, own_ref, other_ref, *refs):
    if backward and not forward:
        slope_ref, refs = refs[0], refs[1:]
    weight_in_ref, weight_out_ref, own_out_ref, other_out_ref = refs[:4]
    kept_refs, total_ref = refs[4:-1], refs[-1]
    grad_at = slice(D, 2 * D) if forward else slice(0, D)
    extent = own_ref.shape[0]
    step = pl.program_id(0)

    @pl.when(step == 0)
    def _():
        total_ref[...] = jnp.zeros_like(total_ref)

    rows = jnp.concatenate([own_ref[...], other_ref[...]], axis=0)
    if keep:
        kept_refs[-1][...] = rows[:, :D]
    if forward:
        active, slope = gelu_parts(dot(rows[:, :D], weight_in_ref[...]))
        total_ref[:, :D] += dot(active, weight_out_ref[...])
        if keep:
            kept_refs[0][...] = active
            kept_refs[1][...] = slope
    else:
        slope = slope_ref[...]
    if backward:
        grad_hidden = (
            dot_nt(rows[:, grad_at], weight_out_ref[...]) * slope.astype(f32)
        ).astype(bf16)
        total_ref[:, grad_at] += dot_nt(grad_hidden, weight_in_ref[...])
        if not forward:
            kept_refs[0][...] = grad_hidden

    @pl.when(step == pl.num_programs(0) - 1)
    def _():
        own_out_ref[...] = total_ref[:extent].astype(bf16)
        other_out_ref[...] = total_ref[extent:].astype(bf16)


def merge_back(
    grad_out, result, grad_sent, middle, gate, route_probs, choose, router_ref, gains_ref
):
    grad_gate = jnp.sum(grad_out * result, axis=-1, keepdims=True)
    grad_logits = (grad_gate * gate * (choose - route_probs)).astype(bf16)
    grad_routed = grad_sent + dot(grad_logits, router_ref[...])
    grad_middle_norm, grad_gain = norm_backward(grad_routed, middle, gains_ref[1:2])
    return (grad_out + grad_middle_norm, grad_gain, grad_logits)


def attention_back(
    grad_middle, inputs, gains_ref, held, projected_ref, probs_ref, grads_ref, table_ref
):
    weight_ref, copies = held
    copies[1].wait()
    grad_attended = dot_nt(grad_middle.astype(bf16), weight_ref[:, 3 * D :]).astype(bf16)
    low, first, second = lane_masks()
    width = 2 * HEAD_DIM
    scale_qk = HEAD_DIM ** (-0.5)
    places = [lax.broadcasted_iota(jnp.int32, (SLOT, SLOT), axis) for axis in range(2)]
    reverse = jnp.where(places[0] + places[1] == SLOT - 1, 1.0, 0.0).astype(bf16)
    for pair in range(HEADS // 2):
        columns = [
            slice(part * D + pair * width, part * D + (pair + 1) * width) for part in range(3)
        ]
        queries, keys, values = [projected_ref[:, part] for part in columns]
        grads = both_heads(grad_attended[:, pair * width : (pair + 1) * width], first, second)
        probs = probs_ref[pair]
        grad_probs = dot_nt(grads, values)
        grad_scores = (
            probs * (grad_probs - jnp.sum(probs * grad_probs, axis=-1, keepdims=True))
        ).astype(bf16)
        grads_ref[:, columns[0]] = (own_lanes(low, dot(grad_scores, keys)) * scale_qk).astype(bf16)
        grads_ref[:, columns[1]] = (
            dot_tn(grad_scores, both_heads(queries, first, second)) * scale_qk
        ).astype(bf16)
        grads_ref[:, columns[2]] = dot_tn(probs.astype(bf16), grads).astype(bf16)
        if table_ref is not None:
            for own in range(2):
                part = dot(reverse, grad_scores[own * SLOT : (own + 1) * SLOT])
                wide = jnp.concatenate([part, jnp.zeros_like(part)], axis=1)
                moved = pltpu.roll(wide, 1, 1, stride=1, stride_axis=0)
                head = 2 * pair + own
                table_ref[head : head + 1] = jnp.sum(moved, axis=0, keepdims=True)
    copies[0].wait()
    grad_normed = dot_nt(grads_ref[...], weight_ref[:, : 3 * D])
    grad_inputs_norm, grad_gain = norm_backward(grad_normed, inputs, gains_ref[0:1])
    return (grad_middle + grad_inputs_norm, grad_gain)


def start_weight(weight_ref, held_ref, sems):
    copies = load_weight(weight_ref, held_ref, sems)
    for copy in reversed(copies):
        copy.start()
    return (held_ref, copies)


def turn_kernel(
    cotangent_ref,
    returned_ref,
    placing_ref,
    choose_ref,
    inputs_ref,
    gains_ref,
    weight_ref,
    router_ref,
    projected_ref,
    probs_ref,
    middle_ref,
    route_probs_ref,
    gate_ref,
    outputs_ref,
    result_ref,
    grad_inputs_ref,
    grads_ref,
    held_ref,
    sems,
):
    held = start_weight(weight_ref, held_ref, sems)
    both = dot(placing_ref[...], returned_ref[...])
    result = both[:, :D]
    result_ref[...] = result
    middle, gate = middle_ref[...], gate_ref[...]
    outputs_ref[...] = middle + gate * result
    grad_middle, _, _ = merge_back(
        cotangent_ref[...].astype(f32),
        result,
        both[:, D:],
        middle,
        gate,
        route_probs_ref[...],
        choose_ref[...],
        router_ref,
        gains_ref,
    )
    grad_inputs, _ = attention_back(
        grad_middle,
        inputs_ref[...].astype(f32),
        gains_ref,
        held,
        projected_ref,
        probs_ref,
        grads_ref,
        None,
    )
    grad_inputs_ref[...] = grad_inputs.astype(bf16)


def back_kernel(
    experts,
    last,
    grad_out_ref,
    returned_ref,
    placing_ref,
    choose_ref,
    inputs_ref,
    gains_ref,
    weight_ref,
    router_ref,
    projected_ref,
    probs_ref,
    attended_ref,
    middle_ref,
    route_probs_ref,
    gate_ref,
    result_ref,
    *refs,
):
    if last:
        earlier = len(refs) - 11
        order_ref, earlier_refs, refs = refs[0], refs[1:earlier], refs[earlier:]
        quarter_refs, refs = refs[:4], refs[4:]
    else:
        grad_middle_ref, refs = refs[0], refs[1:]
    grad_inputs_ref, grads_ref, gain_ref, table_ref, small_ref, held_ref, sems = refs[-7:]
    held = start_weight(weight_ref, held_ref, sems)
    middle = middle_ref[...]
    grad_middle, grad_gain, grad_logits = merge_back(
        grad_out_ref[...].astype(f32),
        result_ref[...],
        dot(placing_ref[...], returned_ref[...]),
        middle,
        gate_ref[...],
        route_probs_ref[...],
        choose_ref[...],
        router_ref,
        gains_ref,
    )
    routed = (middle * rms_scale(middle) * gains_ref[1:2]).astype(bf16)
    small_ref[0:8] = jnp.broadcast_to(grad_gain[None], (8, D))
    small_ref[8:] = dot_tn(grad_logits, routed)[:experts]
    if last:
        half = len(earlier_refs) // 2
        attended = [ref[...] for ref in earlier_refs[:half]] + [attended_ref[...]]
        grads = [ref[...] for ref in earlier_refs[half:]] + [grad_middle]
        ordered = dot(jnp.concatenate(attended, axis=0), order_ref[...]).astype(bf16)
        total = dot_tn(ordered, jnp.concatenate(grads, axis=0).astype(bf16)).astype(bf16)
        for i, quarter_ref in enumerate(quarter_refs):
            quarter_ref[...] = total[i * D // 4 : (i + 1) * D // 4]
    else:
        grad_middle_ref[...] = grad_middle
    grad_inputs_ref[...], grad_gain = attention_back(
        grad_middle,
        inputs_ref[...].astype(f32),
        gains_ref,
        held,
        projected_ref,
        probs_ref,
        grads_ref,
        table_ref,
    )
    gain_ref[...] = grad_gain[None]


def qkv_grad_kernel(blocks, experts, order_ref, gains_ref, spread_ref, owner_ref, *refs):
    chunks, wide_ref = refs[-9:-1], refs[-1]
    inputs_refs, grads_refs, gain_refs, table_refs, small_refs = [
        refs[part * blocks : (part + 1) * blocks] for part in range(5)
    ]
    ordering = order_ref[...]
    inputs = jnp.concatenate([ref[...] for ref in inputs_refs], axis=0).astype(f32)
    normed = (inputs * rms_scale(inputs) * gains_ref[0:1]).astype(bf16)
    normed = dot(normed, ordering).astype(bf16)
    cut = chunks[0].shape[1]

    def keep(start, total):
        first = start if start < cut else start - cut
        columns = slice(first, first + total.shape[1])
        for i, quarter_ref in enumerate(chunks[:4] if start < cut else chunks[4:]):
            quarter_ref[:, columns] = total[i * D // 4 : (i + 1) * D // 4]

    for start, stop in ((0, D), (D, cut), (cut, 2 * D), (2 * D, 3 * D)):
        grads = jnp.concatenate([grads_ref[:, start:stop] for grads_ref in grads_refs], axis=0)
        keep(start, dot_tn(normed, grads).astype(bf16))
    diagonals = sum([table_ref[...] for table_ref in table_refs])
    entries = jnp.sum(
        owner_ref[...]
        * jnp.dot(
            diagonals,
            spread_ref[...],
            preferred_element_type=f32,
            precision=lax.Precision.HIGHEST,
        ),
        axis=0,
        keepdims=True,
    )
    small = sum([small_ref[...] for small_ref in small_refs])
    wide_ref[...] = jnp.zeros_like(wide_ref)
    wide_ref[0:1] = sum([gain_ref[...] for gain_ref in gain_refs])
    wide_ref[1:2] = small[0:1]
    wide_ref[2:3] = entries
    wide_ref[8 : 8 + experts] = small[8:]
    keep(3 * D, dot_tn(ordering, wide_ref[...].T.astype(bf16)).astype(bf16))


def kernel_call(kernel, name, out_shape, operands, micros, scratch=(), grant=62, **blocks):
    return pl.pallas_call(
        kernel,
        out_shape=tuple(jax.ShapeDtypeStruct(*pair) for pair in out_shape),
        scratch_shapes=list(scratch),
        compiler_params=pltpu.CompilerParams(vmem_limit_bytes=grant * 1024 * 1024),
        cost_estimate=pl.CostEstimate(
            flops=int(micros * 5e8), bytes_accessed=int(micros * 3e6), transcendentals=0
        ),
        name=name,
        **blocks,
    )(*operands)


def whole_blocks(operands, apart):
    spaces = {"hbm": pl.ANY, "scalar": pltpu.SMEM, "vmem": pltpu.VMEM}
    return [pl.BlockSpec(memory_space=spaces[apart.get(i, "vmem")]) for i in range(len(operands))]


def front_call(inputs, own, dense, place):
    same_seq, choose, _, target_row = place
    slots = 4 * SLOT // lax.axis_size("dp") * (lax.axis_size("dp") // 2)
    operands = () if own is None else own
    operands = operands + (inputs, same_seq, choose, target_row)
    out_shape = (
        ((slots, D if own is None else 2 * D), bf16),
        ((SLOT, 3 * D), bf16),
        ((HEADS // 2, 2 * SLOT, SLOT), f32),
        ((SLOT, D), bf16),
        ((SLOT, D), f32),
        ((SLOT, 128), f32),
        ((SLOT, 1), f32),
    )
    pieces, width, out_apart = 0, 4 * D, {}
    if own is not None:
        out_shape = out_shape + (((SLOT, D), bf16),)
    if isinstance(dense, tuple):
        gains, weight, router, diagonals = dense
        apart = {len(operands): "hbm"} if own is None else {0: "scalar", len(operands): "hbm"}
        operands = operands + (weight, gains, router, diagonals)
    else:
        offsets, spread, owner, *held = dense
        pieces, width = len(held), 4 * D + 128
        first = len(operands)
        apart = {first: "scalar", **{first + 3 + i: "hbm" for i in range(pieces)}}
        operands = operands + tuple(dense)
        out_apart = {len(out_shape): "hbm"}
        out_shape = out_shape + (
            ((D, 4 * D), bf16),
            ((8, D), f32),
            ((128, D), bf16),
            ((HEADS, 2 * SLOT), f32),
        )
    return kernel_call(
        functools.partial(
            front_kernel, lax.axis_size("dp") // 2, own is not None, pieces
        ),
        "gathered_front" if pieces else "attention_front",
        out_shape,
        operands,
        5,
        (pltpu.VMEM((D, width), bf16), pltpu.SemaphoreType.DMA((max(2, pieces),))),
        in_specs=whole_blocks(operands, apart),
        out_specs=tuple(whole_blocks(out_shape, out_apart)),
    )


def expert_call(arrived, slope, experts_held, forward, backward, keep):
    own, other = arrived
    extent, units = own.shape[0], experts_held[0].shape[1]
    width = 2 * D if forward and backward else D
    kept = 0 if not keep else 2 if forward else 1
    row_kept = 1 if keep else 0
    step = 768
    replies = pl.BlockSpec((extent, width), lambda i: (0, 0))
    hidden = pl.BlockSpec((2 * extent, step), lambda i: (0, i))
    in_specs = [replies, replies] + ([] if slope is None else [hidden])
    in_specs = in_specs + [
        pl.BlockSpec((D, step), lambda i: (0, i)),
        pl.BlockSpec((step, D), lambda i: (i, 0)),
    ]
    return kernel_call(
        functools.partial(expert_kernel, forward, backward, keep),
        "experts_" + ("f" if forward else "") + ("b" if backward else ""),
        (((extent, width), bf16),) * 2
        + (((2 * extent, units), bf16),) * kept
        + (((2 * extent, D), bf16),) * row_kept,
        (own, other) + (() if slope is None else (slope,)) + experts_held,
        6 if width == D else 10,
        (pltpu.VMEM((2 * extent, width), f32),),
        grid=(units // step,),
        in_specs=in_specs,
        out_specs=(replies, replies)
        + (hidden,) * kept
        + (pl.BlockSpec((2 * extent, D), lambda i: (0, 0)),) * row_kept,
    )


def turn_call(cotangent, returned, inputs, kept, dense, place):
    gains, weight, router, _ = dense
    _, choose, placing, _ = place
    projected, probs, _, middle, route_probs, gate = kept
    rows = ((SLOT, D), f32)
    operands = (cotangent, returned, placing, choose, inputs, gains, weight)
    operands = operands + (router, projected, probs, middle, route_probs, gate)
    out_shape = (rows, rows, ((SLOT, D), bf16), ((SLOT, 3 * D), bf16))
    return kernel_call(
        turn_kernel,
        "turn_back",
        out_shape,
        operands,
        7,
        (pltpu.VMEM((D, 4 * D), bf16), pltpu.SemaphoreType.DMA((2,))),
        in_specs=whole_blocks(operands, {6: "hbm"}),
        out_specs=tuple(whole_blocks(out_shape, {})),
    )


def back_call(grad_out, returned, inputs, kept, result, dense, place, earlier):
    gains, weight, router, _ = dense
    _, choose, placing, _ = place
    experts = lax.axis_size("dp") // 2
    operands = (grad_out, returned, placing, choose, inputs, gains, weight, router)
    operands = operands + tuple(kept) + (result,) + earlier
    out_shape = (
        ((SLOT, D), f32),
        ((SLOT, 3 * D), bf16),
        ((1, D), f32),
        ((HEADS, 2 * SLOT), f32),
        ((8 + experts, D), f32),
    )
    first = (((D // 4, D), bf16),) * 4 if earlier else (((SLOT, D), f32),)
    out_shape = first + out_shape
    return kernel_call(
        functools.partial(back_kernel, experts, len(earlier) > 0),
        "back_and_out_gradient" if earlier else "back",
        out_shape,
        operands,
        9,
        (pltpu.VMEM((D, 4 * D), bf16), pltpu.SemaphoreType.DMA((2,))),
        in_specs=whole_blocks(operands, {6: "hbm"}),
        out_specs=tuple(whole_blocks(out_shape, {})),
    )


def pack_dense(gains, qkv, out, router, table):
    rows, kind = qkv.shape[0], qkv.dtype
    blank = jnp.zeros((rows, 128 - 8 - router.shape[1]), kind)
    entries = jnp.pad(table, (0, rows - table.shape[0]))[:, None]
    return jnp.concatenate(
        [qkv, out, gains.T, entries, jnp.zeros((rows, 5), kind), router, blank], axis=1
    )


def gather_pieces(piece, early):
    devices, extent = lax.axis_size("dp"), piece.shape[0]
    if devices != 16:
        gathered = lax.all_gather(piece, "dp", axis=0, tiled=True)
        return (jnp.zeros((1,), jnp.int32), [gathered], early)
    me = lax.axis_index("dp")

    def send(block, distance):
        return lax.ppermute(block, "dp", [(i, i ^ distance) for i in range(devices)])

    near, far = send(piece, 4), send(piece, 12)
    far, early = lax.optimization_barrier((far, early))
    pieces, owners = [], []
    for distance, block in ((0, piece), (4, near), (12, far), (8, send(far, 4))):
        for other_y, column in enumerate((block, send(block, 2))):
            for other_core, held in enumerate((column, send(column, 1))):
                pieces.append(held)
                owners.append(me ^ (distance + 2 * other_y + other_core))
    return (jnp.stack(owners).astype(jnp.int32) * extent, pieces, early)


def swap(block, distance):
    route = [(i, i ^ distance) for i in range(lax.axis_size("dp"))]
    return lax.ppermute(block, "dp", route)


def sum_of_four(near, far, near_there, far_there):
    far = (far.astype(f32) + swap(far_there, 1).astype(f32)).astype(bf16)
    near = near.astype(f32) + swap(near_there, 1).astype(f32)
    return (near + swap(far, 2).astype(f32)).astype(bf16)


def total_of(summed):
    devices = lax.axis_size("dp")
    groups = [list(range(first, devices, 4)) for first in range(4)]
    came = lax.all_to_all(
        summed.reshape(devices // 4, D // devices, -1),
        "dp",
        split_axis=0,
        concat_axis=0,
        tiled=True,
        axis_index_groups=groups,
    )
    return jnp.sum(came.astype(f32), axis=0)


def feature_order(devices):
    extent = D // devices
    places = np.arange(D)
    quarter, rest = places // (D // 4), places % (D // 4)
    place = (quarter // 2 + 2 * (quarter % 2)) ^ (lax.axis_index("dp") % 4)
    features = (4 * (rest // extent) + place) * extent + rest % extent
    return (jnp.arange(D)[:, None] == features[None]).astype(bf16)


def table_places(onehot, devices):
    extent, used = D // devices, BUCKETS * HEADS // devices
    places = np.arange(D)
    held = places % extent < used
    entry = np.where(held, places // extent * used + places % extent, 0)
    spread = onehot[:, entry // HEADS] * held
    owner = entry % HEADS == np.arange(HEADS)[:, None]
    return (spread.astype(np.float32), owner.astype(np.float32))


def shards(
    edge_rows,
    lengths,
    routes,
    norm_gains,
    qkv_weight,
    out_weight,
    router_weight,
    bias_table,
    expert_in,
    expert_out,
):
    devices = lax.axis_size("dp")
    experts = devices // 2
    first_section = lax.axis_index("section") == 0
    onehot = bucket_onehot()
    experts_held = (expert_in[0], expert_out[0])
    spread, owner = table_places(onehot, devices)
    same_seq = same_sequence(lengths)
    capacity = 4 * SLOT // devices
    blocks = range(edge_rows.shape[1] // SLOT)
    local_rows = [edge_rows[0, b * SLOT : (b + 1) * SLOT] for b in blocks]
    slot_ids = jnp.arange(experts * capacity, dtype=jnp.int32)
    places, placings = [], []
    for b in blocks:
        route_ids = routes[0, b * SLOT : (b + 1) * SLOT, 0]
        targets = expert_places(route_ids, experts, capacity)
        choose = (route_ids[:, None] == jnp.arange(128, dtype=jnp.int32)[None]).astype(f32)
        placing = (targets[:, None] == slot_ids[None]).astype(bf16)
        places.append((same_seq[b], choose, placing, targets[None, :]))
        placings.append(placing)
    early = (local_rows, places, placings, feature_order(devices))
    offsets, pieces, early = gather_pieces(
        pack_dense(norm_gains[0], qkv_weight[0], out_weight[0], router_weight[0], bias_table[0]),
        early,
    )
    local_rows, places, placings, order = early
    gathering = [offsets, jnp.asarray(spread), jnp.asarray(owner), *pieces]
    dense = None
    first_flag = first_section.astype(jnp.int32).reshape(1)

    def stream(b):
        nonlocal dense
        place, placing, local = places[b], placings[b], local_rows[b]
        packed, _, _, _, middle, _, gate, *made = front_call(
            local, None, dense or gathering, place
        )
        if dense is None:
            weight, *small = made
            dense = (small[0], weight, small[1], small[2])
        came = yield packed
        own, other = expert_call(arrive(came), None, experts_held, True, False, False)
        came = yield join_halves(own, other)
        outputs = middle + gate * dot(placing, came)
        carried = section_shift(outputs.astype(bf16), 1)
        packed, *kept, inputs = front_call(carried, (first_flag, local), dense, place)
        came = yield packed
        own, other, active, slope, arrived = expert_call(
            arrive(came), None, experts_held, True, True, True
        )
        came = yield join_halves(own, other)
        outputs, result, grad_inputs, _ = turn_call(local, came, inputs, kept, dense, place)
        carried = section_shift(grad_inputs, -1)
        grad_out = jnp.where(first_section, carried, local)

        grad_result = (kept[5] * grad_out).astype(bf16)
        came = yield jnp.einsum(
            "ts,td->sd", placing, grad_result, preferred_element_type=f32
        ).astype(bf16)
        own, other, grad_hidden, grad_rows = expert_call(
            arrive(came), slope, experts_held, False, True, True
        )
        came = yield join_halves(own, other)
        rest = (inputs, outputs, kept, (arrived, active, grad_rows, grad_hidden))
        if b == len(blocks) - 1:
            return (came, rest, (grad_out, result))
        return (back_call(grad_out, came, inputs, kept, result, dense, place, ()), rest)

    ends = in_turns([stream(b) for b in blocks])
    inputs, outputs, kept, expert_rows = zip(*[end[1] for end in ends])
    backs = [end[0] for end in ends[:-1]]
    earlier = (order, *[now[2] for now in kept[:-1]], *[back[0] for back in backs])
    returned, _, (grad_out, result) = ends[-1]
    made = back_call(
        grad_out, returned, inputs[-1], kept[-1], result, dense, places[-1], earlier
    )
    back = made[4:]
    grad_first = sum_of_four(*made[:4])
    grad_inputs, grads, gain_ones, tables, smalls = zip(*[now[1:] for now in backs], back)
    cut = D + D // 2
    quarters = kernel_call(
        functools.partial(qkv_grad_kernel, len(blocks), experts),
        "qkv_gradient",
        (((D // 4, cut), bf16),) * 4 + (((D // 4, 3 * D - cut + 128), bf16),) * 4,
        (order, dense[0], spread, owner)
        + (*inputs, *grads, *gain_ones, *tables, *smalls),
        4,
        (pltpu.VMEM((128, D), f32),),
    )
    grad_qkv = sum_of_four(*quarters[:4])
    grad_last = sum_of_four(*quarters[4:])
    total_out = total_of(grad_first)
    total_out, grad_qkv = lax.optimization_barrier((total_out, grad_qkv))
    total_qkv = total_of(grad_qkv)
    total_qkv, grad_last = lax.optimization_barrier((total_qkv, grad_last))
    total_last = total_of(grad_last)
    arrived, active, grad_rows, grad_hidden = zip(*expert_rows)
    grad_expert_out = jnp.einsum(
        "rf,rd->fd",
        jnp.concatenate(active),
        jnp.concatenate(grad_rows),
        preferred_element_type=f32,
    )
    grad_expert_in = jnp.einsum(
        "rd,rf->df",
        jnp.concatenate(arrived),
        jnp.concatenate(grad_hidden),
        preferred_element_type=f32,
    )
    edge_results = jnp.concatenate(
        [jnp.where(first_section, grad_inputs[b], outputs[b]) for b in blocks]
    )
    extra = total_last[:, 3 * D - cut :]
    grad_qkv = jnp.concatenate([total_qkv, total_last[:, : 3 * D - cut]], axis=1)
    return (
        edge_results[None],
        extra[None, :, 0:2].swapaxes(1, 2),
        grad_qkv[None],
        total_out[None],
        extra[None, :, 8 : 8 + experts],
        extra[None, : BUCKETS * HEADS // devices, 2],
        grad_expert_in[None],
        grad_expert_out[None],
    )


def solution(mesh):
    return jax.shard_map(
        shards,
        mesh=mesh,
        in_specs=(
            P("section", "dp", None),
            P("dp", None),
            P("section", "dp", None),
            P("section", None, "dp"),
            P("section", "dp", None),
            P("section", "dp", None),
            P("section", "dp", None),
            P("section", "dp"),
            P("section", None, "dp"),
            P("section", "dp", None),
        ),
        out_specs=(
            P("section", "dp", None),
            P("section", None, "dp"),
            P("section", "dp", None),
            P("section", "dp", None),
            P("section", "dp", None),
            P("section", "dp"),
            P("section", None, "dp"),
            P("section", "dp", None),
        ),
        check_vma=False,
    )
```

```python
import functools

import jax
import jax.numpy as jnp
import numpy as np
from jax import lax
from jax.experimental import pallas as pl
from jax.experimental.pallas import tpu as pltpu
from jax.sharding import PartitionSpec as P

D = 768
HEADS = 12
HEAD_DIM = 64
BUCKETS = 32
SLOT = 128


norm_eps = 1e-06
masked_score = -1e30
bucket_edges = (1, 2, 3, 4, 5, 6, 7, 8, 12, 16, 23, 32, 46, 64, 91)
bf16 = jnp.bfloat16
f32 = jnp.float32


def dot(lhs, rhs):
    return jnp.dot(lhs, rhs, preferred_element_type=f32)


def section_shift(block, distance):
    devices = range(lax.axis_size("section"))
    route = [(i - distance, i) for i in devices if i - distance in devices]
    return lax.ppermute(block, "section", route)


def pair_swap(block):
    return lax.ppermute(block, "dp", [(i, i ^ 1) for i in range(lax.axis_size("dp"))])


def chip_all_to_all(block):
    devices = lax.axis_size("dp")
    groups = [list(range(core, devices, 2)) for core in range(2)]
    return lax.all_to_all(
        block, "dp", split_axis=0, concat_axis=0, tiled=True, axis_index_groups=groups
    )


def rms_scale(values):
    return lax.rsqrt(jnp.mean(values * values, axis=-1, keepdims=True) + norm_eps)


def norm_backward(grad_normed, values, gain_row):
    inv_rms = rms_scale(values)
    weighted = grad_normed * gain_row
    grad_gain = jnp.sum(grad_normed * values * inv_rms, axis=0)
    grad_values = inv_rms * weighted - values * inv_rms**3 * jnp.mean(
        weighted * values, axis=-1, keepdims=True
    )
    return (grad_values, grad_gain)


def bucket_onehot():
    offset = np.arange(2 * SLOT) - SLOT
    bucket = np.sum(np.abs(offset)[:, None] >= np.array(bucket_edges), axis=1)
    bucket = bucket + BUCKETS // 2 * (offset > 0)
    return (bucket[:, None] == np.arange(BUCKETS)).astype(np.float32)


def same_sequence(lengths):
    bounds = jnp.cumsum(lengths, axis=-1)
    places = jnp.arange(SLOT, dtype=jnp.int32)
    owners = jnp.sum((places[:, None] >= bounds[:, None, :]).astype(jnp.int32), axis=-1)
    return (owners[:, :, None] == owners[:, None, :]).astype(f32)


def expert_places(route_ids, experts, capacity):
    names = jnp.arange(experts, dtype=jnp.int32)
    choose = (route_ids[:, None] == names).astype(jnp.int32)
    places = jnp.arange(SLOT, dtype=jnp.int32)
    earlier = (places[:, None] > places[None, :]).astype(bf16)
    before = dot(earlier, choose.astype(bf16)).astype(jnp.int32)
    rank_ids = jnp.sum(before * choose, axis=-1)
    return route_ids * capacity + rank_ids


def arrive(block):
    return (block, pair_swap(block))


def join_halves(own, other):
    return (own.astype(f32) + pair_swap(other).astype(f32)).astype(bf16)


def in_turns(streams):
    ends, values = [None] * len(streams), [None] * len(streams)
    travelling = None
    running = list(range(len(streams)))
    while running:
        for turn in list(running):
            try:
                block = streams[turn].send(values[turn])
            except StopIteration as stop:
                ends[turn] = stop.value
                running.remove(turn)
                if travelling is not None and running:
                    last, held = travelling
                    held, first = lax.optimization_barrier((held, ends[turn][0]))
                    ends[turn] = (first,) + ends[turn][1:]
                    values[last], travelling = held, None
                continue
            if travelling is not None:
                last, held = travelling
                held, block = lax.optimization_barrier((held, block))
                values[last] = held
            experts, width = lax.axis_size("dp") // 2, block.shape[-1]
            came = chip_all_to_all(block.reshape(experts, -1, width)).reshape(-1, width)
            values[turn], travelling = came, (turn, came)
    return ends


def dot_nt(lhs, rhs):
    return lax.dot_general(lhs, rhs, (((1,), (1,)), ((), ())), preferred_element_type=f32)


def dot_tn(lhs, rhs):
    return lax.dot_general(lhs, rhs, (((0,), (0,)), ((), ())), preferred_element_type=f32)


def lane_masks():
    low = lax.broadcasted_iota(jnp.int32, (1, 2 * HEAD_DIM), 1) < HEAD_DIM
    first = jnp.where(low, 1.0, 0.0)
    return (low, first.astype(bf16), (1.0 - first).astype(bf16))


def both_heads(slab, first, second):
    return jnp.concatenate([slab * first, slab * second], axis=0)


def own_lanes(low, stacked):
    return jnp.where(low, stacked[:SLOT], stacked[SLOT:])


def gelu_parts(hidden):
    rate, cubic = 0.7978845608028654, 0.044715
    squared = hidden * hidden
    bend = jnp.tanh(rate * hidden * (1.0 + cubic * squared))
    active = 0.5 * hidden * (1.0 + bend)
    slope = 0.5 * (1.0 + bend) + 0.5 * hidden * (1.0 - bend * bend) * rate * (
        1.0 + 3.0 * cubic * squared
    )
    return (active.astype(bf16), slope.astype(bf16))


def placing_of(targets, slots, dtype=bf16):
    return jnp.where(slots == targets, 1.0, 0.0).astype(dtype)


def load_weight(weight_ref, held_ref, sems):
    parts = [slice(0, 3 * D), slice(3 * D, 4 * D)]
    copies = [
        pltpu.make_async_copy(weight_ref.at[:, part], held_ref.at[:, part], sems.at[i])
        for i, part in enumerate(parts)
    ]
    return copies


def place_pieces(offsets_ref, piece_refs, held_ref, sems):
    copies = []
    for i, piece_ref in enumerate(piece_refs):
        rows = piece_ref.shape[0]
        start = pl.multiple_of(offsets_ref[i], 16) if len(piece_refs) > 1 else 0
        copies.append(
            pltpu.make_async_copy(piece_ref, held_ref.at[pl.ds(start, rows)], sems.at[i])
        )
    return copies


def front_kernel(experts, cotangent, pieces, *refs):
    if cotangent:
        first_ref, cotangent_ref, refs = refs[0], refs[1], refs[2:]
    inputs_ref, same_ref, choose_ref, target_ref = refs[:4]
    refs = refs[4:]
    held_ref, sems = refs[-2:]
    if pieces:
        offsets_ref, spread_ref, owner_ref = refs[:3]
        piece_refs = refs[3 : 3 + pieces]
        refs = refs[3 + pieces :]
        weight_ref, gains_ref, router_ref, diagonals_ref = refs[7:11]
        copies = place_pieces(offsets_ref, piece_refs, held_ref, sems)
        for copy in copies:
            copy.start()
    else:
        weight_ref, gains_ref, router_ref, diagonals_ref = refs[:4]
        refs = refs[4:]
        copies = load_weight(weight_ref, held_ref, sems)
        for copy in copies:
            copy.start()
    (
        packed_ref,
        projected_ref,
        probs_ref,
        attended_ref,
        middle_ref,
        route_probs_ref,
        gate_ref,
    ) = refs[:7]
    inputs = inputs_ref[...].astype(f32)
    if cotangent:
        inputs = jnp.where(first_ref[0] > 0, cotangent_ref[...].astype(f32), inputs)
        refs[7][...] = inputs.astype(bf16)
    inv_rms = rms_scale(inputs)
    if pieces:
        for copy in copies:
            copy.wait()
        keep = pltpu.make_async_copy(held_ref.at[:, : 4 * D], weight_ref, sems.at[0])
        keep.start()
        extra = held_ref[:, 4 * D :].astype(f32).T
        gains_ref[...] = extra[0:8]
        router = jnp.concatenate([extra[8:128], jnp.zeros((8, D), f32)], axis=0)
        router_ref[...] = router.astype(bf16)
        diagonals_ref[...] = lax.dot_general(
            owner_ref[...] * extra[2:3],
            spread_ref[...],
            (((1,), (1,)), ((), ())),
            preferred_element_type=f32,
            precision=lax.Precision.HIGHEST,
        )
    else:
        copies[0].wait()
    normed = (inputs * inv_rms * gains_ref[0:1]).astype(bf16)
    projected_ref[...] = dot(normed, held_ref[:, : 3 * D]).astype(bf16)
    low, first, second = lane_masks()
    width = 2 * HEAD_DIM
    same = same_ref[...]
    same = jnp.concatenate([same, same], axis=0) > 0
    for pair in range(HEADS // 2):
        relative = jnp.concatenate(
            [
                pltpu.roll(
                    jnp.broadcast_to(diagonals_ref[head : head + 1], (SLOT, 2 * SLOT)),
                    SLOT,
                    1,
                    stride=1,
                    stride_axis=0,
                )[:, :SLOT]
                for head in (2 * pair, 2 * pair + 1)
            ],
            axis=0,
        )
        queries, keys, values = [
            projected_ref[:, part * D + pair * width : part * D + (pair + 1) * width]
            for part in range(3)
        ]
        scores = dot_nt(both_heads(queries, first, second), keys) * HEAD_DIM ** (-0.5) + relative
        scores = jnp.where(same, scores, masked_score)
        raised = jnp.exp(scores - jnp.max(scores, axis=-1, keepdims=True))
        probs = raised / jnp.sum(raised, axis=-1, keepdims=True)
        probs_ref[pair] = probs
        attended_ref[:, pair * width : (pair + 1) * width] = own_lanes(
            low, dot(probs.astype(bf16), values)
        ).astype(bf16)
    if not pieces:
        copies[1].wait()
    middle = inputs + dot(attended_ref[...], held_ref[:, 3 * D : 4 * D])
    middle_ref[...] = middle
    routed = (middle * rms_scale(middle) * gains_ref[1:2]).astype(bf16)
    logits = dot_nt(routed, router_ref[...])
    names = lax.broadcasted_iota(jnp.int32, (1, logits.shape[1]), 1)
    logits = jnp.where(names < experts, logits, masked_score)
    raised = jnp.exp(logits - jnp.max(logits, axis=-1, keepdims=True))
    route_probs = raised / jnp.sum(raised, axis=-1, keepdims=True)
    route_probs_ref[...] = route_probs
    gate = jnp.sum(choose_ref[...] * route_probs, axis=-1, keepdims=True)
    gate_ref[...] = gate
    slots = lax.broadcasted_iota(jnp.int32, (packed_ref.shape[0], 1), 0)
    placing = placing_of(target_ref[...], slots)
    packed_ref[:, :D] = dot(placing, routed).astype(bf16)
    if cotangent:
        grad_result = (gate * cotangent_ref[...].astype(f32)).astype(bf16)
        packed_ref[:, D:] = dot(placing, grad_result).astype(bf16)
    if pieces:
        keep.wait()


def expert_kernel(forward, backward, keep, own_ref, other_ref, *refs):
    if backward and not forward:
        slope_ref, refs = refs[0], refs[1:]
    weight_in_ref, weight_out_ref, own_out_ref, other_out_ref = refs[:4]
    kept_refs, total_ref = refs[4:-1], refs[-1]
    grad_at = slice(D, 2 * D) if forward else slice(0, D)
    extent = own_ref.shape[0]
    step = pl.program_id(0)

    @pl.when(step == 0)
    def _():
        total_ref[...] = jnp.zeros_like(total_ref)

    rows = jnp.concatenate([own_ref[...], other_ref[...]], axis=0)
    if keep:
        kept_refs[-1][...] = rows[:, :D]
    if forward:
        active, slope = gelu_parts(dot(rows[:, :D], weight_in_ref[...]))
        total_ref[:, :D] += dot(active, weight_out_ref[...])
        if keep:
            kept_refs[0][...] = active
            kept_refs[1][...] = slope
    else:
        slope = slope_ref[...]
    if backward:
        grad_hidden = (
            dot_nt(rows[:, grad_at], weight_out_ref[...]) * slope.astype(f32)
        ).astype(bf16)
        total_ref[:, grad_at] += dot_nt(grad_hidden, weight_in_ref[...])
        if not forward:
            kept_refs[0][...] = grad_hidden

    @pl.when(step == pl.num_programs(0) - 1)
    def _():
        own_out_ref[...] = total_ref[:extent].astype(bf16)
        other_out_ref[...] = total_ref[extent:].astype(bf16)


def merge_back(
    grad_out, result, grad_sent, middle, gate, route_probs, choose, router_ref, gains_ref
):
    grad_gate = jnp.sum(grad_out * result, axis=-1, keepdims=True)
    grad_logits = (grad_gate * gate * (choose - route_probs)).astype(bf16)
    grad_routed = grad_sent + dot(grad_logits, router_ref[...])
    grad_middle_norm, grad_gain = norm_backward(grad_routed, middle, gains_ref[1:2])
    return (grad_out + grad_middle_norm, grad_gain, grad_logits)


def attention_back(
    grad_middle, inputs, gains_ref, held, projected_ref, probs_ref, grads_ref, table_ref
):
    weight_ref, copies = held
    copies[1].wait()
    grad_attended = dot_nt(grad_middle.astype(bf16), weight_ref[:, 3 * D :]).astype(bf16)
    low, first, second = lane_masks()
    width = 2 * HEAD_DIM
    scale_qk = HEAD_DIM ** (-0.5)
    places = [lax.broadcasted_iota(jnp.int32, (SLOT, SLOT), axis) for axis in range(2)]
    reverse = jnp.where(places[0] + places[1] == SLOT - 1, 1.0, 0.0).astype(bf16)
    for pair in range(HEADS // 2):
        columns = [
            slice(part * D + pair * width, part * D + (pair + 1) * width) for part in range(3)
        ]
        queries, keys, values = [projected_ref[:, part] for part in columns]
        grads = both_heads(grad_attended[:, pair * width : (pair + 1) * width], first, second)
        probs = probs_ref[pair]
        grad_probs = dot_nt(grads, values)
        grad_scores = (
            probs * (grad_probs - jnp.sum(probs * grad_probs, axis=-1, keepdims=True))
        ).astype(bf16)
        grads_ref[:, columns[0]] = (own_lanes(low, dot(grad_scores, keys)) * scale_qk).astype(bf16)
        grads_ref[:, columns[1]] = (
            dot_tn(grad_scores, both_heads(queries, first, second)) * scale_qk
        ).astype(bf16)
        grads_ref[:, columns[2]] = dot_tn(probs.astype(bf16), grads).astype(bf16)
        if table_ref is not None:
            for own in range(2):
                part = dot(reverse, grad_scores[own * SLOT : (own + 1) * SLOT])
                wide = jnp.concatenate([part, jnp.zeros_like(part)], axis=1)
                moved = pltpu.roll(wide, 1, 1, stride=1, stride_axis=0)
                head = 2 * pair + own
                table_ref[head : head + 1] = jnp.sum(moved, axis=0, keepdims=True)
    copies[0].wait()
    grad_normed = dot_nt(grads_ref[...], weight_ref[:, : 3 * D])
    grad_inputs_norm, grad_gain = norm_backward(grad_normed, inputs, gains_ref[0:1])
    return (grad_middle + grad_inputs_norm, grad_gain)


def start_weight(weight_ref, held_ref, sems):
    copies = load_weight(weight_ref, held_ref, sems)
    for copy in reversed(copies):
        copy.start()
    return (held_ref, copies)


def turn_kernel(
    cotangent_ref,
    returned_ref,
    placing_ref,
    choose_ref,
    inputs_ref,
    gains_ref,
    weight_ref,
    router_ref,
    projected_ref,
    probs_ref,
    middle_ref,
    route_probs_ref,
    gate_ref,
    outputs_ref,
    result_ref,
    grad_inputs_ref,
    grads_ref,
    held_ref,
    sems,
):
    held = start_weight(weight_ref, held_ref, sems)
    both = dot(placing_ref[...], returned_ref[...])
    result = both[:, :D]
    result_ref[...] = result
    middle, gate = middle_ref[...], gate_ref[...]
    outputs_ref[...] = middle + gate * result
    grad_middle, _, _ = merge_back(
        cotangent_ref[...].astype(f32),
        result,
        both[:, D:],
        middle,
        gate,
        route_probs_ref[...],
        choose_ref[...],
        router_ref,
        gains_ref,
    )
    grad_inputs, _ = attention_back(
        grad_middle,
        inputs_ref[...].astype(f32),
        gains_ref,
        held,
        projected_ref,
        probs_ref,
        grads_ref,
        None,
    )
    grad_inputs_ref[...] = grad_inputs.astype(bf16)


def back_kernel(
    experts,
    last,
    grad_out_ref,
    returned_ref,
    placing_ref,
    choose_ref,
    inputs_ref,
    gains_ref,
    weight_ref,
    router_ref,
    projected_ref,
    probs_ref,
    attended_ref,
    middle_ref,
    route_probs_ref,
    gate_ref,
    result_ref,
    *refs,
):
    if last:
        earlier = len(refs) - 11
        order_ref, earlier_refs, refs = refs[0], refs[1:earlier], refs[earlier:]
        quarter_refs, refs = refs[:4], refs[4:]
    else:
        grad_middle_ref, refs = refs[0], refs[1:]
    grad_inputs_ref, grads_ref, gain_ref, table_ref, small_ref, held_ref, sems = refs[-7:]
    held = start_weight(weight_ref, held_ref, sems)
    middle = middle_ref[...]
    grad_middle, grad_gain, grad_logits = merge_back(
        grad_out_ref[...].astype(f32),
        result_ref[...],
        dot(placing_ref[...], returned_ref[...]),
        middle,
        gate_ref[...],
        route_probs_ref[...],
        choose_ref[...],
        router_ref,
        gains_ref,
    )
    routed = (middle * rms_scale(middle) * gains_ref[1:2]).astype(bf16)
    small_ref[0:8] = jnp.broadcast_to(grad_gain[None], (8, D))
    small_ref[8:] = dot_tn(grad_logits, routed)[:experts]
    if last:
        half = len(earlier_refs) // 2
        attended = [ref[...] for ref in earlier_refs[:half]] + [attended_ref[...]]
        grads = [ref[...] for ref in earlier_refs[half:]] + [grad_middle]
        ordered = dot(jnp.concatenate(attended, axis=0), order_ref[...]).astype(bf16)
        total = dot_tn(ordered, jnp.concatenate(grads, axis=0).astype(bf16)).astype(bf16)
        for i, quarter_ref in enumerate(quarter_refs):
            quarter_ref[...] = total[i * D // 4 : (i + 1) * D // 4]
    else:
        grad_middle_ref[...] = grad_middle
    grad_inputs_ref[...], grad_gain = attention_back(
        grad_middle,
        inputs_ref[...].astype(f32),
        gains_ref,
        held,
        projected_ref,
        probs_ref,
        grads_ref,
        table_ref,
    )
    gain_ref[...] = grad_gain[None]


def qkv_grad_kernel(blocks, experts, order_ref, gains_ref, spread_ref, owner_ref, *refs):
    chunks, wide_ref = refs[-9:-1], refs[-1]
    inputs_refs, grads_refs, gain_refs, table_refs, small_refs = [
        refs[part * blocks : (part + 1) * blocks] for part in range(5)
    ]
    ordering = order_ref[...]
    inputs = jnp.concatenate([ref[...] for ref in inputs_refs], axis=0).astype(f32)
    normed = (inputs * rms_scale(inputs) * gains_ref[0:1]).astype(bf16)
    normed = dot(normed, ordering).astype(bf16)
    cut = chunks[0].shape[1]

    def keep(start, total):
        first = start if start < cut else start - cut
        columns = slice(first, first + total.shape[1])
        for i, quarter_ref in enumerate(chunks[:4] if start < cut else chunks[4:]):
            quarter_ref[:, columns] = total[i * D // 4 : (i + 1) * D // 4]

    for start, stop in ((0, D), (D, cut), (cut, 2 * D), (2 * D, 3 * D)):
        grads = jnp.concatenate([grads_ref[:, start:stop] for grads_ref in grads_refs], axis=0)
        keep(start, dot_tn(normed, grads).astype(bf16))
    diagonals = sum([table_ref[...] for table_ref in table_refs])
    entries = jnp.sum(
        owner_ref[...]
        * jnp.dot(
            diagonals,
            spread_ref[...],
            preferred_element_type=f32,
            precision=lax.Precision.HIGHEST,
        ),
        axis=0,
        keepdims=True,
    )
    small = sum([small_ref[...] for small_ref in small_refs])
    wide_ref[...] = jnp.zeros_like(wide_ref)
    wide_ref[0:1] = sum([gain_ref[...] for gain_ref in gain_refs])
    wide_ref[1:2] = small[0:1]
    wide_ref[2:3] = entries
    wide_ref[8 : 8 + experts] = small[8:]
    keep(3 * D, dot_tn(ordering, wide_ref[...].T.astype(bf16)).astype(bf16))


def kernel_call(kernel, name, out_shape, operands, micros, scratch=(), grant=62, **blocks):
    return pl.pallas_call(
        kernel,
        out_shape=tuple(jax.ShapeDtypeStruct(*pair) for pair in out_shape),
        scratch_shapes=list(scratch),
        compiler_params=pltpu.CompilerParams(vmem_limit_bytes=grant * 1024 * 1024),
        cost_estimate=pl.CostEstimate(
            flops=int(micros * 5e8), bytes_accessed=int(micros * 3e6), transcendentals=0
        ),
        name=name,
        **blocks,
    )(*operands)


def whole_blocks(operands, apart):
    spaces = {"hbm": pl.ANY, "scalar": pltpu.SMEM, "vmem": pltpu.VMEM}
    return [pl.BlockSpec(memory_space=spaces[apart.get(i, "vmem")]) for i in range(len(operands))]


def front_call(inputs, own, dense, place):
    same_seq, choose, _, target_row = place
    slots = 4 * SLOT // lax.axis_size("dp") * (lax.axis_size("dp") // 2)
    operands = () if own is None else own
    operands = operands + (inputs, same_seq, choose, target_row)
    out_shape = (
        ((slots, D if own is None else 2 * D), bf16),
        ((SLOT, 3 * D), bf16),
        ((HEADS // 2, 2 * SLOT, SLOT), f32),
        ((SLOT, D), bf16),
        ((SLOT, D), f32),
        ((SLOT, 128), f32),
        ((SLOT, 1), f32),
    )
    pieces, width, out_apart = 0, 4 * D, {}
    if own is not None:
        out_shape = out_shape + (((SLOT, D), bf16),)
    if isinstance(dense, tuple):
        gains, weight, router, diagonals = dense
        apart = {len(operands): "hbm"} if own is None else {0: "scalar", len(operands): "hbm"}
        operands = operands + (weight, gains, router, diagonals)
    else:
        offsets, spread, owner, *held = dense
        pieces, width = len(held), 4 * D + 128
        first = len(operands)
        apart = {first: "scalar", **{first + 3 + i: "hbm" for i in range(pieces)}}
        operands = operands + tuple(dense)
        out_apart = {len(out_shape): "hbm"}
        out_shape = out_shape + (
            ((D, 4 * D), bf16),
            ((8, D), f32),
            ((128, D), bf16),
            ((HEADS, 2 * SLOT), f32),
        )
    return kernel_call(
        functools.partial(
            front_kernel, lax.axis_size("dp") // 2, own is not None, pieces
        ),
        "gathered_front" if pieces else "attention_front",
        out_shape,
        operands,
        5,
        (pltpu.VMEM((D, width), bf16), pltpu.SemaphoreType.DMA((max(2, pieces),))),
        in_specs=whole_blocks(operands, apart),
        out_specs=tuple(whole_blocks(out_shape, out_apart)),
    )


def expert_call(arrived, slope, experts_held, forward, backward, keep):
    own, other = arrived
    extent, units = own.shape[0], experts_held[0].shape[1]
    width = 2 * D if forward and backward else D
    kept = 0 if not keep else 2 if forward else 1
    row_kept = 1 if keep else 0
    step = 768
    replies = pl.BlockSpec((extent, width), lambda i: (0, 0))
    hidden = pl.BlockSpec((2 * extent, step), lambda i: (0, i))
    in_specs = [replies, replies] + ([] if slope is None else [hidden])
    in_specs = in_specs + [
        pl.BlockSpec((D, step), lambda i: (0, i)),
        pl.BlockSpec((step, D), lambda i: (i, 0)),
    ]
    return kernel_call(
        functools.partial(expert_kernel, forward, backward, keep),
        "experts_" + ("f" if forward else "") + ("b" if backward else ""),
        (((extent, width), bf16),) * 2
        + (((2 * extent, units), bf16),) * kept
        + (((2 * extent, D), bf16),) * row_kept,
        (own, other) + (() if slope is None else (slope,)) + experts_held,
        6 if width == D else 10,
        (pltpu.VMEM((2 * extent, width), f32),),
        grid=(units // step,),
        in_specs=in_specs,
        out_specs=(replies, replies)
        + (hidden,) * kept
        + (pl.BlockSpec((2 * extent, D), lambda i: (0, 0)),) * row_kept,
    )


def turn_call(cotangent, returned, inputs, kept, dense, place):
    gains, weight, router, _ = dense
    _, choose, placing, _ = place
    projected, probs, _, middle, route_probs, gate = kept
    rows = ((SLOT, D), f32)
    operands = (cotangent, returned, placing, choose, inputs, gains, weight)
    operands = operands + (router, projected, probs, middle, route_probs, gate)
    out_shape = (rows, rows, ((SLOT, D), bf16), ((SLOT, 3 * D), bf16))
    return kernel_call(
        turn_kernel,
        "turn_back",
        out_shape,
        operands,
        7,
        (pltpu.VMEM((D, 4 * D), bf16), pltpu.SemaphoreType.DMA((2,))),
        in_specs=whole_blocks(operands, {6: "hbm"}),
        out_specs=tuple(whole_blocks(out_shape, {})),
    )


def back_call(grad_out, returned, inputs, kept, result, dense, place, earlier):
    gains, weight, router, _ = dense
    _, choose, placing, _ = place
    experts = lax.axis_size("dp") // 2
    operands = (grad_out, returned, placing, choose, inputs, gains, weight, router)
    operands = operands + tuple(kept) + (result,) + earlier
    out_shape = (
        ((SLOT, D), f32),
        ((SLOT, 3 * D), bf16),
        ((1, D), f32),
        ((HEADS, 2 * SLOT), f32),
        ((8 + experts, D), f32),
    )
    first = (((D // 4, D), bf16),) * 4 if earlier else (((SLOT, D), f32),)
    out_shape = first + out_shape
    return kernel_call(
        functools.partial(back_kernel, experts, len(earlier) > 0),
        "back_and_out_gradient" if earlier else "back",
        out_shape,
        operands,
        9,
        (pltpu.VMEM((D, 4 * D), bf16), pltpu.SemaphoreType.DMA((2,))),
        in_specs=whole_blocks(operands, {6: "hbm"}),
        out_specs=tuple(whole_blocks(out_shape, {})),
    )


def pack_dense(gains, qkv, out, router, table):
    rows, kind = qkv.shape[0], qkv.dtype
    blank = jnp.zeros((rows, 128 - 8 - router.shape[1]), kind)
    entries = jnp.pad(table, (0, rows - table.shape[0]))[:, None]
    return jnp.concatenate(
        [qkv, out, gains.T, entries, jnp.zeros((rows, 5), kind), router, blank], axis=1
    )


def gather_pieces(piece, early):
    devices, extent = lax.axis_size("dp"), piece.shape[0]
    if devices != 16:
        gathered = lax.all_gather(piece, "dp", axis=0, tiled=True)
        return (jnp.zeros((1,), jnp.int32), [gathered], early)
    me = lax.axis_index("dp")

    def send(block, distance):
        return lax.ppermute(block, "dp", [(i, i ^ distance) for i in range(devices)])

    near, far = send(piece, 4), send(piece, 12)
    far, early = lax.optimization_barrier((far, early))
    pieces, owners = [], []
    for distance, block in ((0, piece), (4, near), (12, far), (8, send(far, 4))):
        for other_y, column in enumerate((block, send(block, 2))):
            for other_core, held in enumerate((column, send(column, 1))):
                pieces.append(held)
                owners.append(me ^ (distance + 2 * other_y + other_core))
    return (jnp.stack(owners).astype(jnp.int32) * extent, pieces, early)


def swap(block, distance):
    route = [(i, i ^ distance) for i in range(lax.axis_size("dp"))]
    return lax.ppermute(block, "dp", route)


def sum_of_four(near, far, near_there, far_there):
    far = (far.astype(f32) + swap(far_there, 1).astype(f32)).astype(bf16)
    near = near.astype(f32) + swap(near_there, 1).astype(f32)
    return (near + swap(far, 2).astype(f32)).astype(bf16)


def total_of(summed):
    devices = lax.axis_size("dp")
    groups = [list(range(first, devices, 4)) for first in range(4)]
    came = lax.all_to_all(
        summed.reshape(devices // 4, D // devices, -1),
        "dp",
        split_axis=0,
        concat_axis=0,
        tiled=True,
        axis_index_groups=groups,
    )
    return jnp.sum(came.astype(f32), axis=0)


def feature_order(devices):
    extent = D // devices
    places = np.arange(D)
    quarter, rest = places // (D // 4), places % (D // 4)
    place = (quarter // 2 + 2 * (quarter % 2)) ^ (lax.axis_index("dp") % 4)
    features = (4 * (rest // extent) + place) * extent + rest % extent
    return (jnp.arange(D)[:, None] == features[None]).astype(bf16)


def table_places(onehot, devices):
    extent, used = D // devices, BUCKETS * HEADS // devices
    places = np.arange(D)
    held = places % extent < used
    entry = np.where(held, places // extent * used + places % extent, 0)
    spread = onehot[:, entry // HEADS] * held
    owner = entry % HEADS == np.arange(HEADS)[:, None]
    return (spread.astype(np.float32), owner.astype(np.float32))


def shards(
    edge_rows,
    lengths,
    routes,
    norm_gains,
    qkv_weight,
    out_weight,
    router_weight,
    bias_table,
    expert_in,
    expert_out,
):
    devices = lax.axis_size("dp")
    experts = devices // 2
    first_section = lax.axis_index("section") == 0
    onehot = bucket_onehot()
    experts_held = (expert_in[0], expert_out[0])
    spread, owner = table_places(onehot, devices)
    same_seq = same_sequence(lengths)
    capacity = 4 * SLOT // devices
    blocks = range(edge_rows.shape[1] // SLOT)
    local_rows = [edge_rows[0, b * SLOT : (b + 1) * SLOT] for b in blocks]
    slot_ids = jnp.arange(experts * capacity, dtype=jnp.int32)
    places, placings = [], []
    for b in blocks:
        route_ids = routes[0, b * SLOT : (b + 1) * SLOT, 0]
        targets = expert_places(route_ids, experts, capacity)
        choose = (route_ids[:, None] == jnp.arange(128, dtype=jnp.int32)[None]).astype(f32)
        placing = (targets[:, None] == slot_ids[None]).astype(bf16)
        places.append((same_seq[b], choose, placing, targets[None, :]))
        placings.append(placing)
    early = (local_rows, places, placings, feature_order(devices))
    offsets, pieces, early = gather_pieces(
        pack_dense(norm_gains[0], qkv_weight[0], out_weight[0], router_weight[0], bias_table[0]),
        early,
    )
    local_rows, places, placings, order = early
    gathering = [offsets, jnp.asarray(spread), jnp.asarray(owner), *pieces]
    dense = None
    first_flag = first_section.astype(jnp.int32).reshape(1)

    def stream(b):
        nonlocal dense
        place, placing, local = places[b], placings[b], local_rows[b]
        packed, _, _, _, middle, _, gate, *made = front_call(
            local, None, dense or gathering, place
        )
        if dense is None:
            weight, *small = made
            dense = (small[0], weight, small[1], small[2])
        came = yield packed
        own, other = expert_call(arrive(came), None, experts_held, True, False, False)
        came = yield join_halves(own, other)
        outputs = middle + gate * dot(placing, came)
        carried = section_shift(outputs.astype(bf16), 1)
        packed, *kept, inputs = front_call(carried, (first_flag, local), dense, place)
        came = yield packed
        own, other, active, slope, arrived = expert_call(
            arrive(came), None, experts_held, True, True, True
        )
        came = yield join_halves(own, other)
        outputs, result, grad_inputs, _ = turn_call(local, came, inputs, kept, dense, place)
        carried = section_shift(grad_inputs, -1)
        grad_out = jnp.where(first_section, carried, local)

        grad_result = (kept[5] * grad_out).astype(bf16)
        came = yield jnp.einsum(
            "ts,td->sd", placing, grad_result, preferred_element_type=f32
        ).astype(bf16)
        own, other, grad_hidden, grad_rows = expert_call(
            arrive(came), slope, experts_held, False, True, True
        )
        came = yield join_halves(own, other)
        rest = (inputs, outputs, kept, (arrived, active, grad_rows, grad_hidden))
        if b == len(blocks) - 1:
            return (came, rest, (grad_out, result))
        return (back_call(grad_out, came, inputs, kept, result, dense, place, ()), rest)

    ends = in_turns([stream(b) for b in blocks])
    inputs, outputs, kept, expert_rows = zip(*[end[1] for end in ends])
    backs = [end[0] for end in ends[:-1]]
    earlier = (order, *[now[2] for now in kept[:-1]], *[back[0] for back in backs])
    returned, _, (grad_out, result) = ends[-1]
    made = back_call(
        grad_out, returned, inputs[-1], kept[-1], result, dense, places[-1], earlier
    )
    back = made[4:]
    grad_first = sum_of_four(*made[:4])
    grad_inputs, grads, gain_ones, tables, smalls = zip(*[now[1:] for now in backs], back)
    cut = D + D // 2
    quarters = kernel_call(
        functools.partial(qkv_grad_kernel, len(blocks), experts),
        "qkv_gradient",
        (((D // 4, cut), bf16),) * 4 + (((D // 4, 3 * D - cut + 128), bf16),) * 4,
        (order, dense[0], spread, owner)
        + (*inputs, *grads, *gain_ones, *tables, *smalls),
        4,
        (pltpu.VMEM((128, D), f32),),
    )
    grad_qkv = sum_of_four(*quarters[:4])
    grad_last = sum_of_four(*quarters[4:])
    total_out = total_of(grad_first)
    total_out, grad_qkv = lax.optimization_barrier((total_out, grad_qkv))
    total_qkv = total_of(grad_qkv)
    total_qkv, grad_last = lax.optimization_barrier((total_qkv, grad_last))
    total_last = total_of(grad_last)
    arrived, active, grad_rows, grad_hidden = zip(*expert_rows)
    grad_expert_out = jnp.einsum(
        "rf,rd->fd",
        jnp.concatenate(active),
        jnp.concatenate(grad_rows),
        preferred_element_type=f32,
    )
    grad_expert_in = jnp.einsum(
        "rd,rf->df",
        jnp.concatenate(arrived),
        jnp.concatenate(grad_hidden),
        preferred_element_type=f32,
    )
    edge_results = jnp.concatenate(
        [jnp.where(first_section, grad_inputs[b], outputs[b]) for b in blocks]
    )
    extra = total_last[:, 3 * D - cut :]
    grad_qkv = jnp.concatenate([total_qkv, total_last[:, : 3 * D - cut]], axis=1)
    return (
        edge_results[None],
        extra[None, :, 0:2].swapaxes(1, 2),
        grad_qkv[None],
        total_out[None],
        extra[None, :, 8 : 8 + experts],
        extra[None, : BUCKETS * HEADS // devices, 2],
        grad_expert_in[None],
        grad_expert_out[None],
    )


def solution(mesh):
    return jax.shard_map(
        shards,
        mesh=mesh,
        in_specs=(
            P("section", "dp", None),
            P("dp", None),
            P("section", "dp", None),
            P("section", None, "dp"),
            P("section", "dp", None),
            P("section", "dp", None),
            P("section", "dp", None),
            P("section", "dp"),
            P("section", None, "dp"),
            P("section", "dp", None),
        ),
        out_specs=(
            P("section", "dp", None),
            P("section", None, "dp"),
            P("section", "dp", None),
            P("section", "dp", None),
            P("section", "dp", None),
            P("section", "dp"),
            P("section", None, "dp"),
            P("section", "dp", None),
        ),
        check_vma=False,
    )
```
